128 devices in a mesh: bx: 8 (over x, y_hi), by: 16 (over y_lo, z, core).
Axes of the slice: x: 4, y: 4 (y_hi: 2, y_lo: 2; y = y_hi * 2 + y_lo), z: 4, core: 2. Of those that a mesh axis runs over, the one named last changes fastest.
Arguments:
- features: bfloat16 [8, 16, 128, 25, 128], P('bx', 'by'), may hold values from -6 to 6
- send_index: int32 [8, 16, 3, 3, 16], P('bx', 'by'), may hold values from 0 to 128
- atom_vectors: float32 [8, 16, 3, 1024], P('bx', 'by'), may hold values from -4 to 4, as said below
- atom_source: int32 [8, 16, 1024], P('bx', 'by'), may hold values from 0 to 256
- atom_target: int32 [8, 16, 1024], P('bx', 'by'), may hold values from 0 to 128
- probe_vectors: float32 [8, 16, 3, 512], P('bx', 'by'), may hold values from -4 to 4, as said below
- probe_atoms: int32 [8, 16, 512], P('bx', 'by'), may hold values from 0 to 256
- density_grid: float32 [8, 16, 32768], P('bx', 'by'), may hold values from -6 to 6
- probe_index: int32 [8, 16, 128], P('bx', 'by'), may hold values from 0 to 32767
- radial_first: float32 [20, 64], replicated, may hold values from -1.25 to 1.25
- radial_second: float32 [64, 1280], replicated, may hold values from -0.75 to 0.75
- mixing: float32 [5, 128, 128], replicated, may hold values from -0.5 to 0.5
- probe_first: float32 [20, 64], replicated, may hold values from -1.25 to 1.25
- probe_second: float32 [64, 640], replicated, may hold values from -0.75 to 0.75
- readout_first: float32 [128, 128], replicated, may hold values from -0.5 to 0.5
- readout_second: float32 [128], replicated, may hold values from -0.5 to 0.5
Outputs:
- loss_value: float32 [], replicated
- feature_grad: float32 [8, 16, 128, 25, 128], P('bx', 'by')
- radial_first_grad: float32 [20, 64], replicated
- radial_second_grad: float32 [64, 1280], replicated
- mixing_grad: float32 [5, 128, 128], replicated
- probe_first_grad: float32 [20, 64], replicated
- probe_second_grad: float32 [64, 640], replicated
- readout_first_grad: float32 [128, 128], replicated
- readout_second_grad: float32 [128], replicated
The draws below stay inside these ranges and needn't reach their ends.
Inputs may be any that keep to these rules, and one draw needn't show every extreme that they name: `atom_vectors`: each column is a displacement of length 0.7 to 4.0. `probe_vectors`: each column is a displacement of length 0.7 to 4.0.
All inputs are finite; a program needn't handle non-finite values.
Results may differ from the reference program's by a relative error of at most 0.0075.
Values may be sent and summed in bfloat16 or wider, within the bound.
No kernel may reach another device: no remote copies, remote signals or barrier semaphores. Data moves between devices by JAX's collectives and lax.ppermute only.
A program may use at most 192 MiB of HBM per device.

```python
import math
import jax
import jax.numpy as jnp
import numpy as np
from jax import lax

CHANNELS = 128
COMP = 25
BASIS = 20
RADIAL_HIDDEN = 64
ATOMS_DEV = 128
GHOSTS = 16
NEIGHBOURS = 8
EDGES_DEV = 1024
PROBES_DEV = 128
PROBE_EDGES = 4
PEDGES_DEV = 512
GRID_DEV = 32768
BLOCK = 512
N_BX = 8
N_BY = 16


def displacements(key, edge_shape, exponent):
    key_list = jax.random.split(key, 3)
    uniform_part = jax.random.uniform(key_list[0], edge_shape, jnp.float32)
    radius = 0.7 + 3.3 * uniform_part ** exponent
    polar_cos = jax.random.uniform(key_list[1], edge_shape, jnp.float32, -1.0, 1.0)
    azimuth = jax.random.uniform(key_list[2], edge_shape, jnp.float32, -math.pi, math.pi)
    polar_sin = jnp.sqrt(jnp.maximum(1.0 - polar_cos * polar_cos, 0.0))
    return jnp.stack([radius * polar_sin * jnp.cos(azimuth), radius * polar_sin * jnp.sin(azimuth), radius * polar_cos], axis=2)


def draw_atom_vectors(key, part):
    key = jax.random.fold_in(key, 11)
    return displacements(key, (N_BX, N_BY, EDGES_DEV), 1.0)


def draw_probe_vectors(key, part):
    key = jax.random.fold_in(key, 23)
    return displacements(key, (N_BX, N_BY, PEDGES_DEV), 1.0)


def plant(values, own_key, low, high):
    dims = values.shape
    place = [jax.random.randint(jax.random.fold_in(own_key, axis), (), 0, dims[axis]) for axis in range(len(dims))]
    values = values.at[tuple(place)].set(low)
    longest = dims.index(max(dims))
    place[longest] = (place[longest] + 1) % dims[longest]
    return values.at[tuple(place)].set(high)


def steps_of(stream_key, dims, shards, low, largest):
    gain = 1.0
    for axis_at, shards_of in shards:
        draws = jax.random.uniform(jax.random.fold_in(jax.random.fold_in(stream_key, 6), axis_at), (shards_of,), jnp.float32, low / len(shards), largest / len(shards))
        gain = gain * jnp.repeat(jnp.exp(draws), dims[axis_at] // shards_of).reshape((-1,) + (1,) * (len(dims) - 1 - axis_at))
    return gain


def gaussian(stream_key, extent, scale, most, shards=(), held_as=jnp.bfloat16):
    values = jax.random.normal(stream_key, extent, jnp.float32) * scale
    if len(shards) > 0:
        values = steps_of(stream_key, extent, shards, -0.22, 0.18) * values
    return jnp.clip(values, min=-most, max=most).astype(held_as)


def setup_inputs(seed: int = 0) -> dict:
    keys = jax.random.split(jax.random.key(seed), 17)
    features = gaussian(keys[0], (N_BX, N_BY, ATOMS_DEV, COMP, CHANNELS), 1.0, 6.0, ((0, 8), (1, 16)))
    send_index = plant(jax.random.randint(keys[1], (N_BX, N_BY, 3, 3, GHOSTS), 0, ATOMS_DEV + 1), jax.random.fold_in(keys[1], 1), 0, ATOMS_DEV).astype(jnp.int32)
    atom_vectors = draw_atom_vectors(jax.random.fold_in(keys[16], 71), 0)
    atom_source = plant(jax.random.randint(keys[3], (N_BX, N_BY, EDGES_DEV), 0, ATOMS_DEV + 1 + 8 * GHOSTS), jax.random.fold_in(keys[3], 1), 0, (ATOMS_DEV + 1 + 8 * GHOSTS) - 1).astype(jnp.int32)
    atom_target = plant(jax.random.randint(keys[4], (N_BX, N_BY, EDGES_DEV), 0, ATOMS_DEV + 1), jax.random.fold_in(keys[4], 1), 0, ATOMS_DEV).astype(jnp.int32)
    probe_vectors = draw_probe_vectors(jax.random.fold_in(keys[16], 71), 0)
    probe_atoms = plant(jax.random.randint(keys[6], (N_BX, N_BY, PEDGES_DEV), 0, ATOMS_DEV + 1 + 8 * GHOSTS), jax.random.fold_in(keys[6], 1), 0, (ATOMS_DEV + 1 + 8 * GHOSTS) - 1).astype(jnp.int32)
    density_grid = gaussian(keys[7], (N_BX, N_BY, GRID_DEV), 1.0, 6.0, ((0, 8), (1, 16)), jnp.float32)
    probe_index = plant(jax.random.randint(keys[8], (N_BX, N_BY, PROBES_DEV), 0, GRID_DEV), jax.random.fold_in(keys[8], 1), 0, GRID_DEV - 1).astype(jnp.int32)
    radial_first = gaussian(keys[9], (BASIS, RADIAL_HIDDEN), BASIS ** -0.5, 1.25, (), jnp.float32)
    radial_second = gaussian(keys[10], (RADIAL_HIDDEN, 10 * CHANNELS), RADIAL_HIDDEN ** -0.5, 0.75, (), jnp.float32)
    mixing = gaussian(keys[11], (5, CHANNELS, CHANNELS), CHANNELS ** -0.5, 0.5, (), jnp.float32)
    probe_first = gaussian(keys[12], (BASIS, RADIAL_HIDDEN), BASIS ** -0.5, 1.25, (), jnp.float32)
    probe_second = gaussian(keys[13], (RADIAL_HIDDEN, 5 * CHANNELS), RADIAL_HIDDEN ** -0.5, 0.75, (), jnp.float32)
    readout_first = gaussian(keys[14], (CHANNELS, CHANNELS), CHANNELS ** -0.5, 0.5, (), jnp.float32)
    readout_second = gaussian(keys[15], (CHANNELS,), CHANNELS ** -0.5, 0.5, (), jnp.float32)
    return dict(features=features, send_index=send_index, atom_vectors=atom_vectors, atom_source=atom_source, atom_target=atom_target, probe_vectors=probe_vectors, probe_atoms=probe_atoms, density_grid=density_grid, probe_index=probe_index, radial_first=radial_first, radial_second=radial_second, mixing=mixing, probe_first=probe_first, probe_second=probe_second, readout_first=readout_first, readout_second=readout_second)


HIGHEST = lax.Precision.HIGHEST
OFFSETS = ((-1, -1), (-1, 0), (-1, 1), (0, -1), (0, 1), (1, -1), (1, 0), (1, 1))
DEGREES = (1, 3, 5, 7, 9)
STARTS = (0, 1, 4, 9, 16)

def harmonics(unit_dirs):
    x = unit_dirs[0]
    y = unit_dirs[1]
    z = unit_dirs[2]
    z_square = z * z
    listed = [jnp.ones_like(x), 1.7320508 * y, 1.7320508 * z, 1.7320508 * x, 3.8729833 * x * y, 3.8729833 * y * z, 1.118034 * (3.0 * z_square - 1.0), 3.8729833 * x * z, 1.9364917 * (x * x - y * y), 2.0916501 * y * (3.0 * x * x - y * y), 10.246951 * x * y * z, 1.6201852 * y * (5.0 * z_square - 1.0), 1.3228757 * z * (5.0 * z_square - 3.0), 1.6201852 * x * (5.0 * z_square - 1.0), 5.1234754 * z * (x * x - y * y), 2.0916501 * x * (x * x - 3.0 * y * y), 8.8741197 * x * y * (x * x - y * y), 6.2749502 * y * z * (3.0 * x * x - y * y), 3.354102 * x * y * (7.0 * z_square - 1.0), 2.3717082 * y * z * (7.0 * z_square - 3.0), 0.375 * (35.0 * z_square * z_square - 30.0 * z_square + 3.0), 2.3717082 * x * z * (7.0 * z_square - 3.0), 1.677051 * (x * x - y * y) * (7.0 * z_square - 1.0), 6.2749502 * x * z * (x * x - 3.0 * y * y), 2.2185299 * (x * x * x * x - 6.0 * x * x * y * y + y * y * y * y)]
    return jnp.stack(listed, axis=1)

def geometry(vectors):
    radius = jnp.sqrt(lax.optimization_barrier(jnp.sum(vectors * vectors, axis=0)))
    unit_dirs = vectors / radius
    centers = 0.5 + 4.0 * jnp.arange(BASIS, dtype=jnp.float32) / (BASIS - 1)
    radial_basis = jnp.exp(-((radius[:, None] - centers[None, :]) / 0.4) ** 2)
    return (radial_basis, harmonics(unit_dirs))

def radial(radial_basis, first_layer, second_layer):
    hidden = jax.nn.silu(jnp.dot(radial_basis, first_layer, precision=HIGHEST))
    return jnp.dot(hidden, second_layer, precision=HIGHEST)

def spread(values, axis):
    return jnp.repeat(values, np.array(DEGREES), axis=axis, total_repeat_length=COMP)

def update_layer(table, radial_first, radial_second, mixing, vectors, source, target):
    blocks = source.shape[0] // BLOCK

    def edge_step(running, pieces):
        vector_block, source_block, target_block = pieces
        radial_basis, angular = geometry(vector_block)
        weights = radial(radial_basis, radial_first, radial_second).reshape(-1, 2, 5, CHANNELS)
        self_weight = spread(weights[:, 0], 1)
        cross = spread(weights[:, 1], 1)
        sender = table[source_block]
        message = self_weight * sender + cross * sender[:, 0:1, :] * angular[:, :, None]
        return (running.at[target_block].add(message), None)
    scanned = (vectors.reshape(3, blocks, BLOCK).transpose(1, 0, 2), source.reshape(blocks, BLOCK), target.reshape(blocks, BLOCK))
    start = jnp.zeros((ATOMS_DEV + 1, COMP, CHANNELS), jnp.float32)
    running, _ = lax.scan(jax.checkpoint(edge_step), start, scanned)
    gathered = running[:ATOMS_DEV] / NEIGHBOURS
    mixed_list = []
    for degree in range(5):
        part_in = gathered[:, STARTS[degree]:STARTS[degree] + DEGREES[degree]]
        mixed_list.append(jnp.einsum('amc,cd->amd', part_in, mixing[degree], precision=HIGHEST))
    mixed_out = jnp.concatenate(mixed_list, axis=1)
    previous = table[:ATOMS_DEV]
    scalar = previous[:, 0:1] + jax.nn.silu(mixed_out[:, 0:1])
    higher = previous[:, 1:] + mixed_out[:, 1:] * jax.nn.sigmoid(mixed_out[:, 0:1])
    return jnp.concatenate([scalar, higher], axis=1).astype(jnp.bfloat16)

def readout(table, probe_first, probe_second, readout_first, readout_second, vectors, atoms, grid, index):
    blocks = atoms.shape[0] // BLOCK

    def probe_block(pieces):
        vector_block, atom_block = pieces
        radial_basis, angular = geometry(vector_block)
        weights = spread(radial(radial_basis, probe_first, probe_second).reshape(-1, 5, CHANNELS), 1)
        sender = table[atom_block]
        contribution = lax.optimization_barrier(jnp.sum(weights * sender * angular[:, :, None], axis=1))
        return contribution.reshape(-1, PROBE_EDGES, CHANNELS).sum(axis=1)
    scanned = (vectors.reshape(3, blocks, BLOCK).transpose(1, 0, 2), atoms.reshape(blocks, BLOCK))
    summed = lax.map(jax.checkpoint(probe_block), scanned).reshape(-1, CHANNELS)
    hidden = jax.nn.silu(jnp.dot(summed, readout_first, precision=HIGHEST))
    density = jnp.dot(hidden, readout_second, precision=HIGHEST)
    misfit = density - grid[index]
    return jnp.sum(misfit * misfit) / (2.0 * index.shape[0])

def pick_rows(source_rows, chosen):
    return source_rows[chosen]

def tables(atom_field, send_index):
    zero_row = jnp.zeros(atom_field.shape[:2] + (1,) + atom_field.shape[3:], atom_field.dtype)
    padded = jnp.concatenate([atom_field, zero_row], axis=2)
    pieces_list = [padded]
    for step_x, step_y in OFFSETS:
        neighbour = jnp.roll(padded, (-step_x, -step_y), axis=(0, 1))
        send_lists = jnp.roll(send_index, (-step_x, -step_y), axis=(0, 1))[:, :, 1 - step_x, 1 - step_y]
        pieces_list.append(jax.vmap(jax.vmap(pick_rows))(neighbour, send_lists))
    whole = jnp.concatenate(pieces_list, axis=2)
    return whole.reshape((-1,) + whole.shape[2:])

def flatten(array):
    return array.reshape((N_BX * N_BY,) + array.shape[2:])

def reference(features, send_index, atom_vectors, atom_source, atom_target, probe_vectors, probe_atoms, density_grid, probe_index, radial_first, radial_second, mixing, probe_first, probe_second, readout_first, readout_second):

    def forward(atom_field, first_radial, second_radial, channel_mix, first_probe, second_probe, first_readout, second_readout):
        first_table = tables(atom_field, send_index)

        def one_layer(pieces):
            table, vectors, source, target = pieces
            return update_layer(table, first_radial, second_radial, channel_mix, vectors, source, target)
        updated = lax.map(jax.checkpoint(one_layer), (first_table, flatten(atom_vectors), flatten(atom_source), flatten(atom_target)))
        second_table = tables(updated.astype(jnp.float32).reshape(N_BX, N_BY, ATOMS_DEV, COMP, CHANNELS), send_index)

        def one_probe(pieces):
            table, vectors, atoms, grid, index = pieces
            return readout(table, first_probe, second_probe, first_readout, second_readout, vectors, atoms, grid, index)
        losses = lax.map(jax.checkpoint(one_probe), (second_table, flatten(probe_vectors), flatten(probe_atoms), flatten(density_grid), flatten(probe_index)))
        return jnp.sum(losses)
    loss_value, pullback = jax.vjp(forward, features.astype(jnp.float32), radial_first, radial_second, mixing, probe_first, probe_second, readout_first, readout_second)
    gradients = pullback(jnp.ones_like(loss_value))
    return (loss_value, gradients[0], gradients[1], gradients[2], gradients[3], gradients[4], gradients[5], gradients[6], gradients[7])
```

```python
import functools

import jax
import jax.numpy as jnp
from jax import lax
from jax.experimental import pallas as pl
from jax.experimental.pallas import tpu as pltpu
from jax.sharding import PartitionSpec as P

C = 128
COMP = 25
BASIS = 20
HIDDEN = 64
ATOMS = 128
EDGES = 1024
PEDGES = 512
PROBES = 128
WIDE = COMP * C
EB = 256
DEGREES = (1, 3, 5, 7, 9)
STARTS = (0, 1, 4, 9, 16)
HIGHEST = lax.Precision.HIGHEST
F32 = jnp.float32
BF16 = jnp.bfloat16
REDUCE_ROWS = 2048


def dot(a, b):
    return jnp.dot(a, b, preferred_element_type=F32)


def dot_exact(a, b):
    return jnp.dot(a, b, preferred_element_type=F32, precision=HIGHEST)


def dot_nt(a, b, precision=None):
    return lax.dot_general(
        a, b, (((1,), (1,)), ((), ())), preferred_element_type=F32, precision=precision
    )


def dot_tn(a, b, precision=None):
    return lax.dot_general(
        a, b, (((0,), (0,)), ((), ())), preferred_element_type=F32, precision=precision
    )


def split(a):
    high = a.astype(BF16)
    return high, (a - high.astype(F32)).astype(BF16)


def sigmoid(a):
    return 1.0 / (1.0 + jnp.exp(-a))


def cols(component):
    return slice(component * C, (component + 1) * C)


def chunks(degree):
    first = STARTS[degree]
    last = first + DEGREES[degree]
    return [(at, min(at + 2, last)) for at in range(first, last, 2)]


def harmonics(x, y, z):
    z_square = z * z
    return [
        jnp.ones_like(x),
        1.7320508 * y,
        1.7320508 * z,
        1.7320508 * x,
        3.8729833 * x * y,
        3.8729833 * y * z,
        1.118034 * (3.0 * z_square - 1.0),
        3.8729833 * x * z,
        1.9364917 * (x * x - y * y),
        2.0916501 * y * (3.0 * x * x - y * y),
        10.246951 * x * y * z,
        1.6201852 * y * (5.0 * z_square - 1.0),
        1.3228757 * z * (5.0 * z_square - 3.0),
        1.6201852 * x * (5.0 * z_square - 1.0),
        5.1234754 * z * (x * x - y * y),
        2.0916501 * x * (x * x - 3.0 * y * y),
        8.8741197 * x * y * (x * x - y * y),
        6.2749502 * y * z * (3.0 * x * x - y * y),
        3.354102 * x * y * (7.0 * z_square - 1.0),
        2.3717082 * y * z * (7.0 * z_square - 3.0),
        0.375 * (35.0 * z_square * z_square - 30.0 * z_square + 3.0),
        2.3717082 * x * z * (7.0 * z_square - 3.0),
        1.677051 * (x * x - y * y) * (7.0 * z_square - 1.0),
        6.2749502 * x * z * (x * x - 3.0 * y * y),
        2.2185299 * (x * x * x * x - 6.0 * x * x * y * y + y * y * y * y),
    ]


def pack_kernel(features, send_row, own, low, middle, high, wide):
    for row in range(0, ATOMS, 16):
        wide[pl.ds(row, 16), 0:COMP, :] = features[pl.ds(row, 16)].astype(F32)
    atom_at = lax.broadcasted_iota(jnp.int32, (ATOMS, C), 0)
    chosen = (send_row[...] == atom_at).astype(F32).T.astype(BF16)
    for component in range(COMP):
        rows = wide[:, component, :].astype(BF16)
        own[:, cols(component)] = rows
        packet = dot(chosen, rows).astype(BF16)
        low[:, cols(component)] = packet[0:48]
        middle[:, cols(component)] = packet[48:80]
        high[:, cols(component)] = packet[80:128]


def geometry(vectors, index_rows, edges, turned, basis_out):
    x, y, z = vectors[0:1], vectors[1:2], vectors[2:3]
    radius = jnp.sqrt(x * x + y * y + z * z)
    rows = harmonics(x / radius, y / radius, z / radius) + index_rows
    for at, row in enumerate(rows):
        turned[at : at + 1, :] = row
    center = 0.5 + 4.0 * lax.broadcasted_iota(jnp.int32, (24, edges), 0).astype(F32) / (BASIS - 1)
    offset = (radius - center) / 0.4
    basis = jnp.exp(-(offset * offset))
    live = lax.broadcasted_iota(jnp.int32, (24, edges), 0) < BASIS
    basis_out[...] = jnp.where(live, basis, 0.0)
    return turned[...].T


def prepare_kernel(
    vectors,
    source,
    target,
    probe_vectors,
    probe_atoms,
    grid,
    probe_index,
    first,
    second,
    pfirst,
    psecond,
    columns_out,
    basis_out,
    pre_out,
    hidden3_out,
    second3_out,
    pcolumns_out,
    pbasis_out,
    ppre_out,
    phidden3_out,
    psecond3_out,
    picked_out,
    turned,
    pturned,
):
    turned[...] = jnp.zeros_like(turned)
    pturned[...] = jnp.zeros_like(pturned)
    row = source[...]
    slot = jnp.where(row > ATOMS, row - 1, jnp.where(row == ATOMS, 512, row))
    columns_out[...] = geometry(
        vectors[...], [slot.astype(F32), target[...].astype(F32)], EDGES, turned, basis_out
    )
    prow = probe_atoms[...]
    pslot = jnp.where(prow > ATOMS, prow - 1, jnp.where(prow == ATOMS, 512, prow))
    pcolumns_out[...] = geometry(
        probe_vectors[...], [pslot.astype(F32)], PEDGES, pturned, pbasis_out
    )

    for basis, layer, pre, hidden3 in (
        (basis_out, first, pre_out, hidden3_out),
        (pbasis_out, pfirst, ppre_out, phidden3_out),
    ):
        before = dot_tn(layer[...], basis[0:BASIS, :], HIGHEST)
        pre[...] = before
        hidden = (before * sigmoid(before)).T
        upper, lower = split(hidden)
        hidden3[:, 0:HIDDEN] = upper
        hidden3[:, HIDDEN : 2 * HIDDEN] = upper
        hidden3[:, 2 * HIDDEN : 3 * HIDDEN] = lower
    for degree in range(5):
        for path in range(2):
            upper, lower = split(second[:, cols(path * 5 + degree)])
            at = cols(2 * degree + path)
            second3_out[0:HIDDEN, at] = upper
            second3_out[HIDDEN : 2 * HIDDEN, at] = lower
            second3_out[2 * HIDDEN : 3 * HIDDEN, at] = upper
    upper, lower = split(psecond[...])
    psecond3_out[0:HIDDEN, :] = upper
    psecond3_out[HIDDEN : 2 * HIDDEN, :] = lower
    psecond3_out[2 * HIDDEN : 3 * HIDDEN, :] = upper

    place = probe_index[...]
    grid_row = lax.broadcasted_iota(jnp.int32, (grid.shape[0], PROBES), 0)
    hit = (place // C == grid_row).astype(F32)
    lines = dot_tn(grid[...], hit, HIGHEST)
    lane = lax.broadcasted_iota(jnp.int32, (C, PROBES), 0)
    values = jnp.sum(jnp.where(place % C == lane, lines, 0.0), axis=0, keepdims=True)
    picked_out[...] = jnp.broadcast_to(values, (C, PROBES)).T


def fill_table(table, own, low, high, left, right):
    table[0:ATOMS, :] = own[...]
    pieces = (
        left[16:32],
        low[16:32],
        right[16:32],
        left[0:16],
        right[0:16],
        left[32:48],
        high[16:32],
        right[32:48],
    )
    for at, piece in enumerate(pieces):
        table[ATOMS + 16 * at : ATOMS + 16 * at + 16, :] = piece


def one_hot_lanes(column, width):
    lane = lax.broadcasted_iota(jnp.int32, (EB, width), 1).astype(F32)
    return (column == lane).astype(F32).astype(BF16)


def one_hot_rows(row, height):
    place = lax.broadcasted_iota(jnp.int32, (height, row.shape[1]), 0)
    return (row == place).astype(F32).astype(BF16)


def fold_source(row):
    return jnp.where(row > ATOMS, row - 1, jnp.where(row == ATOMS, 512, row))


def layer_kernel(
    own,
    low,
    high,
    left,
    right,
    columns,
    target,
    hidden3,
    second3,
    mixing,
    send_row,
    updated,
    gathered,
    mixed,
    table_out,
    low_out,
    middle_out,
    high_out,
):
    table = table_out
    fill_table(table, own, low, high, left, right)
    gathered[...] = jnp.zeros_like(gathered)

    def block(step, carry):
        at = pl.multiple_of(step * EB, EB)
        rows = pl.ds(at, EB)
        column = columns[rows, :]
        pick = one_hot_lanes(column[:, 25:26], 2 * ATOMS)
        put = one_hot_rows(target[:, rows], ATOMS)
        hidden = hidden3[rows, :]
        scalar = dot(pick, table[:, cols(0)])
        for degree in range(5):
            weight = dot(hidden, second3[:, 2 * degree * C : 2 * (degree + 1) * C])
            straight = weight[:, 0:C]
            cross = weight[:, C:] * scalar
            for first, last in chunks(degree):
                sender = dot(pick, table[:, first * C : last * C])
                parts = []
                for component in range(first, last):
                    value = sender[:, cols(component - first)]
                    message = straight * value + cross * column[:, component : component + 1]
                    parts.append(message.astype(BF16))
                both = parts[0] if len(parts) == 1 else jnp.concatenate(parts, axis=1)
                gathered[:, first * C : last * C] += dot(put, both)
        return carry

    lax.fori_loop(0, EDGES // EB, block, 0)

    chosen = (send_row[...] == lax.broadcasted_iota(jnp.int32, (ATOMS, C), 0)).astype(F32)
    chosen = chosen.T.astype(BF16)
    gate = None
    for degree in range(5):
        weight = mixing[degree]
        for component in range(STARTS[degree], STARTS[degree] + DEGREES[degree]):
            here = gathered[:, cols(component)] * 0.125
            gathered[:, cols(component)] = here
            out = dot_exact(here, weight)
            mixed[:, cols(component)] = out
            if component == 0:
                gate = sigmoid(out)
            new = (own[:, cols(component)].astype(F32) + out * gate).astype(BF16)
            updated[:, cols(component)] = new
            packet = dot(chosen, new).astype(BF16)
            low_out[:, cols(component)] = packet[0:48]
            middle_out[:, cols(component)] = packet[48:80]
            high_out[:, cols(component)] = packet[80:128]


def probe_kernel(
    own,
    low,
    high,
    left,
    right,
    columns,
    atoms,
    hidden3,
    second3,
    first_readout,
    second_readout,
    picked,
    grad_own,
    low_out,
    middle_out,
    high_out,
    weight_grad,
    readout_grads,
    table,
    partial,
    contribution,
    grad_table,
):
    fill_table(table, own, low, high, left, right)

    def forward(step, carry):
        rows = pl.ds(pl.multiple_of(step * EB, EB), EB)
        column = columns[rows, :]
        pick = one_hot_lanes(column[:, 25:26], 2 * ATOMS)
        hidden = hidden3[rows, :]
        total = jnp.zeros((EB, C), F32)
        for degree in range(5):
            weight = dot(hidden, second3[:, cols(degree)])
            here = jnp.zeros((EB, C), F32)
            for first, last in chunks(degree):
                sender = dot(pick, table[:, first * C : last * C])
                for component in range(first, last):
                    value = sender[:, cols(component - first)]
                    here = here + value * column[:, component : component + 1]
            partial[rows, cols(degree)] = here
            total = total + weight * here
        contribution[rows, :] = total
        return carry

    lax.fori_loop(0, PEDGES // EB, forward, 0)

    edge = lax.broadcasted_iota(jnp.int32, (PROBES, PEDGES), 1)
    probe = lax.broadcasted_iota(jnp.int32, (PROBES, PEDGES), 0)
    pool = (edge // 4 == probe).astype(F32)
    summed = dot_exact(pool, contribution[...])
    before = dot_exact(summed, first_readout[...])
    gate = sigmoid(before)
    hidden = before * gate
    vector = second_readout[...]
    density = jnp.sum(hidden * vector, axis=1, keepdims=True)
    misfit = density - picked[...]
    loss = jnp.sum(misfit[:, 0:1] * misfit[:, 0:1], axis=0, keepdims=True) / (2.0 * PROBES)
    slope = misfit / PROBES
    d_before = slope * vector * gate * (1.0 + before * (1.0 - gate))
    readout_grads[0:C, :] = dot_tn(summed, d_before, HIGHEST)
    readout_grads[C : C + 8, :] = jnp.broadcast_to(
        jnp.sum(hidden * slope, axis=0, keepdims=True), (8, C)
    )
    readout_grads[C + 8 : C + 16, :] = jnp.broadcast_to(loss, (8, C))
    d_summed = dot_nt(d_before, first_readout[...], HIGHEST)
    contribution[...] = dot_tn(pool, d_summed, HIGHEST)
    grad_table[...] = jnp.zeros_like(grad_table)

    def backward(step, carry):
        rows = pl.ds(pl.multiple_of(step * EB, EB), EB)
        column = columns[rows, :]
        put = one_hot_rows(fold_source(atoms[:, rows]), 2 * ATOMS)
        hidden = hidden3[rows, :]
        slope_here = contribution[rows, :]
        for degree in range(5):
            weight = dot(hidden, second3[:, cols(degree)])
            weight_grad[rows, cols(degree)] = slope_here * partial[rows, cols(degree)]
            down = slope_here * weight
            for first, last in chunks(degree):
                parts = []
                for component in range(first, last):
                    parts.append((down * column[:, component : component + 1]).astype(BF16))
                both = parts[0] if len(parts) == 1 else jnp.concatenate(parts, axis=1)
                grad_table[:, first * C : last * C] += dot(put, both)
        return carry

    lax.fori_loop(0, PEDGES // EB, backward, 0)
    grad_own[...] = grad_table[0:ATOMS, :]
    low_out[...] = grad_table[ATOMS : ATOMS + 48, :].astype(BF16)
    middle_out[...] = grad_table[ATOMS + 48 : ATOMS + 80, :].astype(BF16)
    high_out[...] = grad_table[ATOMS + 80 :, :].astype(BF16)


def network_grads(weight_grad, basis, pre, hidden3, second_rows, out_second, out_first):
    hidden = hidden3[:, 0:HIDDEN].astype(F32) + hidden3[:, 2 * HIDDEN :].astype(F32)
    upper, lower = split(hidden)
    turned = None
    for at, block, row in second_rows:
        grad_upper, grad_lower = split(weight_grad[:, at])
        out_second(
            row, dot_tn(upper, grad_upper) + dot_tn(lower, grad_upper) + dot_tn(upper, grad_lower)
        )
        block_upper, block_lower = split(block)
        piece = (
            dot_nt(block_upper, grad_upper)
            + dot_nt(block_lower, grad_upper)
            + dot_nt(block_upper, grad_lower)
        )
        turned = piece if turned is None else turned + piece
    before = pre[...]
    gate = sigmoid(before)
    d_before = turned * gate * (1.0 + before * (1.0 - gate))
    out_first(dot_nt(basis[...], d_before, HIGHEST))


def probe_network_kernel(weight_grad, basis, pre, hidden3, second, readout_grads, out):
    def out_second(row, value):
        out[row * HIDDEN : (row + 1) * HIDDEN, :] = value

    def out_first(value):
        out[448:512, :] = jnp.zeros((64, C), F32)
        out[464:488, 0:HIDDEN] = value

    rows = [(cols(degree), second[:, cols(degree)], degree) for degree in range(5)]
    network_grads(weight_grad, basis, pre, hidden3, rows, out_second, out_first)
    out[320:464, :] = readout_grads[...]


def add_returned(send_row, low, high, left, right, start, stop):
    pieces = (
        left[16:32, start:stop],
        low[16:32, start:stop],
        right[16:32, start:stop],
        left[0:16, start:stop],
        right[0:16, start:stop],
        left[32:48, start:stop],
        high[16:32, start:stop],
        right[32:48, start:stop],
    )
    return dot(one_hot_rows(send_row[...], ATOMS), jnp.concatenate(pieces, axis=0))


def layer_back_kernel(
    grad_own,
    low,
    high,
    left,
    right,
    table,
    gathered,
    mixed,
    columns,
    source,
    basis,
    pre,
    hidden3,
    second3,
    second,
    mixing,
    send_row,
    probe_grads,
    field_grad,
    low_out,
    middle_out,
    high_out,
    reduced,
    d_gathered,
    grad_table,
    weight_grad,
):
    gate_in = mixed[:, cols(0)]
    gate = sigmoid(gate_in)
    d_gate = jnp.zeros((ATOMS, C), F32)
    for degree in (4, 3, 2, 1, 0):
        weight = mixing[degree]
        d_mixing = jnp.zeros((C, C), F32)
        for component in range(STARTS[degree], STARTS[degree] + DEGREES[degree]):
            at = cols(component)
            whole = grad_own[:, at] + add_returned(
                send_row, low, high, left, right, component * C, (component + 1) * C
            )
            d_updated = whole.astype(BF16).astype(F32)
            field_grad[:, at] = d_updated
            if component > 0:
                d_gate = d_gate + d_updated * mixed[:, at]
                d_mixed = d_updated * gate
            else:
                d_mixed = d_updated * gate * (1.0 + gate_in * (1.0 - gate)) + d_gate * gate * (
                    1.0 - gate
                )
            d_mixing = d_mixing + dot_tn(gathered[:, at], d_mixed, HIGHEST)
            d_gathered[:, at] = (dot_nt(d_mixed, weight, HIGHEST) * 0.125).astype(BF16)
        reduced[640 + degree * C : 640 + (degree + 1) * C, :] = d_mixing

    grad_table[...] = jnp.zeros_like(grad_table)

    def block(step, carry):
        rows = pl.ds(pl.multiple_of(step * EB, EB), EB)
        column = columns[rows, :]
        pick = one_hot_lanes(column[:, 25:26], 2 * ATOMS)
        pick_target = one_hot_lanes(column[:, 26:27], ATOMS)
        put = one_hot_rows(fold_source(source[:, rows]), 2 * ATOMS)
        hidden = hidden3[rows, :]
        scalar = dot(pick, table[:, cols(0)])
        d_scalar = jnp.zeros((EB, C), F32)
        for degree in (4, 3, 2, 1, 0):
            weight = dot(hidden, second3[:, 2 * degree * C : 2 * (degree + 1) * C])
            straight = weight[:, 0:C]
            d_straight = jnp.zeros((EB, C), F32)
            d_cross = jnp.zeros((EB, C), F32)
            for first, last in chunks(degree):
                wide = slice(first * C, last * C)
                sender = dot(pick, table[:, wide])
                d_message = dot(pick_target, d_gathered[:, wide])
                parts = []
                for component in range(first, last):
                    here = cols(component - first)
                    d_here = d_message[:, here]
                    d_straight = d_straight + d_here * sender[:, here]
                    d_cross = d_cross + d_here * column[:, component : component + 1]
                    parts.append(straight * d_here)
                if degree == 0:
                    d_scalar = d_scalar + d_cross * weight[:, C:]
                    parts[0] = parts[0] + d_scalar
                parts = [part.astype(BF16) for part in parts]
                both = parts[0] if len(parts) == 1 else jnp.concatenate(parts, axis=1)
                grad_table[:, wide] += dot(put, both)
            weight_grad[rows, cols(2 * degree)] = d_straight
            weight_grad[rows, cols(2 * degree + 1)] = d_cross * scalar
            if degree > 0:
                d_scalar = d_scalar + d_cross * weight[:, C:]
        return carry

    lax.fori_loop(0, EDGES // EB, block, 0)
    field_grad[...] += grad_table[0:ATOMS, :]
    low_out[...] = grad_table[ATOMS : ATOMS + 48, :].astype(BF16)
    middle_out[...] = grad_table[ATOMS + 48 : ATOMS + 80, :].astype(BF16)
    high_out[...] = grad_table[ATOMS + 80 :, :].astype(BF16)

    def out_second(row, value):
        reduced[row * HIDDEN : (row + 1) * HIDDEN, :] = value

    def out_first(value):
        reduced[1792:2048, :] = jnp.zeros((256, C), F32)
        reduced[1792:1816, 0:HIDDEN] = value

    rows = []
    for degree in range(5):
        for path in range(2):
            rows.append((cols(2 * degree + path), second[:, cols(path * 5 + degree)], path * 5 + degree))
    network_grads(weight_grad, basis, pre, hidden3, rows, out_second, out_first)
    reduced[1280:1792, :] = probe_grads[...]


def finish_kernel(field_grad, low, high, left, right, send_row, out):
    for component in range(COMP):
        out[:, component, :] = field_grad[:, cols(component)] + add_returned(
            send_row, low, high, left, right, component * C, (component + 1) * C
        )


def unpack_kernel(sums, loss, first, second, mixing, pfirst, psecond, readout, vector):
    for block in range(10):
        second[:, cols(block)] = sums[block * HIDDEN : (block + 1) * HIDDEN, :]
    for degree in range(5):
        mixing[degree] = sums[640 + degree * C : 640 + (degree + 1) * C, :]
        psecond[:, cols(degree)] = sums[1280 + degree * HIDDEN : 1280 + (degree + 1) * HIDDEN, :]
    readout[...] = sums[1600:1728, :]
    vector[...] = sums[1728:1729, :]
    loss[...] = sums[1736:1737, :]
    pfirst[...] = sums[1744 : 1744 + BASIS, 0:HIDDEN]
    first[...] = sums[1792 : 1792 + BASIS, 0:HIDDEN]


def call(kernel, outs, scratch, flops, *operands):
    shapes = [jax.ShapeDtypeStruct(shape, dtype) for shape, dtype in outs]
    moved = sum(x.size * x.dtype.itemsize for x in list(operands) + shapes)
    whole = pl.BlockSpec(memory_space=pltpu.VMEM)
    return pl.pallas_call(
        kernel,
        out_shape=shapes,
        in_specs=[whole] * len(operands),
        out_specs=[whole] * len(shapes),
        scratch_shapes=[pltpu.VMEM(shape, dtype) for shape, dtype in scratch],
        compiler_params=pltpu.CompilerParams(vmem_limit_bytes=50 * 1024 * 1024),
        cost_estimate=pl.CostEstimate(flops=flops, bytes_accessed=moved, transcendentals=0),
    )(*operands)


PACKETS = [((48, WIDE), BF16), ((32, WIDE), BF16), ((48, WIDE), BF16)]


def ring(axis):
    count = lax.axis_size(axis)
    up = [(i, (i + 1) % count) for i in range(count)]
    down = [(b, a) for a, b in up]
    return up, down


def exchange(low_packet, middle_packet, high_packet):
    up, down = ring("bx")
    low = lax.ppermute(high_packet, "bx", up)
    high = lax.ppermute(low_packet, "bx", down)
    up, down = ring("by")
    left = lax.ppermute(
        jnp.concatenate([middle_packet[16:32], low[32:48], high[32:48]]), "by", up
    )
    right = lax.ppermute(jnp.concatenate([middle_packet[0:16], low[0:16], high[0:16]]), "by", down)
    return low, high, left, right


def reduce_all(values):
    n_x, n_y = lax.axis_size("bx"), lax.axis_size("by")
    half = n_x * n_y // 2
    axes = ("bx", "by")
    swap = [(i, i ^ 1) for i in range(n_y)]
    groups = [[2 * i + core for i in range(half)] for core in range(2)]
    core = lax.axis_index("by") % 2
    halves = values.reshape(2, half, -1, C)
    mine = lax.dynamic_index_in_dim(halves, core, 0, False)
    other = lax.dynamic_index_in_dim(halves, 1 - core, 0, False)
    pair = mine + lax.ppermute(other, "by", swap)
    pieces = lax.all_to_all(pair, axes, 0, 0, axis_index_groups=groups, tiled=True)
    share = jnp.sum(pieces, axis=0)
    spread = jnp.broadcast_to(share[None], pair.shape)
    mine = lax.all_to_all(spread, axes, 0, 0, axis_index_groups=groups, tiled=True)
    other = lax.ppermute(mine, "by", swap)
    both = jnp.where(core == 0, jnp.stack([mine, other]), jnp.stack([other, mine]))
    return both.reshape(REDUCE_ROWS, C)


def on_device(
    features,
    send_index,
    atom_vectors,
    atom_source,
    atom_target,
    probe_vectors,
    probe_atoms,
    density_grid,
    probe_index,
    radial_first,
    radial_second,
    mixing,
    probe_first,
    probe_second,
    readout_first,
    readout_second,
):
    field = features[0, 0]
    slots = send_index.reshape(1, 144)
    send_row = jnp.concatenate([slots[:, 0:64], slots[:, 80:144]], axis=1)
    source = atom_source.reshape(1, EDGES)
    target = atom_target.reshape(1, EDGES)
    atoms = probe_atoms.reshape(1, PEDGES)

    own, *packets = call(
        pack_kernel,
        [((ATOMS, WIDE), BF16)] + PACKETS,
        [((ATOMS, 32, C), F32)],
        2 * C * C * WIDE,
        field,
        send_row,
    )
    received = exchange(*packets)
    (
        columns,
        basis,
        pre,
        hidden3,
        second3,
        pcolumns,
        pbasis,
        ppre,
        phidden3,
        psecond3,
        picked,
    ) = call(
        prepare_kernel,
        [
            ((EDGES, C), F32),
            ((24, EDGES), F32),
            ((HIDDEN, EDGES), F32),
            ((EDGES, 3 * HIDDEN), BF16),
            ((3 * HIDDEN, 10 * C), BF16),
            ((PEDGES, C), F32),
            ((24, PEDGES), F32),
            ((HIDDEN, PEDGES), F32),
            ((PEDGES, 3 * HIDDEN), BF16),
            ((3 * HIDDEN, 5 * C), BF16),
            ((PROBES, C), F32),
        ],
        [((C, EDGES), F32), ((C, PEDGES), F32)],
        10**9,
        atom_vectors[0, 0],
        source,
        target,
        probe_vectors[0, 0],
        atoms,
        density_grid.reshape(-1, C),
        probe_index.reshape(1, PROBES),
        radial_first,
        radial_second,
        probe_first,
        probe_second,
    )
    updated, gathered, mixed, table, *packets = call(
        layer_kernel,
        [
            ((ATOMS, WIDE), BF16),
            ((ATOMS, WIDE), F32),
            ((ATOMS, WIDE), F32),
            ((2 * ATOMS, WIDE), BF16),
        ]
        + PACKETS,
        [],
        4 * 10**9,
        own,
        *received,
        columns,
        target,
        hidden3,
        second3,
        mixing,
        send_row,
    )
    received = exchange(*packets)
    grad_own, low, middle, high, weight_grad, readout_grads = call(
        probe_kernel,
        [((ATOMS, WIDE), F32)]
        + PACKETS
        + [
            ((PEDGES, 5 * C), F32),
            ((C + 16, C), F32),
        ],
        [
            ((2 * ATOMS, WIDE), BF16),
            ((PEDGES, 5 * C), F32),
            ((PEDGES, C), F32),
            ((2 * ATOMS, WIDE), F32),
        ],
        4 * 10**9,
        updated,
        *received,
        pcolumns,
        atoms,
        phidden3,
        psecond3,
        readout_first,
        readout_second.reshape(1, C),
        picked,
    )
    received = exchange(low, middle, high)
    (probe_grads,) = call(
        probe_network_kernel,
        [((512, C), F32)],
        [],
        10**9,
        weight_grad,
        pbasis,
        ppre,
        phidden3,
        probe_second,
        readout_grads,
    )
    field_grad, low, middle, high, reduced = call(
        layer_back_kernel,
        [((ATOMS, WIDE), F32)] + PACKETS + [((REDUCE_ROWS, C), F32)],
        [
            ((ATOMS, WIDE), BF16),
            ((2 * ATOMS, WIDE), F32),
            ((EDGES, 10 * C), F32),
        ],
        8 * 10**9,
        grad_own,
        *received,
        table,
        gathered,
        mixed,
        columns,
        source,
        basis,
        pre,
        hidden3,
        second3,
        radial_second,
        mixing,
        send_row,
        probe_grads,
    )
    received = exchange(low, middle, high)
    sums = reduce_all(reduced)
    (feature_grad,) = call(
        finish_kernel,
        [((ATOMS, COMP, C), F32)],
        [],
        2 * C * C * WIDE,
        field_grad,
        *received,
        send_row,
    )
    loss, first, second, mixing_grad, pfirst, psecond, readout, vector = call(
        unpack_kernel,
        [
            ((1, C), F32),
            ((BASIS, HIDDEN), F32),
            ((HIDDEN, 10 * C), F32),
            ((5, C, C), F32),
            ((BASIS, HIDDEN), F32),
            ((HIDDEN, 5 * C), F32),
            ((C, C), F32),
            ((1, C), F32),
        ],
        [],
        10**6,
        sums,
    )
    return (
        loss[0, 0],
        feature_grad[None, None],
        first,
        second,
        mixing_grad,
        pfirst,
        psecond,
        readout,
        vector[0],
    )


def solution(mesh):
    brick = [P("bx", "by", *([None] * (rank - 2))) for rank in (5, 5, 4, 3, 3, 4, 3, 3, 3)]
    in_specs = tuple(brick) + (P(),) * 7
    out_specs = (P(), P("bx", "by", None, None, None)) + (P(),) * 7
    return jax.shard_map(
        on_device, mesh=mesh, in_specs=in_specs, out_specs=out_specs, check_vma=False
    )
```

```python
import functools

import jax
import jax.numpy as jnp
from jax import lax
from jax.experimental import pallas as pl
from jax.experimental.pallas import tpu as pltpu
from jax.sharding import PartitionSpec as P

C = 128
COMP = 25
BASIS = 20
HIDDEN = 64
ATOMS = 128
EDGES = 1024
PEDGES = 512
PROBES = 128
WIDE = COMP * C
EB = 256
DEGREES = (1, 3, 5, 7, 9)
STARTS = (0, 1, 4, 9, 16)
HIGHEST = lax.Precision.HIGHEST
F32 = jnp.float32
BF16 = jnp.bfloat16
REDUCE_ROWS = 2048


def dot(a, b):
    return jnp.dot(a, b, preferred_element_type=F32)


def dot_exact(a, b):
    return jnp.dot(a, b, preferred_element_type=F32, precision=HIGHEST)


def dot_nt(a, b, precision=None):
    return lax.dot_general(
        a, b, (((1,), (1,)), ((), ())), preferred_element_type=F32, precision=precision
    )


def dot_tn(a, b, precision=None):
    return lax.dot_general(
        a, b, (((0,), (0,)), ((), ())), preferred_element_type=F32, precision=precision
    )


def split(a):
    high = a.astype(BF16)
    return high, (a - high.astype(F32)).astype(BF16)


def sigmoid(a):
    return 1.0 / (1.0 + jnp.exp(-a))


def cols(component):
    return slice(component * C, (component + 1) * C)


def chunks(degree):
    first = STARTS[degree]
    last = first + DEGREES[degree]
    return [(at, min(at + 2, last)) for at in range(first, last, 2)]


def harmonics(x, y, z):
    z_square = z * z
    return [
        jnp.ones_like(x),
        1.7320508 * y,
        1.7320508 * z,
        1.7320508 * x,
        3.8729833 * x * y,
        3.8729833 * y * z,
        1.118034 * (3.0 * z_square - 1.0),
        3.8729833 * x * z,
        1.9364917 * (x * x - y * y),
        2.0916501 * y * (3.0 * x * x - y * y),
        10.246951 * x * y * z,
        1.6201852 * y * (5.0 * z_square - 1.0),
        1.3228757 * z * (5.0 * z_square - 3.0),
        1.6201852 * x * (5.0 * z_square - 1.0),
        5.1234754 * z * (x * x - y * y),
        2.0916501 * x * (x * x - 3.0 * y * y),
        8.8741197 * x * y * (x * x - y * y),
        6.2749502 * y * z * (3.0 * x * x - y * y),
        3.354102 * x * y * (7.0 * z_square - 1.0),
        2.3717082 * y * z * (7.0 * z_square - 3.0),
        0.375 * (35.0 * z_square * z_square - 30.0 * z_square + 3.0),
        2.3717082 * x * z * (7.0 * z_square - 3.0),
        1.677051 * (x * x - y * y) * (7.0 * z_square - 1.0),
        6.2749502 * x * z * (x * x - 3.0 * y * y),
        2.2185299 * (x * x * x * x - 6.0 * x * x * y * y + y * y * y * y),
    ]


def pack_kernel(features, send_index, own, low, middle, high, chosen_out, placed_out, lists):
    lists[...] = jnp.zeros_like(lists)
    for at in range(8):
        i, j = divmod(at if at < 4 else at + 1, 3)
        lists[at : at + 1, 0:16] = send_index[i, j : j + 1, :].astype(F32)
    turned = lists[...].T
    lane = lax.broadcasted_iota(jnp.int32, (16, C), 1).astype(F32)
    hits = [(turned[0:16, at : at + 1] == lane).astype(F32) for at in range(8)]
    chosen = jnp.concatenate(hits, axis=0)
    chosen_out[...] = chosen.astype(BF16)
    placed_out[...] = chosen.T.astype(BF16)
    for component in range(COMP):
        own[:, cols(component)] = features[component]
    send_packets(chosen_out[...], own, low, middle, high)


def send_packets(chosen, rows, low, middle, high):
    for first in range(0, COMP, 2):
        wide = slice(first * C, min(first + 2, COMP) * C)
        packet = dot(chosen, rows[:, wide]).astype(BF16)
        low[:, wide] = packet[0:48]
        middle[:, wide] = packet[48:80]
        high[:, wide] = packet[80:128]


def geometry(vectors, index_rows, edges, turned, basis_out):
    x, y, z = vectors[0:1], vectors[1:2], vectors[2:3]
    radius = jnp.sqrt(x * x + y * y + z * z)
    rows = harmonics(x / radius, y / radius, z / radius) + index_rows
    for at, row in enumerate(rows):
        turned[at : at + 1, :] = row
    center = 0.5 + 4.0 * lax.broadcasted_iota(jnp.int32, (24, edges), 0).astype(F32) / (BASIS - 1)
    offset = (radius - center) / 0.4
    basis = jnp.exp(-(offset * offset))
    live = lax.broadcasted_iota(jnp.int32, (24, edges), 0) < BASIS
    basis_out[...] = jnp.where(live, basis, 0.0)
    return turned[...].T


def prepare_kernel(
    vectors,
    source,
    target,
    probe_vectors,
    probe_atoms,
    grid,
    probe_index,
    first,
    second,
    pfirst,
    psecond,
    columns_out,
    basis_out,
    pre_out,
    hidden3_out,
    hidden_rows_out,
    second3_out,
    pcolumns_out,
    pbasis_out,
    ppre_out,
    phidden3_out,
    phidden_rows_out,
    psecond3_out,
    picked_out,
    turned,
    pturned,
):
    turned[...] = jnp.zeros_like(turned)
    pturned[...] = jnp.zeros_like(pturned)
    row = source[...]
    slot = jnp.where(row > ATOMS, row - 1, jnp.where(row == ATOMS, 512, row))
    columns_out[...] = geometry(
        vectors[...], [slot.astype(F32), target[...].astype(F32)], EDGES, turned, basis_out
    )
    prow = probe_atoms[...]
    pslot = jnp.where(prow > ATOMS, prow - 1, jnp.where(prow == ATOMS, 512, prow))
    pcolumns_out[...] = geometry(
        probe_vectors[...], [pslot.astype(F32)], PEDGES, pturned, pbasis_out
    )

    for basis, layer, pre, hidden3, hidden_rows in (
        (basis_out, first, pre_out, hidden3_out, hidden_rows_out),
        (pbasis_out, pfirst, ppre_out, phidden3_out, phidden_rows_out),
    ):
        before = dot_tn(layer[...], basis[0:BASIS, :], HIGHEST)
        pre[...] = before.T
        hidden = before * sigmoid(before)
        upper, lower = split(hidden)
        hidden_rows[0:HIDDEN, :] = upper
        hidden_rows[HIDDEN : 2 * HIDDEN, :] = lower
        upper, lower = split(hidden.T)
        hidden3[:, 0:HIDDEN] = upper
        hidden3[:, HIDDEN : 2 * HIDDEN] = upper
        hidden3[:, 2 * HIDDEN : 3 * HIDDEN] = lower
    for degree in range(5):
        for path in range(2):
            upper, lower = split(second[:, cols(path * 5 + degree)])
            at = cols(2 * degree + path)
            second3_out[0:HIDDEN, at] = upper
            second3_out[HIDDEN : 2 * HIDDEN, at] = lower
            second3_out[2 * HIDDEN : 3 * HIDDEN, at] = upper
    upper, lower = split(psecond[...])
    psecond3_out[0:HIDDEN, :] = upper
    psecond3_out[HIDDEN : 2 * HIDDEN, :] = lower
    psecond3_out[2 * HIDDEN : 3 * HIDDEN, :] = upper

    place = probe_index[...]
    grid_row = lax.broadcasted_iota(jnp.int32, (grid.shape[0], PROBES), 0)
    hit = (place // C == grid_row).astype(F32)
    lines = dot_tn(grid[...], hit, HIGHEST)
    lane = lax.broadcasted_iota(jnp.int32, (C, PROBES), 0)
    values = jnp.sum(jnp.where(place % C == lane, lines, 0.0), axis=0, keepdims=True)
    picked_out[...] = jnp.broadcast_to(values, (C, PROBES)).T


def fill_ghosts(rows, base, low, high, left, right):
    pieces = (
        left[16:32],
        low[16:32],
        right[16:32],
        left[0:16],
        right[0:16],
        left[32:48],
        high[16:32],
        right[32:48],
    )
    for at, piece in enumerate(pieces):
        rows[base + 16 * at : base + 16 * at + 16, :] = piece


def comp_rows(component, count=1):
    return slice(component * ATOMS, (component + count) * ATOMS)


def wide_chunks():
    return [(at, min(at + 2, COMP)) for at in range(0, COMP, 2)]


def one_hot_lanes(column, width):
    lane = lax.broadcasted_iota(jnp.int32, (EB, width), 1).astype(F32)
    return (column == lane).astype(F32).astype(BF16)


def one_hot_rows(row, height):
    place = lax.broadcasted_iota(jnp.int32, (height, row.shape[1]), 0)
    return (row == place).astype(F32).astype(BF16)


def fold_source(row):
    return jnp.where(row > ATOMS, row - 1, jnp.where(row == ATOMS, 512, row))


def layer_kernel(
    own,
    low,
    high,
    left,
    right,
    columns,
    target,
    hidden3,
    second3,
    mixing,
    chosen,
    updated,
    gathered,
    mixed,
    table,
    low_out,
    middle_out,
    high_out,
    messages,
    lower_rows,
):
    table[0:ATOMS, :] = own[...]
    fill_ghosts(table, ATOMS, low, high, left, right)

    def block(step, carry):
        rows = pl.ds(pl.multiple_of(step * EB, EB), EB)
        column = columns[rows, :]
        pick = one_hot_lanes(column[:, 25:26], 2 * ATOMS)
        hidden = hidden3[rows, :]
        scalar = dot(pick, table[:, cols(0)])
        for degree in range(5):
            weight = dot(hidden, second3[:, 2 * degree * C : 2 * (degree + 1) * C])
            straight = weight[:, 0:C]
            cross = weight[:, C:] * scalar
            for first, last in chunks(degree):
                sender = dot(pick, table[:, first * C : last * C])
                for component in range(first, last):
                    value = sender[:, cols(component - first)]
                    message = straight * value + cross * column[:, component : component + 1]
                    messages[rows, cols(component)] = message.astype(BF16)
        return carry

    lax.fori_loop(0, EDGES // EB, block, 0)
    put = one_hot_rows(target[...], ATOMS)
    for first, last in wide_chunks():
        here = dot(put, messages[:, first * C : last * C]) * 0.125
        for component in range(first, last):
            upper, lower = split(here[:, cols(component - first)])
            gathered[comp_rows(component), :] = upper
            lower_rows[comp_rows(component), :] = lower
    gate = None
    for degree in range(5):
        upper, lower = split(mixing[degree])
        for component in range(STARTS[degree], STARTS[degree] + DEGREES[degree]):
            rows = comp_rows(component)
            out = dot(gathered[rows, :], upper)
            out += dot(lower_rows[rows, :], upper) + dot(gathered[rows, :], lower)
            mixed[rows, :] = out
            if component == 0:
                gate = sigmoid(out)
            new = own[:, cols(component)].astype(F32) + out * gate
            updated[:, cols(component)] = new.astype(BF16)
    send_packets(chosen[...], updated, low_out, middle_out, high_out)


def sum_table_grads(put, messages, own_grad, low, middle, high, add):
    for first, last in wide_chunks():
        wide = slice(first * C, last * C)
        total = dot(put, messages[:, wide])
        for component in range(first, last):
            here = total[0:ATOMS, cols(component - first)]
            if add is not None:
                here = here + add[comp_rows(component), :]
            own_grad[comp_rows(component), :] = here
        ghosts = total[ATOMS:, :].astype(BF16)
        low[:, wide] = ghosts[0:48]
        middle[:, wide] = ghosts[48:80]
        high[:, wide] = ghosts[80:128]


def probe_kernel(
    own,
    low,
    high,
    left,
    right,
    columns,
    atoms,
    hidden3,
    second3,
    first_readout,
    second_readout,
    picked,
    grad_own,
    low_out,
    middle_out,
    high_out,
    weight_grad,
    readout_grads,
    table,
    partial,
    contribution,
    messages,
):
    table[0:ATOMS, :] = own[...]
    fill_ghosts(table, ATOMS, low, high, left, right)

    def forward(step, carry):
        rows = pl.ds(pl.multiple_of(step * EB, EB), EB)
        column = columns[rows, :]
        pick = one_hot_lanes(column[:, 25:26], 2 * ATOMS)
        hidden = hidden3[rows, :]
        total = jnp.zeros((EB, C), F32)
        for degree in range(5):
            weight = dot(hidden, second3[:, cols(degree)])
            here = jnp.zeros((EB, C), F32)
            for first, last in chunks(degree):
                sender = dot(pick, table[:, first * C : last * C])
                for component in range(first, last):
                    value = sender[:, cols(component - first)]
                    here = here + value * column[:, component : component + 1]
            partial[rows, cols(degree)] = here
            total = total + weight * here
        contribution[rows, :] = total
        return carry

    lax.fori_loop(0, PEDGES // EB, forward, 0)

    edge = lax.broadcasted_iota(jnp.int32, (PROBES, PEDGES), 1)
    probe = lax.broadcasted_iota(jnp.int32, (PROBES, PEDGES), 0)
    pool = (edge // 4 == probe).astype(F32)
    summed = dot_exact(pool, contribution[...])
    before = dot_exact(summed, first_readout[...])
    gate = sigmoid(before)
    hidden = before * gate
    vector = second_readout[...]
    density = jnp.sum(hidden * vector, axis=1, keepdims=True)
    misfit = density - picked[...]
    loss = jnp.sum(misfit[:, 0:1] * misfit[:, 0:1], axis=0, keepdims=True) / (2.0 * PROBES)
    slope = misfit / PROBES
    d_before = slope * vector * gate * (1.0 + before * (1.0 - gate))
    readout_grads[0:C, :] = dot_tn(summed, d_before, HIGHEST)
    readout_grads[C : C + 8, :] = jnp.broadcast_to(
        jnp.sum(hidden * slope, axis=0, keepdims=True), (8, C)
    )
    readout_grads[C + 8 : C + 16, :] = jnp.broadcast_to(loss, (8, C))
    d_summed = dot_nt(d_before, first_readout[...], HIGHEST)
    contribution[...] = dot_tn(pool, d_summed, HIGHEST)

    def backward(step, carry):
        rows = pl.ds(pl.multiple_of(step * EB, EB), EB)
        column = columns[rows, :]
        hidden = hidden3[rows, :]
        slope_here = contribution[rows, :]
        for degree in range(5):
            weight = dot(hidden, second3[:, cols(degree)])
            weight_grad[rows, cols(degree)] = (slope_here * partial[rows, cols(degree)]).astype(BF16)
            down = slope_here * weight
            for component in range(STARTS[degree], STARTS[degree] + DEGREES[degree]):
                value = down * column[:, component : component + 1]
                messages[rows, cols(component)] = value.astype(BF16)
        return carry

    lax.fori_loop(0, PEDGES // EB, backward, 0)
    put = one_hot_rows(fold_source(atoms[...]), 2 * ATOMS)
    sum_table_grads(put, messages, grad_own, low_out, middle_out, high_out, None)


def network_grads(weight_grad, basis, pre, hidden_rows, second3):
    both = dot(hidden_rows[...], weight_grad[...])
    second = both[0:HIDDEN, :] + both[HIDDEN:, :]
    grads = weight_grad[...]
    d_hidden = dot_nt(grads, second3[0:HIDDEN, :]) + dot_nt(grads, second3[HIDDEN : 2 * HIDDEN, :])
    before = pre[...]
    gate = sigmoid(before)
    d_before = d_hidden * gate * (1.0 + before * (1.0 - gate))
    return second, dot_exact(basis[...], d_before)


def probe_network_kernel(weight_grad, basis, pre, hidden_rows, second3, readout_grads, out):
    second, first = network_grads(weight_grad, basis, pre, hidden_rows, second3)
    for degree in range(5):
        out[degree * HIDDEN : (degree + 1) * HIDDEN, :] = second[:, cols(degree)]
    out[320:464, :] = readout_grads[...]
    out[464:512, :] = jnp.zeros((48, C), F32)
    out[464:488, 0:HIDDEN] = first


def layer_back_kernel(
    core,
    grad_own,
    low,
    high,
    left,
    right,
    table,
    gathered,
    mixed,
    columns,
    basis,
    pre,
    hidden3,
    hidden_rows,
    second3,
    mixing,
    placed,
    probe_grads,
    grad_updated,
    d_gathered,
    mine_out,
    other_out,
    returned,
    upper_rows,
    lower_rows,
    weight_grad,
    reduced,
):
    fill_ghosts(returned, 0, low, high, left, right)
    for first, last in wide_chunks():
        back = dot(placed[...], returned[:, first * C : last * C])
        for component in range(first, last):
            rows = comp_rows(component)
            whole = grad_own[rows, :] + back[:, cols(component - first)]
            grad_updated[rows, :] = whole.astype(BF16)
    gate_in = mixed[comp_rows(0), :]
    gate = sigmoid(gate_in)
    d_gate = jnp.zeros((ATOMS, C), F32)
    for component in range(COMP - 1, -1, -1):
        rows = comp_rows(component)
        d_updated = grad_updated[rows, :].astype(F32)
        if component > 0:
            d_gate = d_gate + d_updated * mixed[rows, :]
            d_mixed = d_updated * gate
        else:
            d_mixed = d_updated * gate * (1.0 + gate_in * (1.0 - gate)) + d_gate * gate * (
                1.0 - gate
            )
        upper, lower = split(d_mixed)
        upper_rows[rows, :] = upper
        lower_rows[rows, :] = lower
    for degree in range(5):
        upper, lower = split(mixing[degree])
        rows = comp_rows(STARTS[degree], DEGREES[degree])
        reduced[640 + degree * C : 640 + (degree + 1) * C, :] = dot_tn(
            gathered[rows, :], upper_rows[rows, :]
        )
        for component in range(STARTS[degree], STARTS[degree] + DEGREES[degree]):
            rows = comp_rows(component)
            out = dot_nt(upper_rows[rows, :], upper)
            out += dot_nt(lower_rows[rows, :], upper) + dot_nt(upper_rows[rows, :], lower)
            d_gathered[:, cols(component)] = (out * 0.125).astype(BF16)

    def block(step, carry):
        rows = pl.ds(pl.multiple_of(step * EB, EB), EB)
        column = columns[rows, :]
        pick = one_hot_lanes(column[:, 25:26], 2 * ATOMS)
        pick_target = one_hot_lanes(column[:, 26:27], ATOMS)
        scalar = dot(pick, table[:, cols(0)])
        for degree in range(5):
            d_straight = jnp.zeros((EB, C), F32)
            d_cross = jnp.zeros((EB, C), F32)
            for first, last in chunks(degree):
                wide = slice(first * C, last * C)
                sender = dot(pick, table[:, wide])
                d_message = dot(pick_target, d_gathered[:, wide])
                for component in range(first, last):
                    here = cols(component - first)
                    d_here = d_message[:, here]
                    d_straight = d_straight + d_here * sender[:, here]
                    d_cross = d_cross + d_here * column[:, component : component + 1]
            weight_grad[rows, cols(2 * degree)] = d_straight.astype(BF16)
            weight_grad[rows, cols(2 * degree + 1)] = (d_cross * scalar).astype(BF16)
        return carry

    lax.fori_loop(0, EDGES // EB, block, 0)
    second, first = network_grads(weight_grad, basis, pre, hidden_rows, second3)
    for degree in range(5):
        for path in range(2):
            at = (path * 5 + degree) * HIDDEN
            reduced[at : at + HIDDEN, :] = second[:, cols(2 * degree + path)]
    reduced[1280:1792, :] = probe_grads[...]
    reduced[1792:REDUCE_ROWS, :] = jnp.zeros((REDUCE_ROWS - 1792, C), F32)
    reduced[1792:1816, 0:HIDDEN] = first
    half = REDUCE_ROWS // 2
    side = core[0]
    mine_out[...] = reduced[pl.ds(pl.multiple_of(side * half, half), half), :]
    other_out[...] = reduced[pl.ds(pl.multiple_of((1 - side) * half, half), half), :]


def table_back_kernel(
    grad_updated,
    d_gathered,
    columns,
    source,
    hidden3,
    second3,
    field_grad,
    low_out,
    middle_out,
    high_out,
    messages,
):
    def block(step, carry):
        rows = pl.ds(pl.multiple_of(step * EB, EB), EB)
        column = columns[rows, :]
        pick_target = one_hot_lanes(column[:, 26:27], ATOMS)
        hidden = hidden3[rows, :]
        d_scalar = jnp.zeros((EB, C), F32)
        for degree in (4, 3, 2, 1, 0):
            weight = dot(hidden, second3[:, 2 * degree * C : 2 * (degree + 1) * C])
            straight = weight[:, 0:C]
            d_cross = jnp.zeros((EB, C), F32)
            for first, last in chunks(degree):
                d_message = dot(pick_target, d_gathered[:, first * C : last * C])
                for component in range(first, last):
                    d_here = d_message[:, cols(component - first)]
                    d_cross = d_cross + d_here * column[:, component : component + 1]
                    value = straight * d_here
                    if component == 0:
                        value = value + d_scalar + d_cross * weight[:, C:]
                    messages[rows, cols(component)] = value.astype(BF16)
            d_scalar = d_scalar + d_cross * weight[:, C:]
        return carry

    lax.fori_loop(0, EDGES // EB, block, 0)
    put = one_hot_rows(fold_source(source[...]), 2 * ATOMS)
    sum_table_grads(put, messages, field_grad, low_out, middle_out, high_out, grad_updated)


def finish_kernel(field_grad, low, high, left, right, placed, out, returned):
    fill_ghosts(returned, 0, low, high, left, right)
    for first, last in wide_chunks():
        back = dot(placed[...], returned[:, first * C : last * C])
        for component in range(first, last):
            out[component] = field_grad[comp_rows(component), :] + back[:, cols(component - first)]


def unpack_kernel(
    core, mine, other, loss, first, second, mixing, pfirst, psecond, readout, vector, sums
):
    half = REDUCE_ROWS // 2
    side = core[0]
    sums[pl.ds(pl.multiple_of(side * half, half), half), :] = mine[...]
    sums[pl.ds(pl.multiple_of((1 - side) * half, half), half), :] = other[...]
    for block in range(10):
        second[:, cols(block)] = sums[block * HIDDEN : (block + 1) * HIDDEN, :]
    for degree in range(5):
        mixing[degree] = sums[640 + degree * C : 640 + (degree + 1) * C, :]
        psecond[:, cols(degree)] = sums[1280 + degree * HIDDEN : 1280 + (degree + 1) * HIDDEN, :]
    readout[...] = sums[1600:1728, :]
    vector[...] = sums[1728:1729, :]
    loss[...] = sums[1736:1737, :]
    pfirst[...] = sums[1744 : 1744 + BASIS, 0:HIDDEN]
    first[...] = sums[1792 : 1792 + BASIS, 0:HIDDEN]


def call(kernel, outs, scratch, flops, *operands):
    shapes = [jax.ShapeDtypeStruct(shape, dtype) for shape, dtype in outs]
    moved = sum(x.size * x.dtype.itemsize for x in list(operands) + shapes)
    whole = pl.BlockSpec(memory_space=pltpu.VMEM)
    scalar = pl.BlockSpec(memory_space=pltpu.SMEM)
    return pl.pallas_call(
        kernel,
        out_shape=shapes,
        in_specs=[scalar if x.shape == (1,) else whole for x in operands],
        out_specs=[whole] * len(shapes),
        scratch_shapes=[pltpu.VMEM(shape, dtype) for shape, dtype in scratch],
        compiler_params=pltpu.CompilerParams(vmem_limit_bytes=50 * 1024 * 1024),
        cost_estimate=pl.CostEstimate(flops=flops, bytes_accessed=moved, transcendentals=0),
    )(*operands)


PACKETS = [((48, WIDE), BF16), ((32, WIDE), BF16), ((48, WIDE), BF16)]


def ring(axis):
    count = lax.axis_size(axis)
    up = [(i, (i + 1) % count) for i in range(count)]
    down = [(b, a) for a, b in up]
    return up, down


def exchange(low_packet, middle_packet, high_packet):
    up, down = ring("bx")
    low = lax.ppermute(high_packet, "bx", up)
    high = lax.ppermute(low_packet, "bx", down)
    up, down = ring("by")
    left = lax.ppermute(
        jnp.concatenate([middle_packet[16:32], low[32:48], high[32:48]]), "by", up
    )
    right = lax.ppermute(jnp.concatenate([middle_packet[0:16], low[0:16], high[0:16]]), "by", down)
    return low, high, left, right


def reduce_halves(mine, other):
    n_x, n_y = lax.axis_size("bx"), lax.axis_size("by")
    count = n_x * n_y // 2
    axes = ("bx", "by")
    swap = [(i, i ^ 1) for i in range(n_y)]
    groups = [[2 * i + core for i in range(count)] for core in range(2)]
    pair = (mine + lax.ppermute(other, "by", swap)).reshape(count, -1, C)

    def finish():
        pieces = lax.all_to_all(pair, axes, 0, 0, axis_index_groups=groups, tiled=True)
        share = jnp.sum(pieces, axis=0)
        spread = jnp.broadcast_to(share[None], pair.shape)
        whole = lax.all_to_all(spread, axes, 0, 0, axis_index_groups=groups, tiled=True)
        whole = whole.reshape(mine.shape)
        return whole, lax.ppermute(whole, "by", swap)

    return pair, finish


def on_device(
    features,
    send_index,
    atom_vectors,
    atom_source,
    atom_target,
    probe_vectors,
    probe_atoms,
    density_grid,
    probe_index,
    radial_first,
    radial_second,
    mixing,
    probe_first,
    probe_second,
    readout_first,
    readout_second,
):
    field = features[0, 0].transpose(1, 0, 2)
    source = atom_source.reshape(1, EDGES)
    target = atom_target.reshape(1, EDGES)
    atoms = probe_atoms.reshape(1, PEDGES)
    core = (lax.axis_index("by") % 2).reshape(1)

    own, low, middle, high, chosen, placed = call(
        pack_kernel,
        [((ATOMS, WIDE), BF16)] + PACKETS + [((C, ATOMS), BF16), ((ATOMS, C), BF16)],
        [((C, C), F32)],
        2 * C * C * WIDE,
        field,
        send_index[0, 0],
    )
    received = exchange(low, middle, high)
    (
        columns,
        basis,
        pre,
        hidden3,
        hidden_rows,
        second3,
        pcolumns,
        pbasis,
        ppre,
        phidden3,
        phidden_rows,
        psecond3,
        picked,
    ) = call(
        prepare_kernel,
        [
            ((EDGES, C), F32),
            ((24, EDGES), F32),
            ((EDGES, HIDDEN), F32),
            ((EDGES, 3 * HIDDEN), BF16),
            ((2 * HIDDEN, EDGES), BF16),
            ((3 * HIDDEN, 10 * C), BF16),
            ((PEDGES, C), F32),
            ((24, PEDGES), F32),
            ((PEDGES, HIDDEN), F32),
            ((PEDGES, 3 * HIDDEN), BF16),
            ((2 * HIDDEN, PEDGES), BF16),
            ((3 * HIDDEN, 5 * C), BF16),
            ((PROBES, C), F32),
        ],
        [((C, EDGES), F32), ((C, PEDGES), F32)],
        10**9,
        atom_vectors[0, 0],
        source,
        target,
        probe_vectors[0, 0],
        atoms,
        density_grid.reshape(-1, C),
        probe_index.reshape(1, PROBES),
        radial_first,
        radial_second,
        probe_first,
        probe_second,
    )
    updated, gathered, mixed, table, low, middle, high = call(
        layer_kernel,
        [
            ((ATOMS, WIDE), BF16),
            ((COMP * ATOMS, C), BF16),
            ((COMP * ATOMS, C), F32),
            ((2 * ATOMS, WIDE), BF16),
        ]
        + PACKETS,
        [((EDGES, WIDE), BF16), ((COMP * ATOMS, C), BF16)],
        4 * 10**9,
        own,
        *received,
        columns,
        target,
        hidden3,
        second3,
        mixing,
        chosen,
    )
    received = exchange(low, middle, high)
    grad_own, low, middle, high, weight_grad, readout_grads = call(
        probe_kernel,
        [((COMP * ATOMS, C), F32)]
        + PACKETS
        + [
            ((PEDGES, 5 * C), BF16),
            ((C + 16, C), F32),
        ],
        [
            ((2 * ATOMS, WIDE), BF16),
            ((PEDGES, 5 * C), F32),
            ((PEDGES, C), F32),
            ((PEDGES, WIDE), BF16),
        ],
        4 * 10**9,
        updated,
        *received,
        pcolumns,
        atoms,
        phidden3,
        psecond3,
        readout_first,
        readout_second.reshape(1, C),
        picked,
    )
    received = exchange(low, middle, high)
    (probe_grads,) = call(
        probe_network_kernel,
        [((512, C), F32)],
        [],
        10**9,
        weight_grad,
        pbasis,
        ppre,
        phidden_rows,
        psecond3,
        readout_grads,
    )
    grad_updated, d_gathered, mine, other = call(
        layer_back_kernel,
        [
            ((COMP * ATOMS, C), BF16),
            ((ATOMS, WIDE), BF16),
            ((REDUCE_ROWS // 2, C), F32),
            ((REDUCE_ROWS // 2, C), F32),
        ],
        [
            ((C, WIDE), BF16),
            ((COMP * ATOMS, C), BF16),
            ((COMP * ATOMS, C), BF16),
            ((EDGES, 10 * C), BF16),
            ((REDUCE_ROWS, C), F32),
        ],
        6 * 10**9,
        core,
        grad_own,
        *received,
        table,
        gathered,
        mixed,
        columns,
        basis,
        pre,
        hidden3,
        hidden_rows,
        second3,
        mixing,
        placed,
        probe_grads,
    )
    pair, finish_sums = reduce_halves(mine, other)
    _, grad_updated, d_gathered = lax.optimization_barrier((pair, grad_updated, d_gathered))
    field_grad, low, middle, high = call(
        table_back_kernel,
        [((COMP * ATOMS, C), F32)] + PACKETS,
        [((EDGES, WIDE), BF16)],
        4 * 10**9,
        grad_updated,
        d_gathered,
        columns,
        source,
        hidden3,
        second3,
    )
    received = exchange(low, middle, high)
    mine, other = finish_sums()
    (feature_grad,) = call(
        finish_kernel,
        [((COMP, ATOMS, C), F32)],
        [((C, WIDE), BF16)],
        2 * C * C * WIDE,
        field_grad,
        *received,
        placed,
    )
    loss, first, second, mixing_grad, pfirst, psecond, readout, vector = call(
        unpack_kernel,
        [
            ((1, C), F32),
            ((BASIS, HIDDEN), F32),
            ((HIDDEN, 10 * C), F32),
            ((5, C, C), F32),
            ((BASIS, HIDDEN), F32),
            ((HIDDEN, 5 * C), F32),
            ((C, C), F32),
            ((1, C), F32),
        ],
        [((REDUCE_ROWS, C), F32)],
        10**6,
        core,
        mine,
        other,
    )
    return (
        loss[0, 0],
        feature_grad.transpose(1, 0, 2)[None, None],
        first,
        second,
        mixing_grad,
        pfirst,
        psecond,
        readout,
        vector[0],
    )


def solution(mesh):
    brick = [P("bx", "by", *([None] * (rank - 2))) for rank in (5, 5, 4, 3, 3, 4, 3, 3, 3)]
    in_specs = tuple(brick) + (P(),) * 7
    out_specs = (P(), P("bx", "by", None, None, None)) + (P(),) * 7
    return jax.shard_map(
        on_device, mesh=mesh, in_specs=in_specs, out_specs=out_specs, check_vma=False
    )
```

```python
import functools

import jax
import jax.numpy as jnp
import numpy as np
from jax import lax
from jax.experimental import pallas as pl
from jax.experimental.pallas import tpu as pltpu
from jax.sharding import PartitionSpec as P

C = 128
COMP = 25
BASIS = 20
HIDDEN = 64
ATOMS = 128
EDGES = 1024
PEDGES = 512
PROBES = 128
WIDE = COMP * C
EB = 256
DEGREES = (1, 3, 5, 7, 9)
STARTS = (0, 1, 4, 9, 16)
HIGHEST = lax.Precision.HIGHEST
F32 = jnp.float32
BF16 = jnp.bfloat16
REDUCE_ROWS = 2048


def dot(a, b):
    return jnp.dot(a, b, preferred_element_type=F32)


def dot_exact(a, b):
    return jnp.dot(a, b, preferred_element_type=F32, precision=HIGHEST)


def dot_nt(a, b, precision=None):
    return lax.dot_general(
        a, b, (((1,), (1,)), ((), ())), preferred_element_type=F32, precision=precision
    )


def dot_tn(a, b, precision=None):
    return lax.dot_general(
        a, b, (((0,), (0,)), ((), ())), preferred_element_type=F32, precision=precision
    )


def split(a):
    high = a.astype(BF16)
    return high, (a - high.astype(F32)).astype(BF16)


def sigmoid(a):
    return 1.0 / (1.0 + jnp.exp(-a))


def cols(component):
    return slice(component * C, (component + 1) * C)


def chunks(degree):
    first = STARTS[degree]
    last = first + DEGREES[degree]
    return [(at, min(at + 2, last)) for at in range(first, last, 2)]


def harmonics(x, y, z):
    z_square = z * z
    return [
        jnp.ones_like(x),
        1.7320508 * y,
        1.7320508 * z,
        1.7320508 * x,
        3.8729833 * x * y,
        3.8729833 * y * z,
        1.118034 * (3.0 * z_square - 1.0),
        3.8729833 * x * z,
        1.9364917 * (x * x - y * y),
        2.0916501 * y * (3.0 * x * x - y * y),
        10.246951 * x * y * z,
        1.6201852 * y * (5.0 * z_square - 1.0),
        1.3228757 * z * (5.0 * z_square - 3.0),
        1.6201852 * x * (5.0 * z_square - 1.0),
        5.1234754 * z * (x * x - y * y),
        2.0916501 * x * (x * x - 3.0 * y * y),
        8.8741197 * x * y * (x * x - y * y),
        6.2749502 * y * z * (3.0 * x * x - y * y),
        3.354102 * x * y * (7.0 * z_square - 1.0),
        2.3717082 * y * z * (7.0 * z_square - 3.0),
        0.375 * (35.0 * z_square * z_square - 30.0 * z_square + 3.0),
        2.3717082 * x * z * (7.0 * z_square - 3.0),
        1.677051 * (x * x - y * y) * (7.0 * z_square - 1.0),
        6.2749502 * x * z * (x * x - 3.0 * y * y),
        2.2185299 * (x * x * x * x - 6.0 * x * x * y * y + y * y * y * y),
    ]


def pack_kernel(features, send_index, own, low, middle, high, chosen_out, placed_out, lists):
    lists[...] = jnp.zeros_like(lists)
    for at in range(8):
        i, j = divmod(at if at < 4 else at + 1, 3)
        lists[at : at + 1, 0:16] = send_index[i, j : j + 1, :].astype(F32)
    turned = lists[...].T
    lane = lax.broadcasted_iota(jnp.int32, (16, C), 1).astype(F32)
    hits = [(turned[0:16, at : at + 1] == lane).astype(F32) for at in range(8)]
    chosen = jnp.concatenate(hits, axis=0)
    chosen_out[...] = chosen.astype(BF16)
    placed_out[...] = chosen.T.astype(BF16)
    for component in range(COMP):
        own[:, cols(component)] = features[component]
    send_packets(chosen_out[...], own, low, middle, high)


def send_packets(chosen, rows, low, middle, high):
    for first in range(0, COMP, 2):
        wide = slice(first * C, min(first + 2, COMP) * C)
        packet = dot(chosen, rows[:, wide]).astype(BF16)
        low[:, wide] = packet[0:48]
        middle[:, wide] = packet[48:80]
        high[:, wide] = packet[80:128]


def geometry(vectors, index_rows, edges, turned, basis_out):
    x, y, z = vectors[0:1], vectors[1:2], vectors[2:3]
    radius = jnp.sqrt(x * x + y * y + z * z)
    rows = harmonics(x / radius, y / radius, z / radius) + index_rows
    for at, row in enumerate(rows):
        turned[at : at + 1, :] = row
    center = 0.5 + 4.0 * lax.broadcasted_iota(jnp.int32, (24, edges), 0).astype(F32) / (BASIS - 1)
    offset = (radius - center) / 0.4
    basis = jnp.exp(-(offset * offset))
    live = lax.broadcasted_iota(jnp.int32, (24, edges), 0) < BASIS
    basis_out[...] = jnp.where(live, basis, 0.0)
    return turned[...].T


def prepare_kernel(
    vectors,
    source,
    target,
    probe_vectors,
    probe_atoms,
    grid,
    probe_index,
    first,
    second,
    pfirst,
    psecond,
    columns_out,
    basis_out,
    pre_out,
    hidden3_out,
    hidden_rows_out,
    second3_out,
    pcolumns_out,
    pbasis_out,
    ppre_out,
    phidden3_out,
    phidden_rows_out,
    psecond3_out,
    picked_out,
    turned,
    pturned,
):
    turned[...] = jnp.zeros_like(turned)
    pturned[...] = jnp.zeros_like(pturned)
    row = source[...]
    slot = jnp.where(row > ATOMS, row - 1, jnp.where(row == ATOMS, 512, row))
    columns_out[...] = geometry(
        vectors[...], [slot.astype(F32), target[...].astype(F32)], EDGES, turned, basis_out
    )
    prow = probe_atoms[...]
    pslot = jnp.where(prow > ATOMS, prow - 1, jnp.where(prow == ATOMS, 512, prow))
    pcolumns_out[...] = geometry(
        probe_vectors[...], [pslot.astype(F32)], PEDGES, pturned, pbasis_out
    )

    for basis, layer, pre, hidden3, hidden_rows in (
        (basis_out, first, pre_out, hidden3_out, hidden_rows_out),
        (pbasis_out, pfirst, ppre_out, phidden3_out, phidden_rows_out),
    ):
        before = dot_tn(layer[...], basis[0:BASIS, :], HIGHEST)
        pre[...] = before.T
        hidden = before * sigmoid(before)
        upper, lower = split(hidden)
        hidden_rows[0:HIDDEN, :] = upper
        hidden_rows[HIDDEN : 2 * HIDDEN, :] = lower
        upper, lower = split(hidden.T)
        hidden3[:, 0:HIDDEN] = upper
        hidden3[:, HIDDEN : 2 * HIDDEN] = upper
        hidden3[:, 2 * HIDDEN : 3 * HIDDEN] = lower
    for degree in range(5):
        for path in range(2):
            upper, lower = split(second[:, cols(path * 5 + degree)])
            at = cols(2 * degree + path)
            second3_out[0:HIDDEN, at] = upper
            second3_out[HIDDEN : 2 * HIDDEN, at] = lower
            second3_out[2 * HIDDEN : 3 * HIDDEN, at] = upper
    upper, lower = split(psecond[...])
    psecond3_out[0:HIDDEN, :] = upper
    psecond3_out[HIDDEN : 2 * HIDDEN, :] = lower
    psecond3_out[2 * HIDDEN : 3 * HIDDEN, :] = upper

    place = probe_index[...]
    grid_row = lax.broadcasted_iota(jnp.int32, (grid.shape[0], PROBES), 0)
    hit = (place // C == grid_row).astype(F32)
    lines = dot_tn(grid[...], hit, HIGHEST)
    lane = lax.broadcasted_iota(jnp.int32, (C, PROBES), 0)
    values = jnp.sum(jnp.where(place % C == lane, lines, 0.0), axis=0, keepdims=True)
    picked_out[...] = jnp.broadcast_to(values, (C, PROBES)).T


def fill_ghosts(rows, base, low, high, left, right):
    pieces = (
        left[16:32],
        low[16:32],
        right[16:32],
        left[0:16],
        right[0:16],
        left[32:48],
        high[16:32],
        right[32:48],
    )
    for at, piece in enumerate(pieces):
        rows[base + 16 * at : base + 16 * at + 16, :] = piece


def comp_rows(component, count=1):
    return slice(component * ATOMS, (component + count) * ATOMS)


def wide_chunks():
    return [(at, min(at + 2, COMP)) for at in range(0, COMP, 2)]


def one_hot_lanes(column, width):
    lane = lax.broadcasted_iota(jnp.int32, (EB, width), 1).astype(F32)
    return (column == lane).astype(F32).astype(BF16)


def one_hot_rows(row, height):
    place = lax.broadcasted_iota(jnp.int32, (height, row.shape[1]), 0)
    return (row == place).astype(F32).astype(BF16)


def fold_source(row):
    return jnp.where(row > ATOMS, row - 1, jnp.where(row == ATOMS, 512, row))


def layer_kernel(
    own,
    low,
    high,
    left,
    right,
    columns,
    target,
    hidden3,
    second3,
    mixing,
    chosen,
    updated,
    gathered,
    mixed,
    table,
    low_out,
    middle_out,
    high_out,
    messages,
    lower_rows,
):
    table[0:ATOMS, :] = own[...]
    fill_ghosts(table, ATOMS, low, high, left, right)

    def block(step, carry):
        rows = pl.ds(pl.multiple_of(step * EB, EB), EB)
        column = columns[rows, :]
        pick = one_hot_lanes(column[:, 25:26], 2 * ATOMS)
        hidden = hidden3[rows, :]
        scalar = dot(pick, table[:, cols(0)])
        for degree in range(5):
            weight = dot(hidden, second3[:, 2 * degree * C : 2 * (degree + 1) * C])
            straight = weight[:, 0:C]
            cross = weight[:, C:] * scalar
            for first, last in chunks(degree):
                sender = dot(pick, table[:, first * C : last * C])
                for component in range(first, last):
                    value = sender[:, cols(component - first)]
                    message = straight * value + cross * column[:, component : component + 1]
                    messages[rows, cols(component)] = message.astype(BF16)
        return carry

    lax.fori_loop(0, EDGES // EB, block, 0)
    put = one_hot_rows(target[...], ATOMS)
    for first, last in wide_chunks():
        here = dot(put, messages[:, first * C : last * C]) * 0.125
        for component in range(first, last):
            upper, lower = split(here[:, cols(component - first)])
            gathered[comp_rows(component), :] = upper
            lower_rows[comp_rows(component), :] = lower
    gate = None
    for degree in range(5):
        upper, lower = split(mixing[degree])
        for component in range(STARTS[degree], STARTS[degree] + DEGREES[degree]):
            rows = comp_rows(component)
            out = dot(gathered[rows, :], upper)
            out += dot(lower_rows[rows, :], upper) + dot(gathered[rows, :], lower)
            mixed[rows, :] = out
            if component == 0:
                gate = sigmoid(out)
            new = own[:, cols(component)].astype(F32) + out * gate
            updated[:, cols(component)] = new.astype(BF16)
    send_packets(chosen[...], updated, low_out, middle_out, high_out)


def sum_table_grads(put, messages, own_grad, low, middle, high, add):
    for first, last in wide_chunks():
        wide = slice(first * C, last * C)
        total = dot(put, messages[:, wide])
        for component in range(first, last):
            here = total[0:ATOMS, cols(component - first)]
            if add is not None:
                here = here + add[comp_rows(component), :]
            own_grad[comp_rows(component), :] = here
        ghosts = total[ATOMS:, :].astype(BF16)
        low[:, wide] = ghosts[0:48]
        middle[:, wide] = ghosts[48:80]
        high[:, wide] = ghosts[80:128]


def probe_kernel(
    own,
    low,
    high,
    left,
    right,
    columns,
    atoms,
    hidden3,
    second3,
    first_readout,
    second_readout,
    picked,
    grad_own,
    low_out,
    middle_out,
    high_out,
    weight_grad,
    readout_grads,
    table,
    partial,
    contribution,
    messages,
):
    table[0:ATOMS, :] = own[...]
    fill_ghosts(table, ATOMS, low, high, left, right)

    def forward(step, carry):
        rows = pl.ds(pl.multiple_of(step * EB, EB), EB)
        column = columns[rows, :]
        pick = one_hot_lanes(column[:, 25:26], 2 * ATOMS)
        hidden = hidden3[rows, :]
        total = jnp.zeros((EB, C), F32)
        for degree in range(5):
            weight = dot(hidden, second3[:, cols(degree)])
            here = jnp.zeros((EB, C), F32)
            for first, last in chunks(degree):
                sender = dot(pick, table[:, first * C : last * C])
                for component in range(first, last):
                    value = sender[:, cols(component - first)]
                    here = here + value * column[:, component : component + 1]
            partial[rows, cols(degree)] = here
            total = total + weight * here
        contribution[rows, :] = total
        return carry

    lax.fori_loop(0, PEDGES // EB, forward, 0)

    edge = lax.broadcasted_iota(jnp.int32, (PROBES, PEDGES), 1)
    probe = lax.broadcasted_iota(jnp.int32, (PROBES, PEDGES), 0)
    pool = (edge // 4 == probe).astype(F32)
    summed = dot_exact(pool, contribution[...])
    before = dot_exact(summed, first_readout[...])
    gate = sigmoid(before)
    hidden = before * gate
    vector = second_readout[...]
    density = jnp.sum(hidden * vector, axis=1, keepdims=True)
    misfit = density - picked[...]
    loss = jnp.sum(misfit[:, 0:1] * misfit[:, 0:1], axis=0, keepdims=True) / (2.0 * PROBES)
    slope = misfit / PROBES
    d_before = slope * vector * gate * (1.0 + before * (1.0 - gate))
    readout_grads[0:C, :] = dot_tn(summed, d_before, HIGHEST)
    readout_grads[C : C + 8, :] = jnp.broadcast_to(
        jnp.sum(hidden * slope, axis=0, keepdims=True), (8, C)
    )
    readout_grads[C + 8 : C + 16, :] = jnp.broadcast_to(loss, (8, C))
    d_summed = dot_nt(d_before, first_readout[...], HIGHEST)
    contribution[...] = dot_tn(pool, d_summed, HIGHEST)

    def backward(step, carry):
        rows = pl.ds(pl.multiple_of(step * EB, EB), EB)
        column = columns[rows, :]
        hidden = hidden3[rows, :]
        slope_here = contribution[rows, :]
        for degree in range(5):
            weight = dot(hidden, second3[:, cols(degree)])
            weight_grad[rows, cols(degree)] = (slope_here * partial[rows, cols(degree)]).astype(BF16)
            down = slope_here * weight
            for component in range(STARTS[degree], STARTS[degree] + DEGREES[degree]):
                value = down * column[:, component : component + 1]
                messages[rows, cols(component)] = value.astype(BF16)
        return carry

    lax.fori_loop(0, PEDGES // EB, backward, 0)
    put = one_hot_rows(fold_source(atoms[...]), 2 * ATOMS)
    sum_table_grads(put, messages, grad_own, low_out, middle_out, high_out, None)


def network_grads(weight_grad, basis, pre, hidden_rows, second3):
    both = dot(hidden_rows[...], weight_grad[...])
    second = both[0:HIDDEN, :] + both[HIDDEN:, :]
    grads = weight_grad[...]
    d_hidden = dot_nt(grads, second3[0:HIDDEN, :]) + dot_nt(grads, second3[HIDDEN : 2 * HIDDEN, :])
    before = pre[...]
    gate = sigmoid(before)
    d_before = d_hidden * gate * (1.0 + before * (1.0 - gate))
    return second, dot_exact(basis[...], d_before)


def probe_network_kernel(weight_grad, basis, pre, hidden_rows, second3, readout_grads, out):
    second, first = network_grads(weight_grad, basis, pre, hidden_rows, second3)
    for degree in range(5):
        out[degree * HIDDEN : (degree + 1) * HIDDEN, :] = second[:, cols(degree)]
    out[320:464, :] = readout_grads[...]
    out[464:512, :] = jnp.zeros((48, C), F32)
    out[464:488, 0:HIDDEN] = first


def table_back_kernel(
    grad_own,
    low,
    high,
    left,
    right,
    mixed,
    columns,
    source,
    hidden3,
    second3,
    mixing,
    placed,
    field_grad,
    d_gathered,
    d_mixed_out,
    low_out,
    middle_out,
    high_out,
    returned,
    grad_updated,
    lower_rows,
    messages,
):
    fill_ghosts(returned, 0, low, high, left, right)
    for first, last in wide_chunks():
        back = dot(placed[...], returned[:, first * C : last * C])
        for component in range(first, last):
            rows = comp_rows(component)
            whole = grad_own[rows, :] + back[:, cols(component - first)]
            grad_updated[rows, :] = whole.astype(BF16)
    gate_in = mixed[comp_rows(0), :]
    gate = sigmoid(gate_in)
    d_gate = jnp.zeros((ATOMS, C), F32)
    for component in range(COMP - 1, -1, -1):
        rows = comp_rows(component)
        d_updated = grad_updated[rows, :].astype(F32)
        if component > 0:
            d_gate = d_gate + d_updated * mixed[rows, :]
            d_mixed = d_updated * gate
        else:
            d_mixed = d_updated * gate * (1.0 + gate_in * (1.0 - gate)) + d_gate * gate * (
                1.0 - gate
            )
        upper, lower = split(d_mixed)
        d_mixed_out[rows, :] = upper
        lower_rows[rows, :] = lower
    for degree in range(5):
        upper, lower = split(mixing[degree])
        for component in range(STARTS[degree], STARTS[degree] + DEGREES[degree]):
            rows = comp_rows(component)
            out = dot_nt(d_mixed_out[rows, :], upper)
            out += dot_nt(lower_rows[rows, :], upper) + dot_nt(d_mixed_out[rows, :], lower)
            d_gathered[:, cols(component)] = (out * 0.125).astype(BF16)

    def block(step, carry):
        rows = pl.ds(pl.multiple_of(step * EB, EB), EB)
        column = columns[rows, :]
        pick_target = one_hot_lanes(column[:, 26:27], ATOMS)
        hidden = hidden3[rows, :]
        d_scalar = jnp.zeros((EB, C), F32)
        for degree in (4, 3, 2, 1, 0):
            weight = dot(hidden, second3[:, 2 * degree * C : 2 * (degree + 1) * C])
            straight = weight[:, 0:C]
            d_cross = jnp.zeros((EB, C), F32)
            for first, last in chunks(degree):
                d_message = dot(pick_target, d_gathered[:, first * C : last * C])
                for component in range(first, last):
                    d_here = d_message[:, cols(component - first)]
                    d_cross = d_cross + d_here * column[:, component : component + 1]
                    value = straight * d_here
                    if component == 0:
                        value = value + d_scalar + d_cross * weight[:, C:]
                    messages[rows, cols(component)] = value.astype(BF16)
            d_scalar = d_scalar + d_cross * weight[:, C:]
        return carry

    lax.fori_loop(0, EDGES // EB, block, 0)
    put = one_hot_rows(fold_source(source[...]), 2 * ATOMS)
    sum_table_grads(put, messages, field_grad, low_out, middle_out, high_out, grad_updated)


def weights_back_kernel(
    core,
    d_gathered,
    d_mixed,
    table,
    gathered,
    columns,
    basis,
    pre,
    hidden_rows,
    second3,
    probe_grads,
    mine_out,
    other_out,
    weight_grad,
    reduced,
):
    for degree in range(5):
        rows = comp_rows(STARTS[degree], DEGREES[degree])
        reduced[640 + degree * C : 640 + (degree + 1) * C, :] = dot_tn(
            gathered[rows, :], d_mixed[rows, :]
        )

    def block(step, carry):
        rows = pl.ds(pl.multiple_of(step * EB, EB), EB)
        column = columns[rows, :]
        pick = one_hot_lanes(column[:, 25:26], 2 * ATOMS)
        pick_target = one_hot_lanes(column[:, 26:27], ATOMS)
        scalar = dot(pick, table[:, cols(0)])
        for degree in range(5):
            d_straight = jnp.zeros((EB, C), F32)
            d_cross = jnp.zeros((EB, C), F32)
            for first, last in chunks(degree):
                wide = slice(first * C, last * C)
                sender = dot(pick, table[:, wide])
                d_message = dot(pick_target, d_gathered[:, wide])
                for component in range(first, last):
                    here = cols(component - first)
                    d_here = d_message[:, here]
                    d_straight = d_straight + d_here * sender[:, here]
                    d_cross = d_cross + d_here * column[:, component : component + 1]
            weight_grad[rows, cols(2 * degree)] = d_straight.astype(BF16)
            weight_grad[rows, cols(2 * degree + 1)] = (d_cross * scalar).astype(BF16)
        return carry

    lax.fori_loop(0, EDGES // EB, block, 0)
    second, first = network_grads(weight_grad, basis, pre, hidden_rows, second3)
    for degree in range(5):
        for path in range(2):
            at = (path * 5 + degree) * HIDDEN
            reduced[at : at + HIDDEN, :] = second[:, cols(2 * degree + path)]
    reduced[1280:1792, :] = probe_grads[...]
    reduced[1792:REDUCE_ROWS, :] = jnp.zeros((REDUCE_ROWS - 1792, C), F32)
    reduced[1792:1816, 0:HIDDEN] = first
    half = REDUCE_ROWS // 2
    side = core[0]
    mine_out[...] = reduced[pl.ds(pl.multiple_of(side * half, half), half), :]
    other_out[...] = reduced[pl.ds(pl.multiple_of((1 - side) * half, half), half), :]


def share_kernel(pieces, out):
    count = pieces.shape[0]
    total = pieces[0]
    for at in range(1, count):
        total = total + pieces[at]
    for at in range(count):
        out[at] = total


def finish_kernel(field_grad, low, high, left, right, placed, out, returned):
    fill_ghosts(returned, 0, low, high, left, right)
    for first, last in wide_chunks():
        back = dot(placed[...], returned[:, first * C : last * C])
        for component in range(first, last):
            out[component] = field_grad[comp_rows(component), :] + back[:, cols(component - first)]


def unpack_kernel(
    core, mine, other, loss, first, second, mixing, pfirst, psecond, readout, vector, sums
):
    half = REDUCE_ROWS // 2
    side = core[0]
    sums[pl.ds(pl.multiple_of(side * half, half), half), :] = mine[...]
    sums[pl.ds(pl.multiple_of((1 - side) * half, half), half), :] = other[...]
    for block in range(10):
        second[:, cols(block)] = sums[block * HIDDEN : (block + 1) * HIDDEN, :]
    for degree in range(5):
        mixing[degree] = sums[640 + degree * C : 640 + (degree + 1) * C, :]
        psecond[:, cols(degree)] = sums[1280 + degree * HIDDEN : 1280 + (degree + 1) * HIDDEN, :]
    readout[...] = sums[1600:1728, :]
    vector[...] = sums[1728:1729, :]
    loss[...] = sums[1736:1737, :]
    pfirst[...] = sums[1744 : 1744 + BASIS, 0:HIDDEN]
    first[...] = sums[1792 : 1792 + BASIS, 0:HIDDEN]


def call(kernel, outs, scratch, flops, *operands):
    shapes = [jax.ShapeDtypeStruct(shape, dtype) for shape, dtype in outs]
    moved = sum(x.size * x.dtype.itemsize for x in list(operands) + shapes)
    held = sum(np.prod(shape) * jnp.dtype(dtype).itemsize for shape, dtype in scratch)
    whole = pl.BlockSpec(memory_space=pltpu.VMEM)
    scalar = pl.BlockSpec(memory_space=pltpu.SMEM)
    return pl.pallas_call(
        kernel,
        out_shape=shapes,
        in_specs=[scalar if x.shape == (1,) else whole for x in operands],
        out_specs=[whole] * len(shapes),
        scratch_shapes=[pltpu.VMEM(shape, dtype) for shape, dtype in scratch],
        compiler_params=pltpu.CompilerParams(vmem_limit_bytes=int(held) + 12 * 1024 * 1024),
        cost_estimate=pl.CostEstimate(flops=flops, bytes_accessed=moved, transcendentals=0),
    )(*operands)


PACKETS = [((48, WIDE), BF16), ((32, WIDE), BF16), ((48, WIDE), BF16)]


def relay_kernel(middle, low, high, to_right, to_left):
    to_right[0:16, :] = middle[16:32, :]
    to_right[16:32, :] = low[32:48, :]
    to_right[32:48, :] = high[32:48, :]
    to_left[0:16, :] = middle[0:16, :]
    to_left[16:32, :] = low[0:16, :]
    to_left[32:48, :] = high[0:16, :]


def ring(axis):
    count = lax.axis_size(axis)
    up = [(i, (i + 1) % count) for i in range(count)]
    down = [(b, a) for a, b in up]
    return up, down


def exchange(low_packet, middle_packet, high_packet):
    up, down = ring("bx")
    low = lax.ppermute(high_packet, "bx", up)
    high = lax.ppermute(low_packet, "bx", down)
    up, down = ring("by")
    to_right, to_left = call(
        relay_kernel, [((48, WIDE), BF16)] * 2, [], 10**5, middle_packet, low, high
    )
    left = lax.ppermute(to_right, "by", up)
    right = lax.ppermute(to_left, "by", down)
    return (low, high, left, right), (to_right, to_left)


def reduce_halves(mine, other):
    n_x, n_y = lax.axis_size("bx"), lax.axis_size("by")
    count = n_x * n_y // 2
    axes = ("bx", "by")
    swap = [(i, i ^ 1) for i in range(n_y)]
    groups = [[2 * i + core for i in range(count)] for core in range(2)]
    pair = (mine + lax.ppermute(other, "by", swap)).reshape(count, -1, C)
    pieces = lax.all_to_all(pair, axes, 0, 0, axis_index_groups=groups, tiled=True)
    (spread,) = call(share_kernel, [(pair.shape, F32)], [], 10**6, pieces)
    whole = lax.all_to_all(spread, axes, 0, 0, axis_index_groups=groups, tiled=True)
    whole = whole.reshape(mine.shape)
    return whole, lambda after: lax.ppermute(lax.optimization_barrier((whole, after))[0], "by", swap)


def on_device(
    features,
    send_index,
    atom_vectors,
    atom_source,
    atom_target,
    probe_vectors,
    probe_atoms,
    density_grid,
    probe_index,
    radial_first,
    radial_second,
    mixing,
    probe_first,
    probe_second,
    readout_first,
    readout_second,
):
    field = features[0, 0].transpose(1, 0, 2)
    source = atom_source.reshape(1, EDGES)
    target = atom_target.reshape(1, EDGES)
    atoms = probe_atoms.reshape(1, PEDGES)
    core = (lax.axis_index("by") % 2).reshape(1)

    own, low, middle, high, chosen, placed = call(
        pack_kernel,
        [((ATOMS, WIDE), BF16)] + PACKETS + [((C, ATOMS), BF16), ((ATOMS, C), BF16)],
        [((C, C), F32)],
        2 * C * C * WIDE,
        field,
        send_index[0, 0],
    )
    received, _ = exchange(low, middle, high)
    (
        columns,
        basis,
        pre,
        hidden3,
        hidden_rows,
        second3,
        pcolumns,
        pbasis,
        ppre,
        phidden3,
        phidden_rows,
        psecond3,
        picked,
    ) = call(
        prepare_kernel,
        [
            ((EDGES, C), F32),
            ((24, EDGES), F32),
            ((EDGES, HIDDEN), F32),
            ((EDGES, 3 * HIDDEN), BF16),
            ((2 * HIDDEN, EDGES), BF16),
            ((3 * HIDDEN, 10 * C), BF16),
            ((PEDGES, C), F32),
            ((24, PEDGES), F32),
            ((PEDGES, HIDDEN), F32),
            ((PEDGES, 3 * HIDDEN), BF16),
            ((2 * HIDDEN, PEDGES), BF16),
            ((3 * HIDDEN, 5 * C), BF16),
            ((PROBES, C), F32),
        ],
        [((C, EDGES), F32), ((C, PEDGES), F32)],
        10**9,
        atom_vectors[0, 0],
        source,
        target,
        probe_vectors[0, 0],
        atoms,
        density_grid.reshape(-1, C),
        probe_index.reshape(1, PROBES),
        radial_first,
        radial_second,
        probe_first,
        probe_second,
    )
    updated, gathered, mixed, table, low, middle, high = call(
        layer_kernel,
        [
            ((ATOMS, WIDE), BF16),
            ((COMP * ATOMS, C), BF16),
            ((COMP * ATOMS, C), F32),
            ((2 * ATOMS, WIDE), BF16),
        ]
        + PACKETS,
        [((EDGES, WIDE), BF16), ((COMP * ATOMS, C), BF16)],
        4 * 10**9,
        own,
        *received,
        columns,
        target,
        hidden3,
        second3,
        mixing,
        chosen,
    )
    received, _ = exchange(low, middle, high)
    grad_own, low, middle, high, weight_grad, readout_grads = call(
        probe_kernel,
        [((COMP * ATOMS, C), F32)]
        + PACKETS
        + [
            ((PEDGES, 5 * C), BF16),
            ((C + 16, C), F32),
        ],
        [
            ((2 * ATOMS, WIDE), BF16),
            ((PEDGES, 5 * C), F32),
            ((PEDGES, C), F32),
            ((PEDGES, WIDE), BF16),
        ],
        4 * 10**9,
        updated,
        *received,
        pcolumns,
        atoms,
        phidden3,
        psecond3,
        readout_first,
        readout_second.reshape(1, C),
        picked,
    )
    received, _ = exchange(low, middle, high)
    (probe_grads,) = call(
        probe_network_kernel,
        [((512, C), F32)],
        [],
        10**9,
        weight_grad,
        pbasis,
        ppre,
        phidden_rows,
        psecond3,
        readout_grads,
    )
    field_grad, d_gathered, d_mixed, low, middle, high = call(
        table_back_kernel,
        [
            ((COMP * ATOMS, C), F32),
            ((ATOMS, WIDE), BF16),
            ((COMP * ATOMS, C), BF16),
        ]
        + PACKETS,
        [
            ((C, WIDE), BF16),
            ((COMP * ATOMS, C), BF16),
            ((COMP * ATOMS, C), BF16),
            ((EDGES, WIDE), BF16),
        ],
        6 * 10**9,
        grad_own,
        *received,
        mixed,
        columns,
        source,
        hidden3,
        second3,
        mixing,
        placed,
    )
    received, relays = exchange(low, middle, high)
    mine, other = call(
        weights_back_kernel,
        [((REDUCE_ROWS // 2, C), F32), ((REDUCE_ROWS // 2, C), F32)],
        [((EDGES, 10 * C), BF16), ((REDUCE_ROWS, C), F32)],
        6 * 10**9,
        core,
        d_gathered,
        d_mixed,
        table,
        gathered,
        columns,
        basis,
        pre,
        hidden_rows,
        second3,
        probe_grads,
    )
    (feature_grad,) = call(
        finish_kernel,
        [((COMP, ATOMS, C), F32)],
        [((C, WIDE), BF16)],
        2 * C * C * WIDE,
        field_grad,
        *received,
        placed,
    )
    mine, other, *_ = lax.optimization_barrier((mine, other, received[0], received[1]))
    mine, swapped = reduce_halves(mine, other)
    other = swapped(feature_grad)
    loss, first, second, mixing_grad, pfirst, psecond, readout, vector = call(
        unpack_kernel,
        [
            ((1, C), F32),
            ((BASIS, HIDDEN), F32),
            ((HIDDEN, 10 * C), F32),
            ((5, C, C), F32),
            ((BASIS, HIDDEN), F32),
            ((HIDDEN, 5 * C), F32),
            ((C, C), F32),
            ((1, C), F32),
        ],
        [((REDUCE_ROWS, C), F32)],
        10**6,
        core,
        mine,
        other,
    )
    return (
        loss[0, 0],
        feature_grad.transpose(1, 0, 2)[None, None],
        first,
        second,
        mixing_grad,
        pfirst,
        psecond,
        readout,
        vector[0],
    )


def solution(mesh):
    brick = [P("bx", "by", *([None] * (rank - 2))) for rank in (5, 5, 4, 3, 3, 4, 3, 3, 3)]
    in_specs = tuple(brick) + (P(),) * 7
    out_specs = (P(), P("bx", "by", None, None, None)) + (P(),) * 7
    return jax.shard_map(
        on_device, mesh=mesh, in_specs=in_specs, out_specs=out_specs, check_vma=False
    )
```

```python
import functools

import jax
import jax.numpy as jnp
import numpy as np
from jax import lax
from jax.experimental import pallas as pl
from jax.experimental.pallas import tpu as pltpu
from jax.sharding import PartitionSpec as P

C = 128
COMP = 25
BASIS = 20
HIDDEN = 64
ATOMS = 128
EDGES = 1024
PEDGES = 512
PROBES = 128
WIDE = COMP * C
EB = 512
DEGREES = (1, 3, 5, 7, 9)
STARTS = (0, 1, 4, 9, 16)
HIGHEST = lax.Precision.HIGHEST
F32 = jnp.float32
BF16 = jnp.bfloat16
REDUCE_ROWS = 2048


def dot(a, b):
    return jnp.dot(a, b, preferred_element_type=F32)


def dot_exact(a, b):
    return jnp.dot(a, b, preferred_element_type=F32, precision=HIGHEST)


def dot_nt(a, b, precision=None):
    return lax.dot_general(
        a, b, (((1,), (1,)), ((), ())), preferred_element_type=F32, precision=precision
    )


def dot_tn(a, b, precision=None):
    return lax.dot_general(
        a, b, (((0,), (0,)), ((), ())), preferred_element_type=F32, precision=precision
    )


def split(a):
    high = a.astype(BF16)
    return high, (a - high.astype(F32)).astype(BF16)


def sigmoid(a):
    return 1.0 / (1.0 + jnp.exp(-a))


def cols(component):
    return slice(component * C, (component + 1) * C)


def chunks(degree):
    first = STARTS[degree]
    last = first + DEGREES[degree]
    return [(at, min(at + 2, last)) for at in range(first, last, 2)]


def harmonics(x, y, z):
    z_square = z * z
    return [
        jnp.ones_like(x),
        1.7320508 * y,
        1.7320508 * z,
        1.7320508 * x,
        3.8729833 * x * y,
        3.8729833 * y * z,
        1.118034 * (3.0 * z_square - 1.0),
        3.8729833 * x * z,
        1.9364917 * (x * x - y * y),
        2.0916501 * y * (3.0 * x * x - y * y),
        10.246951 * x * y * z,
        1.6201852 * y * (5.0 * z_square - 1.0),
        1.3228757 * z * (5.0 * z_square - 3.0),
        1.6201852 * x * (5.0 * z_square - 1.0),
        5.1234754 * z * (x * x - y * y),
        2.0916501 * x * (x * x - 3.0 * y * y),
        8.8741197 * x * y * (x * x - y * y),
        6.2749502 * y * z * (3.0 * x * x - y * y),
        3.354102 * x * y * (7.0 * z_square - 1.0),
        2.3717082 * y * z * (7.0 * z_square - 3.0),
        0.375 * (35.0 * z_square * z_square - 30.0 * z_square + 3.0),
        2.3717082 * x * z * (7.0 * z_square - 3.0),
        1.677051 * (x * x - y * y) * (7.0 * z_square - 1.0),
        6.2749502 * x * z * (x * x - 3.0 * y * y),
        2.2185299 * (x * x * x * x - 6.0 * x * x * y * y + y * y * y * y),
    ]


def pack_kernel(core, features, send_index, own, low, middle, high, chosen_out, placed_out, lists):
    lists[...] = jnp.zeros_like(lists)
    for at in range(8):
        i, j = divmod(at if at < 4 else at + 1, 3)
        lists[at : at + 1, 0:16] = send_index[i, j : j + 1, :].astype(F32)
    turned = lists[...].T
    lane = lax.broadcasted_iota(jnp.int32, (16, C), 1).astype(F32)
    hits = [(turned[0:16, at : at + 1] == lane).astype(F32) for at in range(8)]
    chosen = jnp.concatenate(hits, axis=0)
    chosen_out[...] = chosen.astype(BF16)
    placed_out[...] = chosen.T.astype(BF16)
    for component in range(COMP):
        own[:, cols(component)] = features[component]
    send_packets(chosen_out[...], own, low, middle, high)


def send_packets(chosen, rows, low, middle, high):
    for first in range(0, COMP, 2):
        wide = slice(first * C, min(first + 2, COMP) * C)
        packet = dot(chosen, rows[:, wide]).astype(BF16)
        low[:, wide] = packet[0:48]
        middle[:, wide] = packet[48:80]
        high[:, wide] = packet[80:128]


def geometry(vectors, index_rows, edges, turned, basis_out):
    x, y, z = vectors[0:1], vectors[1:2], vectors[2:3]
    radius = jnp.sqrt(x * x + y * y + z * z)
    rows = harmonics(x / radius, y / radius, z / radius) + index_rows
    for at, row in enumerate(rows):
        turned[at : at + 1, :] = row
    center = 0.5 + 4.0 * lax.broadcasted_iota(jnp.int32, (24, edges), 0).astype(F32) / (BASIS - 1)
    offset = (radius - center) / 0.4
    basis = jnp.exp(-(offset * offset))
    live = lax.broadcasted_iota(jnp.int32, (24, edges), 0) < BASIS
    basis_out[...] = jnp.where(live, basis, 0.0)
    return turned[...].T


def prepare_kernel(
    vectors,
    source,
    target,
    probe_vectors,
    probe_atoms,
    grid,
    probe_index,
    first,
    second,
    pfirst,
    psecond,
    columns_out,
    basis_out,
    pre_out,
    hidden3_out,
    hidden_rows_out,
    second3_out,
    pcolumns_out,
    pbasis_out,
    ppre_out,
    phidden3_out,
    phidden_rows_out,
    psecond3_out,
    picked_out,
    turned,
    pturned,
):
    turned[...] = jnp.zeros_like(turned)
    pturned[...] = jnp.zeros_like(pturned)
    row = source[...]
    slot = jnp.where(row > ATOMS, row - 1, jnp.where(row == ATOMS, 512, row))
    columns_out[...] = geometry(
        vectors[...], [slot.astype(F32), target[...].astype(F32)], EDGES, turned, basis_out
    )
    prow = probe_atoms[...]
    pslot = jnp.where(prow > ATOMS, prow - 1, jnp.where(prow == ATOMS, 512, prow))
    pcolumns_out[...] = geometry(
        probe_vectors[...], [pslot.astype(F32)], PEDGES, pturned, pbasis_out
    )

    for basis, layer, pre, hidden3, hidden_rows in (
        (basis_out, first, pre_out, hidden3_out, hidden_rows_out),
        (pbasis_out, pfirst, ppre_out, phidden3_out, phidden_rows_out),
    ):
        before = dot_tn(layer[...], basis[0:BASIS, :], HIGHEST)
        pre[...] = before.T
        hidden = before * sigmoid(before)
        upper, lower = split(hidden)
        hidden_rows[0:HIDDEN, :] = upper
        hidden_rows[HIDDEN : 2 * HIDDEN, :] = lower
        upper, lower = split(hidden.T)
        hidden3[:, 0:HIDDEN] = upper
        hidden3[:, HIDDEN : 2 * HIDDEN] = upper
        hidden3[:, 2 * HIDDEN : 3 * HIDDEN] = lower
    for degree in range(5):
        for path in range(2):
            upper, lower = split(second[:, cols(path * 5 + degree)])
            at = cols(2 * degree + path)
            second3_out[0:HIDDEN, at] = upper
            second3_out[HIDDEN : 2 * HIDDEN, at] = lower
            second3_out[2 * HIDDEN : 3 * HIDDEN, at] = upper
    upper, lower = split(psecond[...])
    psecond3_out[0:HIDDEN, :] = upper
    psecond3_out[HIDDEN : 2 * HIDDEN, :] = lower
    psecond3_out[2 * HIDDEN : 3 * HIDDEN, :] = upper

    place = probe_index[...]
    grid_row = lax.broadcasted_iota(jnp.int32, (grid.shape[0], PROBES), 0)
    hit = (place // C == grid_row).astype(F32)
    lines = dot_tn(grid[...], hit, HIGHEST)
    lane = lax.broadcasted_iota(jnp.int32, (C, PROBES), 0)
    values = jnp.sum(jnp.where(place % C == lane, lines, 0.0), axis=0, keepdims=True)
    picked_out[...] = jnp.broadcast_to(values, (C, PROBES)).T


def fill_ghosts(rows, base, low, high, left, right):
    pieces = (
        left[16:32],
        low[16:32],
        right[16:32],
        left[0:16],
        right[0:16],
        left[32:48],
        high[16:32],
        right[32:48],
    )
    for at, piece in enumerate(pieces):
        rows[base + 16 * at : base + 16 * at + 16, :] = piece


def comp_rows(component, count=1):
    return slice(component * ATOMS, (component + count) * ATOMS)


def wide_chunks():
    return [(at, min(at + 2, COMP)) for at in range(0, COMP, 2)]


def one_hot_lanes(column, width):
    lane = lax.broadcasted_iota(jnp.int32, (EB, width), 1).astype(F32)
    return (column == lane).astype(F32).astype(BF16)


def one_hot_rows(row, height):
    place = lax.broadcasted_iota(jnp.int32, (height, row.shape[1]), 0)
    return (row == place).astype(F32).astype(BF16)


def fold_source(row):
    return jnp.where(row > ATOMS, row - 1, jnp.where(row == ATOMS, 512, row))


def layer_kernel(
    own,
    low,
    high,
    left,
    right,
    columns,
    target,
    hidden3,
    second3,
    mixing,
    chosen,
    updated,
    gathered,
    mixed,
    table,
    low_out,
    middle_out,
    high_out,
    messages,
    lower_rows,
):
    table[0:ATOMS, :] = own[...]
    fill_ghosts(table, ATOMS, low, high, left, right)

    def block(step, carry):
        rows = pl.ds(pl.multiple_of(step * EB, EB), EB)
        column = columns[rows, :]
        pick = one_hot_lanes(column[:, 25:26], 2 * ATOMS)
        hidden = hidden3[rows, :]
        scalar = dot(pick, table[:, cols(0)])
        for degree in range(5):
            weight = dot(hidden, second3[:, 2 * degree * C : 2 * (degree + 1) * C])
            straight = weight[:, 0:C]
            cross = weight[:, C:] * scalar
            for first, last in chunks(degree):
                sender = dot(pick, table[:, first * C : last * C])
                for component in range(first, last):
                    value = sender[:, cols(component - first)]
                    message = straight * value + cross * column[:, component : component + 1]
                    messages[rows, cols(component)] = message.astype(BF16)
        return carry

    lax.fori_loop(0, EDGES // EB, block, 0)
    put = one_hot_rows(target[...], ATOMS)
    for first, last in wide_chunks():
        here = dot(put, messages[:, first * C : last * C]) * 0.125
        for component in range(first, last):
            upper, lower = split(here[:, cols(component - first)])
            gathered[comp_rows(component), :] = upper
            lower_rows[comp_rows(component), :] = lower
    gate = None
    for degree in range(5):
        upper, lower = split(mixing[degree])
        for component in range(STARTS[degree], STARTS[degree] + DEGREES[degree]):
            rows = comp_rows(component)
            out = dot(gathered[rows, :], upper)
            out += dot(lower_rows[rows, :], upper) + dot(gathered[rows, :], lower)
            mixed[rows, :] = out
            if component == 0:
                gate = sigmoid(out)
            new = own[:, cols(component)].astype(F32) + out * gate
            updated[:, cols(component)] = new.astype(BF16)
    send_packets(chosen[...], updated, low_out, middle_out, high_out)


def sum_table_grads(put, messages, own_grad, low, middle, high, add):
    for first, last in wide_chunks():
        wide = slice(first * C, last * C)
        total = dot(put, messages[:, wide])
        for component in range(first, last):
            here = total[0:ATOMS, cols(component - first)]
            if add is not None:
                here = here + add[comp_rows(component), :]
            own_grad[comp_rows(component), :] = here
        ghosts = total[ATOMS:, :].astype(BF16)
        low[:, wide] = ghosts[0:48]
        middle[:, wide] = ghosts[48:80]
        high[:, wide] = ghosts[80:128]


def probe_kernel(
    own,
    low,
    high,
    left,
    right,
    columns,
    atoms,
    hidden3,
    second3,
    first_readout,
    second_readout,
    picked,
    grad_own,
    low_out,
    middle_out,
    high_out,
    weight_grad,
    readout_grads,
    table,
    partial,
    contribution,
    messages,
):
    table[0:ATOMS, :] = own[...]
    fill_ghosts(table, ATOMS, low, high, left, right)

    def forward(step, carry):
        rows = pl.ds(pl.multiple_of(step * EB, EB), EB)
        column = columns[rows, :]
        pick = one_hot_lanes(column[:, 25:26], 2 * ATOMS)
        hidden = hidden3[rows, :]
        total = jnp.zeros((EB, C), F32)
        for degree in range(5):
            weight = dot(hidden, second3[:, cols(degree)])
            here = jnp.zeros((EB, C), F32)
            for first, last in chunks(degree):
                sender = dot(pick, table[:, first * C : last * C])
                for component in range(first, last):
                    value = sender[:, cols(component - first)]
                    here = here + value * column[:, component : component + 1]
            partial[rows, cols(degree)] = here
            total = total + weight * here
        contribution[rows, :] = total
        return carry

    lax.fori_loop(0, PEDGES // EB, forward, 0)

    edge = lax.broadcasted_iota(jnp.int32, (PROBES, PEDGES), 1)
    probe = lax.broadcasted_iota(jnp.int32, (PROBES, PEDGES), 0)
    pool = (edge // 4 == probe).astype(F32)
    summed = dot_exact(pool, contribution[...])
    before = dot_exact(summed, first_readout[...])
    gate = sigmoid(before)
    hidden = before * gate
    vector = second_readout[...]
    density = jnp.sum(hidden * vector, axis=1, keepdims=True)
    misfit = density - picked[...]
    loss = jnp.sum(misfit[:, 0:1] * misfit[:, 0:1], axis=0, keepdims=True) / (2.0 * PROBES)
    slope = misfit / PROBES
    d_before = slope * vector * gate * (1.0 + before * (1.0 - gate))
    readout_grads[0:C, :] = dot_tn(summed, d_before, HIGHEST)
    readout_grads[C : C + 8, :] = jnp.broadcast_to(
        jnp.sum(hidden * slope, axis=0, keepdims=True), (8, C)
    )
    readout_grads[C + 8 : C + 16, :] = jnp.broadcast_to(loss, (8, C))
    d_summed = dot_nt(d_before, first_readout[...], HIGHEST)
    contribution[...] = dot_tn(pool, d_summed, HIGHEST)

    def backward(step, carry):
        rows = pl.ds(pl.multiple_of(step * EB, EB), EB)
        column = columns[rows, :]
        hidden = hidden3[rows, :]
        slope_here = contribution[rows, :]
        for degree in range(5):
            weight = dot(hidden, second3[:, cols(degree)])
            weight_grad[rows, cols(degree)] = (slope_here * partial[rows, cols(degree)]).astype(BF16)
            down = slope_here * weight
            for component in range(STARTS[degree], STARTS[degree] + DEGREES[degree]):
                value = down * column[:, component : component + 1]
                messages[rows, cols(component)] = value.astype(BF16)
        return carry

    lax.fori_loop(0, PEDGES // EB, backward, 0)
    put = one_hot_rows(fold_source(atoms[...]), 2 * ATOMS)
    sum_table_grads(put, messages, grad_own, low_out, middle_out, high_out, None)


def network_grads(weight_grad, basis, pre, hidden_rows, second3):
    both = dot(hidden_rows[...], weight_grad[...])
    second = both[0:HIDDEN, :] + both[HIDDEN:, :]
    grads = weight_grad[...]
    d_hidden = dot_nt(grads, second3[0:HIDDEN, :]) + dot_nt(grads, second3[HIDDEN : 2 * HIDDEN, :])
    before = pre[...]
    gate = sigmoid(before)
    d_before = d_hidden * gate * (1.0 + before * (1.0 - gate))
    return second, dot_exact(basis[...], d_before)


def probe_network_kernel(weight_grad, basis, pre, hidden_rows, second3, readout_grads, out):
    second, first = network_grads(weight_grad, basis, pre, hidden_rows, second3)
    for degree in range(5):
        out[degree * HIDDEN : (degree + 1) * HIDDEN, :] = second[:, cols(degree)]
    out[320:464, :] = readout_grads[...]
    out[464:512, :] = jnp.zeros((48, C), F32)
    out[464:488, 0:HIDDEN] = first


def table_back_kernel(
    grad_own,
    low,
    high,
    left,
    right,
    mixed,
    columns,
    source,
    hidden3,
    second3,
    mixing,
    placed,
    field_grad,
    d_gathered,
    d_mixed_out,
    low_out,
    middle_out,
    high_out,
    returned,
    grad_updated,
    lower_rows,
    messages,
):
    fill_ghosts(returned, 0, low, high, left, right)
    for first, last in wide_chunks():
        back = dot(placed[...], returned[:, first * C : last * C])
        for component in range(first, last):
            rows = comp_rows(component)
            whole = grad_own[rows, :] + back[:, cols(component - first)]
            grad_updated[rows, :] = whole.astype(BF16)
    gate_in = mixed[comp_rows(0), :]
    gate = sigmoid(gate_in)
    d_gate = jnp.zeros((ATOMS, C), F32)
    for component in range(COMP - 1, -1, -1):
        rows = comp_rows(component)
        d_updated = grad_updated[rows, :].astype(F32)
        if component > 0:
            d_gate = d_gate + d_updated * mixed[rows, :]
            d_mixed = d_updated * gate
        else:
            d_mixed = d_updated * gate * (1.0 + gate_in * (1.0 - gate)) + d_gate * gate * (
                1.0 - gate
            )
        upper, lower = split(d_mixed)
        d_mixed_out[rows, :] = upper
        lower_rows[rows, :] = lower
    for degree in range(5):
        upper, lower = split(mixing[degree])
        for component in range(STARTS[degree], STARTS[degree] + DEGREES[degree]):
            rows = comp_rows(component)
            out = dot_nt(d_mixed_out[rows, :], upper)
            out += dot_nt(lower_rows[rows, :], upper) + dot_nt(d_mixed_out[rows, :], lower)
            d_gathered[:, cols(component)] = (out * 0.125).astype(BF16)

    def block(step, carry):
        rows = pl.ds(pl.multiple_of(step * EB, EB), EB)
        column = columns[rows, :]
        pick_target = one_hot_lanes(column[:, 26:27], ATOMS)
        hidden = hidden3[rows, :]
        d_scalar = jnp.zeros((EB, C), F32)
        for degree in (4, 3, 2, 1, 0):
            weight = dot(hidden, second3[:, 2 * degree * C : 2 * (degree + 1) * C])
            straight = weight[:, 0:C]
            d_cross = jnp.zeros((EB, C), F32)
            for first, last in chunks(degree):
                d_message = dot(pick_target, d_gathered[:, first * C : last * C])
                for component in range(first, last):
                    d_here = d_message[:, cols(component - first)]
                    d_cross = d_cross + d_here * column[:, component : component + 1]
                    value = straight * d_here
                    if component == 0:
                        value = value + d_scalar + d_cross * weight[:, C:]
                    messages[rows, cols(component)] = value.astype(BF16)
            d_scalar = d_scalar + d_cross * weight[:, C:]
        return carry

    lax.fori_loop(0, EDGES // EB, block, 0)
    put = one_hot_rows(fold_source(source[...]), 2 * ATOMS)
    sum_table_grads(put, messages, field_grad, low_out, middle_out, high_out, grad_updated)


def weights_back_kernel(
    core,
    d_gathered,
    d_mixed,
    table,
    gathered,
    columns,
    basis,
    pre,
    hidden_rows,
    second3,
    probe_grads,
    mine_out,
    other_out,
    weight_grad,
    reduced,
):
    for degree in range(5):
        rows = comp_rows(STARTS[degree], DEGREES[degree])
        reduced[640 + degree * C : 640 + (degree + 1) * C, :] = dot_tn(
            gathered[rows, :], d_mixed[rows, :]
        )

    def block(step, carry):
        rows = pl.ds(pl.multiple_of(step * EB, EB), EB)
        column = columns[rows, :]
        pick = one_hot_lanes(column[:, 25:26], 2 * ATOMS)
        pick_target = one_hot_lanes(column[:, 26:27], ATOMS)
        scalar = dot(pick, table[:, cols(0)])
        for degree in range(5):
            d_straight = jnp.zeros((EB, C), F32)
            d_cross = jnp.zeros((EB, C), F32)
            for first, last in chunks(degree):
                wide = slice(first * C, last * C)
                sender = dot(pick, table[:, wide])
                d_message = dot(pick_target, d_gathered[:, wide])
                for component in range(first, last):
                    here = cols(component - first)
                    d_here = d_message[:, here]
                    d_straight = d_straight + d_here * sender[:, here]
                    d_cross = d_cross + d_here * column[:, component : component + 1]
            weight_grad[rows, cols(2 * degree)] = d_straight.astype(BF16)
            weight_grad[rows, cols(2 * degree + 1)] = (d_cross * scalar).astype(BF16)
        return carry

    lax.fori_loop(0, EDGES // EB, block, 0)
    second, first = network_grads(weight_grad, basis, pre, hidden_rows, second3)
    for degree in range(5):
        for path in range(2):
            at = (path * 5 + degree) * HIDDEN
            reduced[at : at + HIDDEN, :] = second[:, cols(2 * degree + path)]
    reduced[1280:1792, :] = probe_grads[...]
    reduced[1792:REDUCE_ROWS, :] = jnp.zeros((REDUCE_ROWS - 1792, C), F32)
    reduced[1792:1816, 0:HIDDEN] = first
    half = REDUCE_ROWS // 2
    side = core[0]
    mine_out[...] = reduced[pl.ds(pl.multiple_of(side * half, half), half), :]
    other_out[...] = reduced[pl.ds(pl.multiple_of((1 - side) * half, half), half), :]


def share_kernel(pieces, out):
    count = pieces.shape[0]
    total = pieces[0]
    for at in range(1, count):
        total = total + pieces[at]
    for at in range(count):
        out[at] = total


def finish_kernel(field_grad, low, high, left, right, placed, out, returned):
    fill_ghosts(returned, 0, low, high, left, right)
    for first, last in wide_chunks():
        back = dot(placed[...], returned[:, first * C : last * C])
        for component in range(first, last):
            out[component] = field_grad[comp_rows(component), :] + back[:, cols(component - first)]


def unpack_kernel(
    core, mine, other, loss, first, second, mixing, pfirst, psecond, readout, vector, sums
):
    half = REDUCE_ROWS // 2
    side = core[0]
    sums[pl.ds(pl.multiple_of(side * half, half), half), :] = mine[...]
    sums[pl.ds(pl.multiple_of((1 - side) * half, half), half), :] = other[...]
    for block in range(10):
        second[:, cols(block)] = sums[block * HIDDEN : (block + 1) * HIDDEN, :]
    for degree in range(5):
        mixing[degree] = sums[640 + degree * C : 640 + (degree + 1) * C, :]
        psecond[:, cols(degree)] = sums[1280 + degree * HIDDEN : 1280 + (degree + 1) * HIDDEN, :]
    readout[...] = sums[1600:1728, :]
    vector[...] = sums[1728:1729, :]
    loss[...] = sums[1736:1737, :]
    pfirst[...] = sums[1744 : 1744 + BASIS, 0:HIDDEN]
    first[...] = sums[1792 : 1792 + BASIS, 0:HIDDEN]


def call(kernel, outs, scratch, flops, *operands):
    shapes = [jax.ShapeDtypeStruct(shape, dtype) for shape, dtype in outs]
    moved = sum(x.size * x.dtype.itemsize for x in list(operands) + shapes)
    held = sum(np.prod(shape) * jnp.dtype(dtype).itemsize for shape, dtype in scratch)
    whole = pl.BlockSpec(memory_space=pltpu.VMEM)
    scalar = pl.BlockSpec(memory_space=pltpu.SMEM)
    return pl.pallas_call(
        kernel,
        out_shape=shapes,
        in_specs=[scalar if x.shape == (1,) else whole for x in operands],
        out_specs=[whole] * len(shapes),
        scratch_shapes=[pltpu.VMEM(shape, dtype) for shape, dtype in scratch],
        compiler_params=pltpu.CompilerParams(vmem_limit_bytes=int(held) + 12 * 1024 * 1024),
        cost_estimate=pl.CostEstimate(flops=flops, bytes_accessed=moved, transcendentals=0),
    )(*operands)


PACKETS = [((48, WIDE), BF16), ((32, WIDE), BF16), ((48, WIDE), BF16)]


def relay_kernel(middle, low, high, to_right, to_left):
    to_right[0:16, :] = middle[16:32, :]
    to_right[16:32, :] = low[32:48, :]
    to_right[32:48, :] = high[32:48, :]
    to_left[0:16, :] = middle[0:16, :]
    to_left[16:32, :] = low[0:16, :]
    to_left[32:48, :] = high[0:16, :]


def ring(axis):
    count = lax.axis_size(axis)
    up = [(i, (i + 1) % count) for i in range(count)]
    down = [(b, a) for a, b in up]
    return up, down


def exchange(low_packet, middle_packet, high_packet):
    up, down = ring("bx")
    low = lax.ppermute(high_packet, "bx", up)
    high = lax.ppermute(low_packet, "bx", down)
    up, down = ring("by")
    to_right, to_left = call(
        relay_kernel, [((48, WIDE), BF16)] * 2, [], 10**5, middle_packet, low, high
    )
    left = lax.ppermute(to_right, "by", up)
    right = lax.ppermute(to_left, "by", down)
    return (low, high, left, right), (to_right, to_left)


def reduce_halves(mine, other):
    n_x, n_y = lax.axis_size("bx"), lax.axis_size("by")
    count = n_x * n_y // 2
    axes = ("bx", "by")
    swap = [(i, i ^ 1) for i in range(n_y)]
    groups = [[2 * i + core for i in range(count)] for core in range(2)]
    pair = (mine + lax.ppermute(other, "by", swap)).reshape(count, -1, C)
    pieces = lax.all_to_all(pair, axes, 0, 0, axis_index_groups=groups, tiled=True)
    (spread,) = call(share_kernel, [(pair.shape, F32)], [], 10**6, pieces)
    whole = lax.all_to_all(spread, axes, 0, 0, axis_index_groups=groups, tiled=True)
    whole = whole.reshape(mine.shape)
    return whole, lambda after: lax.ppermute(lax.optimization_barrier((whole, after))[0], "by", swap)


def on_device(
    features,
    send_index,
    atom_vectors,
    atom_source,
    atom_target,
    probe_vectors,
    probe_atoms,
    density_grid,
    probe_index,
    radial_first,
    radial_second,
    mixing,
    probe_first,
    probe_second,
    readout_first,
    readout_second,
):
    field = features[0, 0].transpose(1, 0, 2)
    source = atom_source.reshape(1, EDGES)
    target = atom_target.reshape(1, EDGES)
    atoms = probe_atoms.reshape(1, PEDGES)
    core = (lax.axis_index("by") % 2).reshape(1)

    own, low, middle, high, chosen, placed = call(
        pack_kernel,
        [((ATOMS, WIDE), BF16)] + PACKETS + [((C, ATOMS), BF16), ((ATOMS, C), BF16)],
        [((C, C), F32)],
        2 * C * C * WIDE,
        core,
        field,
        send_index[0, 0],
    )
    received, _ = exchange(low, middle, high)
    (
        columns,
        basis,
        pre,
        hidden3,
        hidden_rows,
        second3,
        pcolumns,
        pbasis,
        ppre,
        phidden3,
        phidden_rows,
        psecond3,
        picked,
    ) = call(
        prepare_kernel,
        [
            ((EDGES, C), F32),
            ((24, EDGES), F32),
            ((EDGES, HIDDEN), F32),
            ((EDGES, 3 * HIDDEN), BF16),
            ((2 * HIDDEN, EDGES), BF16),
            ((3 * HIDDEN, 10 * C), BF16),
            ((PEDGES, C), F32),
            ((24, PEDGES), F32),
            ((PEDGES, HIDDEN), F32),
            ((PEDGES, 3 * HIDDEN), BF16),
            ((2 * HIDDEN, PEDGES), BF16),
            ((3 * HIDDEN, 5 * C), BF16),
            ((PROBES, C), F32),
        ],
        [((C, EDGES), F32), ((C, PEDGES), F32)],
        10**9,
        atom_vectors[0, 0],
        source,
        target,
        probe_vectors[0, 0],
        atoms,
        density_grid.reshape(-1, C),
        probe_index.reshape(1, PROBES),
        radial_first,
        radial_second,
        probe_first,
        probe_second,
    )
    updated, gathered, mixed, table, low, middle, high = call(
        layer_kernel,
        [
            ((ATOMS, WIDE), BF16),
            ((COMP * ATOMS, C), BF16),
            ((COMP * ATOMS, C), F32),
            ((2 * ATOMS, WIDE), BF16),
        ]
        + PACKETS,
        [((EDGES, WIDE), BF16), ((COMP * ATOMS, C), BF16)],
        4 * 10**9,
        own,
        *received,
        columns,
        target,
        hidden3,
        second3,
        mixing,
        chosen,
    )
    received, _ = exchange(low, middle, high)
    grad_own, low, middle, high, weight_grad, readout_grads = call(
        probe_kernel,
        [((COMP * ATOMS, C), F32)]
        + PACKETS
        + [
            ((PEDGES, 5 * C), BF16),
            ((C + 16, C), F32),
        ],
        [
            ((2 * ATOMS, WIDE), BF16),
            ((PEDGES, 5 * C), F32),
            ((PEDGES, C), F32),
            ((PEDGES, WIDE), BF16),
        ],
        4 * 10**9,
        updated,
        *received,
        pcolumns,
        atoms,
        phidden3,
        psecond3,
        readout_first,
        readout_second.reshape(1, C),
        picked,
    )
    received, _ = exchange(low, middle, high)
    (probe_grads,) = call(
        probe_network_kernel,
        [((512, C), F32)],
        [],
        10**9,
        weight_grad,
        pbasis,
        ppre,
        phidden_rows,
        psecond3,
        readout_grads,
    )
    field_grad, d_gathered, d_mixed, low, middle, high = call(
        table_back_kernel,
        [
            ((COMP * ATOMS, C), F32),
            ((ATOMS, WIDE), BF16),
            ((COMP * ATOMS, C), BF16),
        ]
        + PACKETS,
        [
            ((C, WIDE), BF16),
            ((COMP * ATOMS, C), BF16),
            ((COMP * ATOMS, C), BF16),
            ((EDGES, WIDE), BF16),
        ],
        6 * 10**9,
        grad_own,
        *received,
        mixed,
        columns,
        source,
        hidden3,
        second3,
        mixing,
        placed,
    )
    received, relays = exchange(low, middle, high)
    mine, other = call(
        weights_back_kernel,
        [((REDUCE_ROWS // 2, C), F32), ((REDUCE_ROWS // 2, C), F32)],
        [((EDGES, 10 * C), BF16), ((REDUCE_ROWS, C), F32)],
        6 * 10**9,
        core,
        d_gathered,
        d_mixed,
        table,
        gathered,
        columns,
        basis,
        pre,
        hidden_rows,
        second3,
        probe_grads,
    )
    (feature_grad,) = call(
        finish_kernel,
        [((COMP, ATOMS, C), F32)],
        [((C, WIDE), BF16)],
        2 * C * C * WIDE,
        field_grad,
        *received,
        placed,
    )
    mine, other, *_ = lax.optimization_barrier((mine, other, received[0], received[1]))
    mine, swapped = reduce_halves(mine, other)
    other = swapped(feature_grad)
    loss, first, second, mixing_grad, pfirst, psecond, readout, vector = call(
        unpack_kernel,
        [
            ((1, C), F32),
            ((BASIS, HIDDEN), F32),
            ((HIDDEN, 10 * C), F32),
            ((5, C, C), F32),
            ((BASIS, HIDDEN), F32),
            ((HIDDEN, 5 * C), F32),
            ((C, C), F32),
            ((1, C), F32),
        ],
        [((REDUCE_ROWS, C), F32)],
        10**6,
        core,
        mine,
        other,
    )
    return (
        loss[0, 0],
        feature_grad.transpose(1, 0, 2)[None, None],
        first,
        second,
        mixing_grad,
        pfirst,
        psecond,
        readout,
        vector[0],
    )


def solution(mesh):
    brick = [P("bx", "by", *([None] * (rank - 2))) for rank in (5, 5, 4, 3, 3, 4, 3, 3, 3)]
    in_specs = tuple(brick) + (P(),) * 7
    out_specs = (P(), P("bx", "by", None, None, None)) + (P(),) * 7
    return jax.shard_map(
        on_device, mesh=mesh, in_specs=in_specs, out_specs=out_specs, check_vma=False
    )
```

```python
import functools

import jax
import jax.numpy as jnp
import numpy as np
from jax import lax
from jax.experimental import pallas as pl
from jax.experimental.pallas import tpu as pltpu
from jax.sharding import PartitionSpec as P

C = 128
COMP = 25
BASIS = 20
HIDDEN = 64
ATOMS = 128
EDGES = 1024
PEDGES = 512
PROBES = 128
WIDE = COMP * C
EB = 512
DEGREES = (1, 3, 5, 7, 9)
STARTS = (0, 1, 4, 9, 16)
HIGHEST = lax.Precision.HIGHEST
F32 = jnp.float32
BF16 = jnp.bfloat16
REDUCE_ROWS = 2048
LOSS_ROW = 1736


def dot(a, b):
    return jnp.dot(a, b, preferred_element_type=F32)


def dot_exact(a, b):
    return jnp.dot(a, b, preferred_element_type=F32, precision=HIGHEST)


def dot_nt(a, b, precision=None):
    return lax.dot_general(
        a, b, (((1,), (1,)), ((), ())), preferred_element_type=F32, precision=precision
    )


def dot_tn(a, b, precision=None):
    return lax.dot_general(
        a, b, (((0,), (0,)), ((), ())), preferred_element_type=F32, precision=precision
    )


def split(a):
    high = a.astype(BF16)
    return high, (a - high.astype(F32)).astype(BF16)


def sigmoid(a):
    return 1.0 / (1.0 + jnp.exp(-a))


def cols(component):
    return slice(component * C, (component + 1) * C)


def chunks(degree):
    first = STARTS[degree]
    last = first + DEGREES[degree]
    return [(at, min(at + 2, last)) for at in range(first, last, 2)]


def harmonics(x, y, z):
    z_square = z * z
    return [
        jnp.ones_like(x),
        1.7320508 * y,
        1.7320508 * z,
        1.7320508 * x,
        3.8729833 * x * y,
        3.8729833 * y * z,
        1.118034 * (3.0 * z_square - 1.0),
        3.8729833 * x * z,
        1.9364917 * (x * x - y * y),
        2.0916501 * y * (3.0 * x * x - y * y),
        10.246951 * x * y * z,
        1.6201852 * y * (5.0 * z_square - 1.0),
        1.3228757 * z * (5.0 * z_square - 3.0),
        1.6201852 * x * (5.0 * z_square - 1.0),
        5.1234754 * z * (x * x - y * y),
        2.0916501 * x * (x * x - 3.0 * y * y),
        8.8741197 * x * y * (x * x - y * y),
        6.2749502 * y * z * (3.0 * x * x - y * y),
        3.354102 * x * y * (7.0 * z_square - 1.0),
        2.3717082 * y * z * (7.0 * z_square - 3.0),
        0.375 * (35.0 * z_square * z_square - 30.0 * z_square + 3.0),
        2.3717082 * x * z * (7.0 * z_square - 3.0),
        1.677051 * (x * x - y * y) * (7.0 * z_square - 1.0),
        6.2749502 * x * z * (x * x - 3.0 * y * y),
        2.2185299 * (x * x * x * x - 6.0 * x * x * y * y + y * y * y * y),
    ]


def pack_kernel(core, owner, features, send_index, own, low, middle, high, chosen_out, placed_out, lists):
    lists[...] = jnp.zeros_like(lists)
    for at in range(8):
        i, j = divmod(at if at < 4 else at + 1, 3)
        lists[at : at + 1, 0:16] = send_index[i, j : j + 1, :].astype(F32)
    turned = lists[...].T
    lane = lax.broadcasted_iota(jnp.int32, (16, C), 1).astype(F32)
    hits = [(turned[0:16, at : at + 1] == lane).astype(F32) for at in range(8)]
    chosen = jnp.concatenate(hits, axis=0)
    chosen_out[...] = chosen.astype(BF16)
    placed_out[...] = chosen.T.astype(BF16)
    for component in range(COMP):
        own[:, cols(component)] = features[component]
    send_packets(chosen_out[...], own, low, middle, high)


def send_packets(chosen, rows, low, middle, high):
    for first in range(0, COMP, 2):
        wide = slice(first * C, min(first + 2, COMP) * C)
        packet = dot(chosen, rows[:, wide]).astype(BF16)
        low[:, wide] = packet[0:48]
        middle[:, wide] = packet[48:80]
        high[:, wide] = packet[80:128]


def geometry(vectors, index_rows, edges, turned, basis_out):
    x, y, z = vectors[0:1], vectors[1:2], vectors[2:3]
    radius = jnp.sqrt(x * x + y * y + z * z)
    rows = harmonics(x / radius, y / radius, z / radius) + index_rows
    for at, row in enumerate(rows):
        turned[at : at + 1, :] = row
    center = 0.5 + 4.0 * lax.broadcasted_iota(jnp.int32, (24, edges), 0).astype(F32) / (BASIS - 1)
    offset = (radius - center) / 0.4
    basis = jnp.exp(-(offset * offset))
    live = lax.broadcasted_iota(jnp.int32, (24, edges), 0) < BASIS
    basis_out[...] = jnp.where(live, basis, 0.0)
    return turned[...].T


def prepare_kernel(
    vectors,
    source,
    target,
    probe_vectors,
    probe_atoms,
    grid,
    probe_index,
    first,
    second,
    pfirst,
    psecond,
    columns_out,
    basis_out,
    pre_out,
    hidden3_out,
    hidden_rows_out,
    second3_out,
    pcolumns_out,
    pbasis_out,
    ppre_out,
    phidden3_out,
    phidden_rows_out,
    psecond3_out,
    picked_out,
    turned,
    pturned,
):
    turned[...] = jnp.zeros_like(turned)
    pturned[...] = jnp.zeros_like(pturned)
    row = source[...]
    slot = jnp.where(row > ATOMS, row - 1, jnp.where(row == ATOMS, 512, row))
    columns_out[...] = geometry(
        vectors[...], [slot.astype(F32), target[...].astype(F32)], EDGES, turned, basis_out
    )
    prow = probe_atoms[...]
    pslot = jnp.where(prow > ATOMS, prow - 1, jnp.where(prow == ATOMS, 512, prow))
    pcolumns_out[...] = geometry(
        probe_vectors[...], [pslot.astype(F32)], PEDGES, pturned, pbasis_out
    )

    for basis, layer, pre, hidden3, hidden_rows in (
        (basis_out, first, pre_out, hidden3_out, hidden_rows_out),
        (pbasis_out, pfirst, ppre_out, phidden3_out, phidden_rows_out),
    ):
        before = dot_tn(layer[...], basis[0:BASIS, :], HIGHEST)
        pre[...] = before.T
        hidden = before * sigmoid(before)
        upper, lower = split(hidden)
        hidden_rows[0:HIDDEN, :] = upper
        hidden_rows[HIDDEN : 2 * HIDDEN, :] = lower
        upper, lower = split(hidden.T)
        hidden3[:, 0:HIDDEN] = upper
        hidden3[:, HIDDEN : 2 * HIDDEN] = upper
        hidden3[:, 2 * HIDDEN : 3 * HIDDEN] = lower
    for degree in range(5):
        for path in range(2):
            upper, lower = split(second[:, cols(path * 5 + degree)])
            at = cols(2 * degree + path)
            second3_out[0:HIDDEN, at] = upper
            second3_out[HIDDEN : 2 * HIDDEN, at] = lower
            second3_out[2 * HIDDEN : 3 * HIDDEN, at] = upper
    upper, lower = split(psecond[...])
    psecond3_out[0:HIDDEN, :] = upper
    psecond3_out[HIDDEN : 2 * HIDDEN, :] = lower
    psecond3_out[2 * HIDDEN : 3 * HIDDEN, :] = upper

    place = probe_index[...]
    grid_row = lax.broadcasted_iota(jnp.int32, (grid.shape[0], PROBES), 0)
    hit = (place // C == grid_row).astype(F32)
    lines = dot_tn(grid[...], hit, HIGHEST)
    lane = lax.broadcasted_iota(jnp.int32, (C, PROBES), 0)
    values = jnp.sum(jnp.where(place % C == lane, lines, 0.0), axis=0, keepdims=True)
    picked_out[...] = jnp.broadcast_to(values, (C, PROBES)).T


def fill_ghosts(rows, base, low, high, left, right):
    pieces = (
        left[16:32],
        low[16:32],
        right[16:32],
        left[0:16],
        right[0:16],
        left[32:48],
        high[16:32],
        right[32:48],
    )
    for at, piece in enumerate(pieces):
        rows[base + 16 * at : base + 16 * at + 16, :] = piece


def comp_rows(component, count=1):
    return slice(component * ATOMS, (component + count) * ATOMS)


def wide_chunks():
    return [(at, min(at + 2, COMP)) for at in range(0, COMP, 2)]


def one_hot_lanes(column, width):
    lane = lax.broadcasted_iota(jnp.int32, (EB, width), 1).astype(F32)
    return (column == lane).astype(F32).astype(BF16)


def one_hot_rows(row, height):
    place = lax.broadcasted_iota(jnp.int32, (height, row.shape[1]), 0)
    return (row == place).astype(F32).astype(BF16)


def fold_source(row):
    return jnp.where(row > ATOMS, row - 1, jnp.where(row == ATOMS, 512, row))


def layer_kernel(
    own,
    low,
    high,
    left,
    right,
    columns,
    target,
    hidden3,
    second3,
    mixing,
    chosen,
    updated,
    gathered,
    mixed,
    table,
    low_out,
    middle_out,
    high_out,
    messages,
    parts,
):
    table[0:ATOMS, :] = own[...]
    fill_ghosts(table, ATOMS, low, high, left, right)

    def block(step, carry):
        rows = pl.ds(pl.multiple_of(step * EB, EB), EB)
        column = columns[rows, :]
        pick = one_hot_lanes(column[:, 25:26], 2 * ATOMS)
        hidden = hidden3[rows, :]
        scalar = dot(pick, table[:, cols(0)])
        for degree in range(5):
            weight = dot(hidden, second3[:, 2 * degree * C : 2 * (degree + 1) * C])
            straight = weight[:, 0:C]
            cross = weight[:, C:] * scalar
            for first, last in chunks(degree):
                sender = dot(pick, table[:, first * C : last * C])
                for component in range(first, last):
                    value = sender[:, cols(component - first)]
                    message = straight * value + cross * column[:, component : component + 1]
                    messages[rows, cols(component)] = message.astype(BF16)
        return carry

    lax.fori_loop(0, EDGES // EB, block, 0)
    put = one_hot_rows(target[...], ATOMS)
    for first, last in wide_chunks():
        here = dot(put, messages[:, first * C : last * C]) * 0.125
        for component in range(first, last):
            upper, lower = split(here[:, cols(component - first)])
            gathered[comp_rows(component), :] = upper
            parts[comp_rows(component), 0:C] = upper
            parts[comp_rows(component), C:] = lower
    gate = None
    for degree in range(5):
        upper, lower = split(mixing[degree])
        twice = jnp.concatenate([upper, upper], axis=0)
        for component in range(STARTS[degree], STARTS[degree] + DEGREES[degree]):
            rows = comp_rows(component)
            out = dot(parts[rows, :], twice) + dot(parts[rows, 0:C], lower)
            mixed[rows, :] = out
            if component == 0:
                gate = sigmoid(out)
            new = own[:, cols(component)].astype(F32) + out * gate
            updated[:, cols(component)] = new.astype(BF16)
    send_packets(chosen[...], updated, low_out, middle_out, high_out)


def sum_table_grads(put, messages, own_grad, low, middle, high, add):
    for first, last in wide_chunks():
        wide = slice(first * C, last * C)
        total = dot(put, messages[:, wide])
        for component in range(first, last):
            here = total[0:ATOMS, cols(component - first)]
            if add is not None:
                here = here + add[comp_rows(component), :]
            own_grad[comp_rows(component), :] = here
        ghosts = total[ATOMS:, :].astype(BF16)
        low[:, wide] = ghosts[0:48]
        middle[:, wide] = ghosts[48:80]
        high[:, wide] = ghosts[80:128]


def probe_kernel(
    own,
    low,
    high,
    left,
    right,
    columns,
    atoms,
    hidden3,
    second3,
    first_readout,
    second_readout,
    picked,
    grad_own,
    low_out,
    middle_out,
    high_out,
    weight_grad,
    readout_grads,
    table,
    partial,
    contribution,
    messages,
):
    table[0:ATOMS, :] = own[...]
    fill_ghosts(table, ATOMS, low, high, left, right)

    def forward(step, carry):
        rows = pl.ds(pl.multiple_of(step * EB, EB), EB)
        column = columns[rows, :]
        pick = one_hot_lanes(column[:, 25:26], 2 * ATOMS)
        hidden = hidden3[rows, :]
        total = jnp.zeros((EB, C), F32)
        for degree in range(5):
            weight = dot(hidden, second3[:, cols(degree)])
            here = jnp.zeros((EB, C), F32)
            for first, last in chunks(degree):
                sender = dot(pick, table[:, first * C : last * C])
                for component in range(first, last):
                    value = sender[:, cols(component - first)]
                    here = here + value * column[:, component : component + 1]
            partial[rows, cols(degree)] = here
            total = total + weight * here
        contribution[rows, :] = total
        return carry

    lax.fori_loop(0, PEDGES // EB, forward, 0)

    edge = lax.broadcasted_iota(jnp.int32, (PROBES, PEDGES), 1)
    probe = lax.broadcasted_iota(jnp.int32, (PROBES, PEDGES), 0)
    pool = (edge // 4 == probe).astype(F32)
    summed = dot_exact(pool, contribution[...])
    before = dot_exact(summed, first_readout[...])
    gate = sigmoid(before)
    hidden = before * gate
    vector = second_readout[...]
    density = jnp.sum(hidden * vector, axis=1, keepdims=True)
    misfit = density - picked[...]
    loss = jnp.sum(misfit[:, 0:1] * misfit[:, 0:1], axis=0, keepdims=True) / (2.0 * PROBES)
    slope = misfit / PROBES
    d_before = slope * vector * gate * (1.0 + before * (1.0 - gate))
    readout_grads[0:C, :] = dot_tn(summed, d_before, HIGHEST)
    readout_grads[C : C + 8, :] = jnp.broadcast_to(
        jnp.sum(hidden * slope, axis=0, keepdims=True), (8, C)
    )
    readout_grads[C + 8 : C + 16, :] = jnp.broadcast_to(loss, (8, C))
    d_summed = dot_nt(d_before, first_readout[...], HIGHEST)
    contribution[...] = dot_tn(pool, d_summed, HIGHEST)

    def backward(step, carry):
        rows = pl.ds(pl.multiple_of(step * EB, EB), EB)
        column = columns[rows, :]
        hidden = hidden3[rows, :]
        slope_here = contribution[rows, :]
        for degree in range(5):
            weight = dot(hidden, second3[:, cols(degree)])
            weight_grad[rows, cols(degree)] = (slope_here * partial[rows, cols(degree)]).astype(BF16)
            down = slope_here * weight
            for component in range(STARTS[degree], STARTS[degree] + DEGREES[degree]):
                value = down * column[:, component : component + 1]
                messages[rows, cols(component)] = value.astype(BF16)
        return carry

    lax.fori_loop(0, PEDGES // EB, backward, 0)
    put = one_hot_rows(fold_source(atoms[...]), 2 * ATOMS)
    sum_table_grads(put, messages, grad_own, low_out, middle_out, high_out, None)


def network_grads(weight_grad, basis, pre, hidden_rows, second3):
    both = dot(hidden_rows[...], weight_grad[...])
    second = both[0:HIDDEN, :] + both[HIDDEN:, :]
    grads = weight_grad[...]
    d_hidden = dot_nt(grads, second3[0:HIDDEN, :]) + dot_nt(grads, second3[HIDDEN : 2 * HIDDEN, :])
    before = pre[...]
    gate = sigmoid(before)
    d_before = d_hidden * gate * (1.0 + before * (1.0 - gate))
    return second, dot_exact(basis[...], d_before)


def probe_network_kernel(weight_grad, basis, pre, hidden_rows, second3, readout_grads, out):
    second, first = network_grads(weight_grad, basis, pre, hidden_rows, second3)
    for degree in range(5):
        out[degree * HIDDEN : (degree + 1) * HIDDEN, :] = second[:, cols(degree)]
    out[320:464, :] = readout_grads[...]
    out[464:512, :] = jnp.zeros((48, C), F32)
    out[464:488, 0:HIDDEN] = first


def table_back_kernel(
    grad_own,
    low,
    high,
    left,
    right,
    mixed,
    columns,
    source,
    hidden3,
    second3,
    mixing,
    placed,
    field_grad,
    d_gathered,
    d_mixed_out,
    low_out,
    middle_out,
    high_out,
    returned,
    grad_updated,
    parts,
    messages,
):
    fill_ghosts(returned, 0, low, high, left, right)
    for first, last in wide_chunks():
        back = dot(placed[...], returned[:, first * C : last * C])
        for component in range(first, last):
            rows = comp_rows(component)
            whole = grad_own[rows, :] + back[:, cols(component - first)]
            grad_updated[rows, :] = whole.astype(BF16)
    gate_in = mixed[comp_rows(0), :]
    gate = sigmoid(gate_in)
    d_gate = jnp.zeros((ATOMS, C), F32)
    for component in range(COMP - 1, -1, -1):
        rows = comp_rows(component)
        d_updated = grad_updated[rows, :].astype(F32)
        if component > 0:
            d_gate = d_gate + d_updated * mixed[rows, :]
            d_mixed = d_updated * gate
        else:
            d_mixed = d_updated * gate * (1.0 + gate_in * (1.0 - gate)) + d_gate * gate * (
                1.0 - gate
            )
        upper, lower = split(d_mixed)
        d_mixed_out[rows, :] = upper
        parts[rows, 0:C] = upper
        parts[rows, C:] = lower
    for degree in range(5):
        upper, lower = split(mixing[degree].T)
        twice = jnp.concatenate([upper, upper], axis=0)
        for component in range(STARTS[degree], STARTS[degree] + DEGREES[degree]):
            rows = comp_rows(component)
            out = dot(parts[rows, :], twice) + dot(parts[rows, 0:C], lower)
            d_gathered[:, cols(component)] = (out * 0.125).astype(BF16)

    def block(step, carry):
        rows = pl.ds(pl.multiple_of(step * EB, EB), EB)
        column = columns[rows, :]
        pick_target = one_hot_lanes(column[:, 26:27], ATOMS)
        hidden = hidden3[rows, :]
        d_scalar = jnp.zeros((EB, C), F32)
        for degree in (4, 3, 2, 1, 0):
            weight = dot(hidden, second3[:, 2 * degree * C : 2 * (degree + 1) * C])
            straight = weight[:, 0:C]
            d_cross = jnp.zeros((EB, C), F32)
            for first, last in chunks(degree):
                d_message = dot(pick_target, d_gathered[:, first * C : last * C])
                for component in range(first, last):
                    d_here = d_message[:, cols(component - first)]
                    d_cross = d_cross + d_here * column[:, component : component + 1]
                    value = straight * d_here
                    if component == 0:
                        value = value + d_scalar + d_cross * weight[:, C:]
                    messages[rows, cols(component)] = value.astype(BF16)
            d_scalar = d_scalar + d_cross * weight[:, C:]
        return carry

    lax.fori_loop(0, EDGES // EB, block, 0)
    put = one_hot_rows(fold_source(source[...]), 2 * ATOMS)
    sum_table_grads(put, messages, field_grad, low_out, middle_out, high_out, grad_updated)


def weights_back_kernel(
    core,
    d_gathered,
    d_mixed,
    table,
    gathered,
    columns,
    basis,
    pre,
    hidden_rows,
    second3,
    probe_grads,
    mine_out,
    other_out,
    weight_grad,
    reduced,
):
    for degree in range(5):
        rows = comp_rows(STARTS[degree], DEGREES[degree])
        reduced[640 + degree * C : 640 + (degree + 1) * C, :] = dot_tn(
            gathered[rows, :], d_mixed[rows, :]
        )

    def block(step, carry):
        rows = pl.ds(pl.multiple_of(step * EB, EB), EB)
        column = columns[rows, :]
        pick = one_hot_lanes(column[:, 25:26], 2 * ATOMS)
        pick_target = one_hot_lanes(column[:, 26:27], ATOMS)
        scalar = dot(pick, table[:, cols(0)])
        for degree in range(5):
            d_straight = jnp.zeros((EB, C), F32)
            d_cross = jnp.zeros((EB, C), F32)
            for first, last in chunks(degree):
                wide = slice(first * C, last * C)
                sender = dot(pick, table[:, wide])
                d_message = dot(pick_target, d_gathered[:, wide])
                for component in range(first, last):
                    here = cols(component - first)
                    d_here = d_message[:, here]
                    d_straight = d_straight + d_here * sender[:, here]
                    d_cross = d_cross + d_here * column[:, component : component + 1]
            weight_grad[rows, cols(2 * degree)] = d_straight.astype(BF16)
            weight_grad[rows, cols(2 * degree + 1)] = (d_cross * scalar).astype(BF16)
        return carry

    lax.fori_loop(0, EDGES // EB, block, 0)
    second, first = network_grads(weight_grad, basis, pre, hidden_rows, second3)
    for degree in range(5):
        for path in range(2):
            at = (path * 5 + degree) * HIDDEN
            reduced[at : at + HIDDEN, :] = second[:, cols(2 * degree + path)]
    reduced[1280:1792, :] = probe_grads[...]
    reduced[1792:REDUCE_ROWS, :] = jnp.zeros((REDUCE_ROWS - 1792, C), F32)
    reduced[1792:1816, 0:HIDDEN] = first
    half = REDUCE_ROWS // 2
    side = core[0]
    mine_out[...] = reduced[pl.ds(pl.multiple_of(side * half, half), half), :]
    other_out[...] = reduced[pl.ds(pl.multiple_of((1 - side) * half, half), half), :]


def share_kernel(place, pieces, out):
    count = pieces.shape[0]
    total = pieces[0]
    for at in range(1, count):
        total = total + pieces[at]
    row = lax.broadcasted_iota(jnp.int32, total.shape, 0)
    rest = total - total.astype(BF16).astype(F32)
    ours = (row >= LOSS_ROW % total.shape[0] + 4) & (row < LOSS_ROW % total.shape[0] + 8)
    total = jnp.where(ours & (place[0] == 1), rest, total).astype(BF16)
    for at in range(count):
        out[at] = total


def finish_kernel(field_grad, low, high, left, right, placed, out, returned):
    fill_ghosts(returned, 0, low, high, left, right)
    for first, last in wide_chunks():
        back = dot(placed[...], returned[:, first * C : last * C])
        for component in range(first, last):
            out[component] = field_grad[comp_rows(component), :] + back[:, cols(component - first)]


def unpack_kernel(
    core, mine, other, loss, first, second, mixing, pfirst, psecond, readout, vector, sums
):
    half = REDUCE_ROWS // 2
    side = core[0]
    sums[pl.ds(pl.multiple_of(side * half, half), half), :] = mine[...].astype(F32)
    sums[pl.ds(pl.multiple_of((1 - side) * half, half), half), :] = other[...].astype(F32)
    for block in range(10):
        second[:, cols(block)] = sums[block * HIDDEN : (block + 1) * HIDDEN, :]
    for degree in range(5):
        mixing[degree] = sums[640 + degree * C : 640 + (degree + 1) * C, :]
        psecond[:, cols(degree)] = sums[1280 + degree * HIDDEN : 1280 + (degree + 1) * HIDDEN, :]
    readout[...] = sums[1600:1728, :]
    vector[...] = sums[1728:1729, :]
    loss[...] = sums[LOSS_ROW : LOSS_ROW + 1, :] + sums[LOSS_ROW + 4 : LOSS_ROW + 5, :]
    pfirst[...] = sums[1744 : 1744 + BASIS, 0:HIDDEN]
    first[...] = sums[1792 : 1792 + BASIS, 0:HIDDEN]


def call(kernel, outs, scratch, flops, *operands):
    shapes = [jax.ShapeDtypeStruct(shape, dtype) for shape, dtype in outs]
    moved = sum(x.size * x.dtype.itemsize for x in list(operands) + shapes)
    held = sum(np.prod(shape) * jnp.dtype(dtype).itemsize for shape, dtype in scratch)
    whole = pl.BlockSpec(memory_space=pltpu.VMEM)
    scalar = pl.BlockSpec(memory_space=pltpu.SMEM)
    return pl.pallas_call(
        kernel,
        out_shape=shapes,
        in_specs=[scalar if x.shape == (1,) else whole for x in operands],
        out_specs=[whole] * len(shapes),
        scratch_shapes=[pltpu.VMEM(shape, dtype) for shape, dtype in scratch],
        compiler_params=pltpu.CompilerParams(vmem_limit_bytes=int(held) + 12 * 1024 * 1024),
        cost_estimate=pl.CostEstimate(flops=flops, bytes_accessed=moved, transcendentals=0),
    )(*operands)


PACKETS = [((48, WIDE), BF16), ((32, WIDE), BF16), ((48, WIDE), BF16)]


def relay_kernel(middle, low, high, to_right, to_left):
    to_right[0:16, :] = middle[16:32, :]
    to_right[16:32, :] = low[32:48, :]
    to_right[32:48, :] = high[32:48, :]
    to_left[0:16, :] = middle[0:16, :]
    to_left[16:32, :] = low[0:16, :]
    to_left[32:48, :] = high[0:16, :]


def ring(axis):
    count = lax.axis_size(axis)
    up = [(i, (i + 1) % count) for i in range(count)]
    down = [(b, a) for a, b in up]
    return up, down


def exchange(low_packet, middle_packet, high_packet):
    up, down = ring("bx")
    low = lax.ppermute(high_packet, "bx", up)
    high = lax.ppermute(low_packet, "bx", down)
    up, down = ring("by")
    to_right, to_left = call(
        relay_kernel, [((48, WIDE), BF16)] * 2, [], 10**5, middle_packet, low, high
    )
    left = lax.ppermute(to_right, "by", up)
    right = lax.ppermute(to_left, "by", down)
    return (low, high, left, right), (to_right, to_left)


def reduce_halves(mine, other, owner):
    n_x, n_y = lax.axis_size("bx"), lax.axis_size("by")
    count = n_x * n_y // 2
    axes = ("bx", "by")
    swap = [(i, i ^ 1) for i in range(n_y)]
    groups = [[2 * i + core for i in range(count)] for core in range(2)]
    pair = (mine + lax.ppermute(other, "by", swap)).reshape(count, -1, C)
    pieces = lax.all_to_all(pair, axes, 0, 0, axis_index_groups=groups, tiled=True)
    (spread,) = call(share_kernel, [(pair.shape, BF16)], [], 10**6, owner, pieces)
    whole = lax.all_to_all(spread, axes, 0, 0, axis_index_groups=groups, tiled=True)
    whole = whole.reshape(mine.shape)
    return whole, lambda after: lax.ppermute(lax.optimization_barrier((whole, after))[0], "by", swap)


def on_device(
    features,
    send_index,
    atom_vectors,
    atom_source,
    atom_target,
    probe_vectors,
    probe_atoms,
    density_grid,
    probe_index,
    radial_first,
    radial_second,
    mixing,
    probe_first,
    probe_second,
    readout_first,
    readout_second,
):
    field = features[0, 0].transpose(1, 0, 2)
    source = atom_source.reshape(1, EDGES)
    target = atom_target.reshape(1, EDGES)
    atoms = probe_atoms.reshape(1, PEDGES)
    n_y = lax.axis_size("by")
    core = (lax.axis_index("by") % 2).reshape(1)
    chunk = REDUCE_ROWS // (lax.axis_size("bx") * n_y)
    half, place = divmod(LOSS_ROW, REDUCE_ROWS // 2)
    loss_at = 2 * (place // chunk) + half
    owner = (lax.axis_index("bx") * n_y + lax.axis_index("by") == loss_at).astype(jnp.int32).reshape(1)

    own, low, middle, high, chosen, placed = call(
        pack_kernel,
        [((ATOMS, WIDE), BF16)] + PACKETS + [((C, ATOMS), BF16), ((ATOMS, C), BF16)],
        [((C, C), F32)],
        2 * C * C * WIDE,
        core,
        owner,
        field,
        send_index[0, 0],
    )
    received, _ = exchange(low, middle, high)
    (
        columns,
        basis,
        pre,
        hidden3,
        hidden_rows,
        second3,
        pcolumns,
        pbasis,
        ppre,
        phidden3,
        phidden_rows,
        psecond3,
        picked,
    ) = call(
        prepare_kernel,
        [
            ((EDGES, C), F32),
            ((24, EDGES), F32),
            ((EDGES, HIDDEN), F32),
            ((EDGES, 3 * HIDDEN), BF16),
            ((2 * HIDDEN, EDGES), BF16),
            ((3 * HIDDEN, 10 * C), BF16),
            ((PEDGES, C), F32),
            ((24, PEDGES), F32),
            ((PEDGES, HIDDEN), F32),
            ((PEDGES, 3 * HIDDEN), BF16),
            ((2 * HIDDEN, PEDGES), BF16),
            ((3 * HIDDEN, 5 * C), BF16),
            ((PROBES, C), F32),
        ],
        [((C, EDGES), F32), ((C, PEDGES), F32)],
        10**9,
        atom_vectors[0, 0],
        source,
        target,
        probe_vectors[0, 0],
        atoms,
        density_grid.reshape(-1, C),
        probe_index.reshape(1, PROBES),
        radial_first,
        radial_second,
        probe_first,
        probe_second,
    )
    updated, gathered, mixed, table, low, middle, high = call(
        layer_kernel,
        [
            ((ATOMS, WIDE), BF16),
            ((COMP * ATOMS, C), BF16),
            ((COMP * ATOMS, C), F32),
            ((2 * ATOMS, WIDE), BF16),
        ]
        + PACKETS,
        [((EDGES, WIDE), BF16), ((COMP * ATOMS, 2 * C), BF16)],
        4 * 10**9,
        own,
        *received,
        columns,
        target,
        hidden3,
        second3,
        mixing,
        chosen,
    )
    received, _ = exchange(low, middle, high)
    grad_own, low, middle, high, weight_grad, readout_grads = call(
        probe_kernel,
        [((COMP * ATOMS, C), F32)]
        + PACKETS
        + [
            ((PEDGES, 5 * C), BF16),
            ((C + 16, C), F32),
        ],
        [
            ((2 * ATOMS, WIDE), BF16),
            ((PEDGES, 5 * C), F32),
            ((PEDGES, C), F32),
            ((PEDGES, WIDE), BF16),
        ],
        4 * 10**9,
        updated,
        *received,
        pcolumns,
        atoms,
        phidden3,
        psecond3,
        readout_first,
        readout_second.reshape(1, C),
        picked,
    )
    received, _ = exchange(low, middle, high)
    (probe_grads,) = call(
        probe_network_kernel,
        [((512, C), F32)],
        [],
        10**9,
        weight_grad,
        pbasis,
        ppre,
        phidden_rows,
        psecond3,
        readout_grads,
    )
    field_grad, d_gathered, d_mixed, low, middle, high = call(
        table_back_kernel,
        [
            ((COMP * ATOMS, C), F32),
            ((ATOMS, WIDE), BF16),
            ((COMP * ATOMS, C), BF16),
        ]
        + PACKETS,
        [
            ((C, WIDE), BF16),
            ((COMP * ATOMS, C), BF16),
            ((COMP * ATOMS, 2 * C), BF16),
            ((EDGES, WIDE), BF16),
        ],
        6 * 10**9,
        grad_own,
        *received,
        mixed,
        columns,
        source,
        hidden3,
        second3,
        mixing,
        placed,
    )
    received, relays = exchange(low, middle, high)
    mine, other = call(
        weights_back_kernel,
        [((REDUCE_ROWS // 2, C), F32), ((REDUCE_ROWS // 2, C), F32)],
        [((EDGES, 10 * C), BF16), ((REDUCE_ROWS, C), F32)],
        6 * 10**9,
        core,
        d_gathered,
        d_mixed,
        table,
        gathered,
        columns,
        basis,
        pre,
        hidden_rows,
        second3,
        probe_grads,
    )
    (feature_grad,) = call(
        finish_kernel,
        [((COMP, ATOMS, C), F32)],
        [((C, WIDE), BF16)],
        2 * C * C * WIDE,
        field_grad,
        *received,
        placed,
    )
    mine, other, *_ = lax.optimization_barrier((mine, other, received[0], received[1]))
    mine, swapped = reduce_halves(mine, other, owner)
    other = swapped(feature_grad)
    loss, first, second, mixing_grad, pfirst, psecond, readout, vector = call(
        unpack_kernel,
        [
            ((1, C), F32),
            ((BASIS, HIDDEN), F32),
            ((HIDDEN, 10 * C), F32),
            ((5, C, C), F32),
            ((BASIS, HIDDEN), F32),
            ((HIDDEN, 5 * C), F32),
            ((C, C), F32),
            ((1, C), F32),
        ],
        [((REDUCE_ROWS, C), F32)],
        10**6,
        core,
        mine,
        other,
    )
    return (
        loss[0, 0],
        feature_grad.transpose(1, 0, 2)[None, None],
        first,
        second,
        mixing_grad,
        pfirst,
        psecond,
        readout,
        vector[0],
    )


def solution(mesh):
    brick = [P("bx", "by", *([None] * (rank - 2))) for rank in (5, 5, 4, 3, 3, 4, 3, 3, 3)]
    in_specs = tuple(brick) + (P(),) * 7
    out_specs = (P(), P("bx", "by", None, None, None)) + (P(),) * 7
    return jax.shard_map(
        on_device, mesh=mesh, in_specs=in_specs, out_specs=out_specs, check_vma=False
    )
```

```python
import functools

import jax
import jax.numpy as jnp
import numpy as np
from jax import lax
from jax.experimental import pallas as pl
from jax.experimental.pallas import tpu as pltpu
from jax.sharding import PartitionSpec as P

C = 128
COMP = 25
BASIS = 20
HIDDEN = 64
ATOMS = 128
EDGES = 1024
PEDGES = 512
PROBES = 128
WIDE = COMP * C
EB = 512
DEGREES = (1, 3, 5, 7, 9)
STARTS = (0, 1, 4, 9, 16)
HIGHEST = lax.Precision.HIGHEST
F32 = jnp.float32
BF16 = jnp.bfloat16
REDUCE_ROWS = 2048
LOSS_ROW = 1736


def dot(a, b):
    return jnp.dot(a, b, preferred_element_type=F32)


def dot_exact(a, b):
    return jnp.dot(a, b, preferred_element_type=F32, precision=HIGHEST)


def dot_nt(a, b, precision=None):
    return lax.dot_general(
        a, b, (((1,), (1,)), ((), ())), preferred_element_type=F32, precision=precision
    )


def dot_tn(a, b, precision=None):
    return lax.dot_general(
        a, b, (((0,), (0,)), ((), ())), preferred_element_type=F32, precision=precision
    )


def split(a):
    high = a.astype(BF16)
    return high, (a - high.astype(F32)).astype(BF16)


def sigmoid(a):
    return 1.0 / (1.0 + jnp.exp(-a))


def cols(component):
    return slice(component * C, (component + 1) * C)


def chunks(degree):
    first = STARTS[degree]
    last = first + DEGREES[degree]
    return [(at, min(at + 2, last)) for at in range(first, last, 2)]


def harmonics(x, y, z):
    z_square = z * z
    return [
        jnp.ones_like(x),
        1.7320508 * y,
        1.7320508 * z,
        1.7320508 * x,
        3.8729833 * x * y,
        3.8729833 * y * z,
        1.118034 * (3.0 * z_square - 1.0),
        3.8729833 * x * z,
        1.9364917 * (x * x - y * y),
        2.0916501 * y * (3.0 * x * x - y * y),
        10.246951 * x * y * z,
        1.6201852 * y * (5.0 * z_square - 1.0),
        1.3228757 * z * (5.0 * z_square - 3.0),
        1.6201852 * x * (5.0 * z_square - 1.0),
        5.1234754 * z * (x * x - y * y),
        2.0916501 * x * (x * x - 3.0 * y * y),
        8.8741197 * x * y * (x * x - y * y),
        6.2749502 * y * z * (3.0 * x * x - y * y),
        3.354102 * x * y * (7.0 * z_square - 1.0),
        2.3717082 * y * z * (7.0 * z_square - 3.0),
        0.375 * (35.0 * z_square * z_square - 30.0 * z_square + 3.0),
        2.3717082 * x * z * (7.0 * z_square - 3.0),
        1.677051 * (x * x - y * y) * (7.0 * z_square - 1.0),
        6.2749502 * x * z * (x * x - 3.0 * y * y),
        2.2185299 * (x * x * x * x - 6.0 * x * x * y * y + y * y * y * y),
    ]


def pack_kernel(core, owner, features, send_index, own, low, middle, high, chosen_out, placed_out, lists):
    lists[...] = jnp.zeros_like(lists)
    for at in range(8):
        j, i = divmod(at if at < 4 else at + 1, 3)
        lists[at : at + 1, 0:16] = send_index[i, j : j + 1, :].astype(F32)
    turned = lists[...].T
    lane = lax.broadcasted_iota(jnp.int32, (16, C), 1).astype(F32)
    hits = [(turned[0:16, at : at + 1] == lane).astype(F32) for at in range(8)]
    chosen = jnp.concatenate(hits, axis=0)
    chosen_out[...] = chosen.astype(BF16)
    placed_out[...] = chosen.T.astype(BF16)
    for component in range(COMP):
        own[:, cols(component)] = features[component]
    send_packets(chosen_out[...], own, low, middle, high)


def send_packets(chosen, rows, low, middle, high):
    for first in range(0, COMP, 2):
        wide = slice(first * C, min(first + 2, COMP) * C)
        packet = dot(chosen, rows[:, wide]).astype(BF16)
        low[:, wide] = packet[0:48]
        middle[:, wide] = packet[48:80]
        high[:, wide] = packet[80:128]


def geometry(vectors, index_rows, edges, turned, basis_out):
    x, y, z = vectors[0:1], vectors[1:2], vectors[2:3]
    radius = jnp.sqrt(x * x + y * y + z * z)
    rows = harmonics(x / radius, y / radius, z / radius) + index_rows
    for at, row in enumerate(rows):
        turned[at : at + 1, :] = row
    center = 0.5 + 4.0 * lax.broadcasted_iota(jnp.int32, (24, edges), 0).astype(F32) / (BASIS - 1)
    offset = (radius - center) / 0.4
    basis = jnp.exp(-(offset * offset))
    live = lax.broadcasted_iota(jnp.int32, (24, edges), 0) < BASIS
    basis_out[...] = jnp.where(live, basis, 0.0)
    return turned[...].T


def prepare_kernel(
    vectors,
    source,
    target,
    probe_vectors,
    probe_atoms,
    grid,
    probe_index,
    first,
    second,
    pfirst,
    psecond,
    columns_out,
    basis_out,
    pre_out,
    hidden3_out,
    hidden_rows_out,
    second3_out,
    pcolumns_out,
    pbasis_out,
    ppre_out,
    phidden3_out,
    phidden_rows_out,
    psecond3_out,
    picked_out,
    turned,
    pturned,
):
    turned[...] = jnp.zeros_like(turned)
    pturned[...] = jnp.zeros_like(pturned)
    row = source[...]
    slot = jnp.where(row > ATOMS, row - 1, jnp.where(row == ATOMS, 512, row))
    columns_out[...] = geometry(
        vectors[...], [slot.astype(F32), target[...].astype(F32)], EDGES, turned, basis_out
    )
    prow = probe_atoms[...]
    pslot = jnp.where(prow > ATOMS, prow - 1, jnp.where(prow == ATOMS, 512, prow))
    pcolumns_out[...] = geometry(
        probe_vectors[...], [pslot.astype(F32)], PEDGES, pturned, pbasis_out
    )

    for basis, layer, pre, hidden3, hidden_rows in (
        (basis_out, first, pre_out, hidden3_out, hidden_rows_out),
        (pbasis_out, pfirst, ppre_out, phidden3_out, phidden_rows_out),
    ):
        before = dot_tn(layer[...], basis[0:BASIS, :], HIGHEST)
        pre[...] = before.T
        hidden = before * sigmoid(before)
        upper, lower = split(hidden)
        hidden_rows[0:HIDDEN, :] = upper
        hidden_rows[HIDDEN : 2 * HIDDEN, :] = lower
        upper, lower = split(hidden.T)
        hidden3[:, 0:HIDDEN] = upper
        hidden3[:, HIDDEN : 2 * HIDDEN] = upper
        hidden3[:, 2 * HIDDEN : 3 * HIDDEN] = lower
    for degree in range(5):
        for path in range(2):
            upper, lower = split(second[:, cols(path * 5 + degree)])
            at = cols(2 * degree + path)
            second3_out[0:HIDDEN, at] = upper
            second3_out[HIDDEN : 2 * HIDDEN, at] = lower
            second3_out[2 * HIDDEN : 3 * HIDDEN, at] = upper
    upper, lower = split(psecond[...])
    psecond3_out[0:HIDDEN, :] = upper
    psecond3_out[HIDDEN : 2 * HIDDEN, :] = lower
    psecond3_out[2 * HIDDEN : 3 * HIDDEN, :] = upper

    place = probe_index[...]
    grid_row = lax.broadcasted_iota(jnp.int32, (grid.shape[0], PROBES), 0)
    hit = (place // C == grid_row).astype(F32)
    lines = dot_tn(grid[...], hit, HIGHEST)
    lane = lax.broadcasted_iota(jnp.int32, (C, PROBES), 0)
    values = jnp.sum(jnp.where(place % C == lane, lines, 0.0), axis=0, keepdims=True)
    picked_out[...] = jnp.broadcast_to(values, (C, PROBES)).T


TABLE_ORDER = (0, 3, 5, 1, 6, 2, 4, 7)
PACKET_ORDER = tuple(range(8))


def fill_ghosts(rows, base, low, high, left, right, order):
    pieces = (
        left[16:32],
        low[16:32],
        right[16:32],
        left[0:16],
        right[0:16],
        left[32:48],
        high[16:32],
        right[32:48],
    )
    for at, piece in zip(order, pieces):
        rows[base + 16 * at : base + 16 * at + 16, :] = piece


def comp_rows(component, count=1):
    return slice(component * ATOMS, (component + count) * ATOMS)


def wide_chunks():
    return [(at, min(at + 2, COMP)) for at in range(0, COMP, 2)]


def one_hot_lanes(column, width):
    lane = lax.broadcasted_iota(jnp.int32, (EB, width), 1).astype(F32)
    return (column == lane).astype(F32).astype(BF16)


def one_hot_rows(row, height):
    place = lax.broadcasted_iota(jnp.int32, (height, row.shape[1]), 0)
    return (row == place).astype(F32).astype(BF16)


def fold_source(row):
    return jnp.where(row > ATOMS, row - 1, jnp.where(row == ATOMS, 512, row))


def layer_kernel(
    own,
    low,
    high,
    left,
    right,
    columns,
    target,
    hidden3,
    second3,
    mixing,
    chosen,
    updated,
    gathered,
    mixed,
    table,
    low_out,
    middle_out,
    high_out,
    messages,
    parts,
):
    table[0:ATOMS, :] = own[...]
    fill_ghosts(table, ATOMS, low, high, left, right, TABLE_ORDER)

    def block(step, carry):
        rows = pl.ds(pl.multiple_of(step * EB, EB), EB)
        column = columns[rows, :]
        pick = one_hot_lanes(column[:, 25:26], 2 * ATOMS)
        hidden = hidden3[rows, :]
        scalar = dot(pick, table[:, cols(0)])
        for degree in range(5):
            weight = dot(hidden, second3[:, 2 * degree * C : 2 * (degree + 1) * C])
            straight = weight[:, 0:C]
            cross = weight[:, C:] * scalar
            for first, last in chunks(degree):
                sender = dot(pick, table[:, first * C : last * C])
                for component in range(first, last):
                    value = sender[:, cols(component - first)]
                    message = straight * value + cross * column[:, component : component + 1]
                    messages[rows, cols(component)] = message.astype(BF16)
        return carry

    lax.fori_loop(0, EDGES // EB, block, 0)
    put = one_hot_rows(target[...], ATOMS)
    for first, last in wide_chunks():
        here = dot(put, messages[:, first * C : last * C]) * 0.125
        for component in range(first, last):
            upper, lower = split(here[:, cols(component - first)])
            gathered[comp_rows(component), :] = upper
            parts[comp_rows(component), 0:C] = upper
            parts[comp_rows(component), C:] = lower
    gate = None
    for degree in range(5):
        upper, lower = split(mixing[degree])
        twice = jnp.concatenate([upper, upper], axis=0)
        for component in range(STARTS[degree], STARTS[degree] + DEGREES[degree]):
            rows = comp_rows(component)
            out = dot(parts[rows, :], twice) + dot(parts[rows, 0:C], lower)
            mixed[rows, :] = out
            if component == 0:
                gate = sigmoid(out)
            new = own[:, cols(component)].astype(F32) + out * gate
            updated[:, cols(component)] = new.astype(BF16)
    send_packets(chosen[...], updated, low_out, middle_out, high_out)


def sum_table_grads(put, messages, own_grad, low, middle, high, add):
    for first, last in wide_chunks():
        wide = slice(first * C, last * C)
        total = dot(put, messages[:, wide])
        for component in range(first, last):
            here = total[0:ATOMS, cols(component - first)]
            if add is not None:
                here = here + add[comp_rows(component), :]
            own_grad[comp_rows(component), :] = here
        ghosts = total[ATOMS:, :].astype(BF16)
        for place, at in enumerate(TABLE_ORDER):
            piece = ghosts[16 * at : 16 * at + 16]
            if place < 3:
                low[16 * place : 16 * place + 16, wide] = piece
            elif place < 5:
                middle[16 * (place - 3) : 16 * (place - 3) + 16, wide] = piece
            else:
                high[16 * (place - 5) : 16 * (place - 5) + 16, wide] = piece


def probe_kernel(
    own,
    low,
    high,
    left,
    right,
    columns,
    atoms,
    hidden3,
    second3,
    first_readout,
    second_readout,
    picked,
    grad_own,
    low_out,
    middle_out,
    high_out,
    weight_grad,
    readout_grads,
    table,
    partial,
    contribution,
    messages,
):
    table[0:ATOMS, :] = own[...]
    fill_ghosts(table, ATOMS, low, high, left, right, TABLE_ORDER)

    def forward(step, carry):
        rows = pl.ds(pl.multiple_of(step * EB, EB), EB)
        column = columns[rows, :]
        pick = one_hot_lanes(column[:, 25:26], 2 * ATOMS)
        hidden = hidden3[rows, :]
        total = jnp.zeros((EB, C), F32)
        for degree in range(5):
            weight = dot(hidden, second3[:, cols(degree)])
            here = jnp.zeros((EB, C), F32)
            for first, last in chunks(degree):
                sender = dot(pick, table[:, first * C : last * C])
                for component in range(first, last):
                    value = sender[:, cols(component - first)]
                    here = here + value * column[:, component : component + 1]
            partial[rows, cols(degree)] = here
            total = total + weight * here
        contribution[rows, :] = total
        return carry

    lax.fori_loop(0, PEDGES // EB, forward, 0)

    edge = lax.broadcasted_iota(jnp.int32, (PROBES, PEDGES), 1)
    probe = lax.broadcasted_iota(jnp.int32, (PROBES, PEDGES), 0)
    pool = (edge // 4 == probe).astype(F32)
    summed = dot_exact(pool, contribution[...])
    before = dot_exact(summed, first_readout[...])
    gate = sigmoid(before)
    hidden = before * gate
    vector = second_readout[...]
    density = jnp.sum(hidden * vector, axis=1, keepdims=True)
    misfit = density - picked[...]
    loss = jnp.sum(misfit[:, 0:1] * misfit[:, 0:1], axis=0, keepdims=True) / (2.0 * PROBES)
    slope = misfit / PROBES
    d_before = slope * vector * gate * (1.0 + before * (1.0 - gate))
    readout_grads[0:C, :] = dot_tn(summed, d_before, HIGHEST)
    readout_grads[C : C + 8, :] = jnp.broadcast_to(
        jnp.sum(hidden * slope, axis=0, keepdims=True), (8, C)
    )
    readout_grads[C + 8 : C + 16, :] = jnp.broadcast_to(loss, (8, C))
    d_summed = dot_nt(d_before, first_readout[...], HIGHEST)
    contribution[...] = dot_tn(pool, d_summed, HIGHEST)

    def backward(step, carry):
        rows = pl.ds(pl.multiple_of(step * EB, EB), EB)
        column = columns[rows, :]
        hidden = hidden3[rows, :]
        slope_here = contribution[rows, :]
        for degree in range(5):
            weight = dot(hidden, second3[:, cols(degree)])
            weight_grad[rows, cols(degree)] = (slope_here * partial[rows, cols(degree)]).astype(BF16)
            down = slope_here * weight
            for component in range(STARTS[degree], STARTS[degree] + DEGREES[degree]):
                value = down * column[:, component : component + 1]
                messages[rows, cols(component)] = value.astype(BF16)
        return carry

    lax.fori_loop(0, PEDGES // EB, backward, 0)
    put = one_hot_rows(fold_source(atoms[...]), 2 * ATOMS)
    sum_table_grads(put, messages, grad_own, low_out, middle_out, high_out, None)


def network_grads(weight_grad, basis, pre, hidden_rows, second3):
    both = dot(hidden_rows[...], weight_grad[...])
    second = both[0:HIDDEN, :] + both[HIDDEN:, :]
    grads = weight_grad[...]
    d_hidden = dot_nt(grads, second3[0:HIDDEN, :]) + dot_nt(grads, second3[HIDDEN : 2 * HIDDEN, :])
    before = pre[...]
    gate = sigmoid(before)
    d_before = d_hidden * gate * (1.0 + before * (1.0 - gate))
    return second, dot_exact(basis[...], d_before)


def probe_network_kernel(weight_grad, basis, pre, hidden_rows, second3, readout_grads, out):
    second, first = network_grads(weight_grad, basis, pre, hidden_rows, second3)
    for degree in range(5):
        out[degree * HIDDEN : (degree + 1) * HIDDEN, :] = second[:, cols(degree)]
    out[320:464, :] = readout_grads[...]
    out[464:512, :] = jnp.zeros((48, C), F32)
    out[464:488, 0:HIDDEN] = first


def table_back_kernel(
    grad_own,
    low,
    high,
    left,
    right,
    mixed,
    columns,
    source,
    hidden3,
    second3,
    mixing,
    placed,
    field_grad,
    d_gathered,
    d_mixed_out,
    low_out,
    middle_out,
    high_out,
    returned,
    grad_updated,
    parts,
    messages,
):
    fill_ghosts(returned, 0, low, high, left, right, PACKET_ORDER)
    for first, last in wide_chunks():
        back = dot(placed[...], returned[:, first * C : last * C])
        for component in range(first, last):
            rows = comp_rows(component)
            whole = grad_own[rows, :] + back[:, cols(component - first)]
            grad_updated[rows, :] = whole.astype(BF16)
    gate_in = mixed[comp_rows(0), :]
    gate = sigmoid(gate_in)
    d_gate = jnp.zeros((ATOMS, C), F32)
    for component in range(COMP - 1, -1, -1):
        rows = comp_rows(component)
        d_updated = grad_updated[rows, :].astype(F32)
        if component > 0:
            d_gate = d_gate + d_updated * mixed[rows, :]
            d_mixed = d_updated * gate
        else:
            d_mixed = d_updated * gate * (1.0 + gate_in * (1.0 - gate)) + d_gate * gate * (
                1.0 - gate
            )
        upper, lower = split(d_mixed)
        d_mixed_out[rows, :] = upper
        parts[rows, 0:C] = upper
        parts[rows, C:] = lower
    for degree in range(5):
        upper, lower = split(mixing[degree].T)
        twice = jnp.concatenate([upper, upper], axis=0)
        for component in range(STARTS[degree], STARTS[degree] + DEGREES[degree]):
            rows = comp_rows(component)
            out = dot(parts[rows, :], twice) + dot(parts[rows, 0:C], lower)
            d_gathered[:, cols(component)] = (out * 0.125).astype(BF16)

    def block(step, carry):
        rows = pl.ds(pl.multiple_of(step * EB, EB), EB)
        column = columns[rows, :]
        pick_target = one_hot_lanes(column[:, 26:27], ATOMS)
        hidden = hidden3[rows, :]
        d_scalar = jnp.zeros((EB, C), F32)
        for degree in (4, 3, 2, 1, 0):
            weight = dot(hidden, second3[:, 2 * degree * C : 2 * (degree + 1) * C])
            straight = weight[:, 0:C]
            d_cross = jnp.zeros((EB, C), F32)
            for first, last in chunks(degree):
                d_message = dot(pick_target, d_gathered[:, first * C : last * C])
                for component in range(first, last):
                    d_here = d_message[:, cols(component - first)]
                    d_cross = d_cross + d_here * column[:, component : component + 1]
                    value = straight * d_here
                    if component == 0:
                        value = value + d_scalar + d_cross * weight[:, C:]
                    messages[rows, cols(component)] = value.astype(BF16)
            d_scalar = d_scalar + d_cross * weight[:, C:]
        return carry

    lax.fori_loop(0, EDGES // EB, block, 0)
    put = one_hot_rows(fold_source(source[...]), 2 * ATOMS)
    sum_table_grads(put, messages, field_grad, low_out, middle_out, high_out, grad_updated)


def weights_back_kernel(
    core,
    d_gathered,
    d_mixed,
    table,
    gathered,
    columns,
    basis,
    pre,
    hidden_rows,
    second3,
    probe_grads,
    mine_out,
    other_out,
    weight_grad,
    reduced,
):
    for degree in range(5):
        rows = comp_rows(STARTS[degree], DEGREES[degree])
        reduced[640 + degree * C : 640 + (degree + 1) * C, :] = dot_tn(
            gathered[rows, :], d_mixed[rows, :]
        )

    def block(step, carry):
        rows = pl.ds(pl.multiple_of(step * EB, EB), EB)
        column = columns[rows, :]
        pick = one_hot_lanes(column[:, 25:26], 2 * ATOMS)
        pick_target = one_hot_lanes(column[:, 26:27], ATOMS)
        scalar = dot(pick, table[:, cols(0)])
        for degree in range(5):
            d_straight = jnp.zeros((EB, C), F32)
            d_cross = jnp.zeros((EB, C), F32)
            for first, last in chunks(degree):
                wide = slice(first * C, last * C)
                sender = dot(pick, table[:, wide])
                d_message = dot(pick_target, d_gathered[:, wide])
                for component in range(first, last):
                    here = cols(component - first)
                    d_here = d_message[:, here]
                    d_straight = d_straight + d_here * sender[:, here]
                    d_cross = d_cross + d_here * column[:, component : component + 1]
            weight_grad[rows, cols(2 * degree)] = d_straight.astype(BF16)
            weight_grad[rows, cols(2 * degree + 1)] = (d_cross * scalar).astype(BF16)
        return carry

    lax.fori_loop(0, EDGES // EB, block, 0)
    second, first = network_grads(weight_grad, basis, pre, hidden_rows, second3)
    for degree in range(5):
        for path in range(2):
            at = (path * 5 + degree) * HIDDEN
            reduced[at : at + HIDDEN, :] = second[:, cols(2 * degree + path)]
    reduced[1280:1792, :] = probe_grads[...]
    reduced[1792:REDUCE_ROWS, :] = jnp.zeros((REDUCE_ROWS - 1792, C), F32)
    reduced[1792:1816, 0:HIDDEN] = first
    half = REDUCE_ROWS // 2
    side = core[0]
    mine_out[...] = reduced[pl.ds(pl.multiple_of(side * half, half), half), :]
    other_out[...] = reduced[pl.ds(pl.multiple_of((1 - side) * half, half), half), :]


def share_kernel(place, pieces, out):
    count = pieces.shape[0]
    total = pieces[0]
    for at in range(1, count):
        total = total + pieces[at]
    row = lax.broadcasted_iota(jnp.int32, total.shape, 0)
    rest = total - total.astype(BF16).astype(F32)
    ours = (row >= LOSS_ROW % total.shape[0] + 4) & (row < LOSS_ROW % total.shape[0] + 8)
    total = jnp.where(ours & (place[0] == 1), rest, total).astype(BF16)
    for at in range(count):
        out[at] = total


def finish_kernel(field_grad, low, high, left, right, placed, out, returned):
    fill_ghosts(returned, 0, low, high, left, right, PACKET_ORDER)
    for first, last in wide_chunks():
        back = dot(placed[...], returned[:, first * C : last * C])
        for component in range(first, last):
            out[component] = field_grad[comp_rows(component), :] + back[:, cols(component - first)]


def unpack_kernel(
    core, mine, other, loss, first, second, mixing, pfirst, psecond, readout, vector, sums
):
    half = REDUCE_ROWS // 2
    side = core[0]
    sums[pl.ds(pl.multiple_of(side * half, half), half), :] = mine[...].astype(F32)
    sums[pl.ds(pl.multiple_of((1 - side) * half, half), half), :] = other[...].astype(F32)
    for block in range(10):
        second[:, cols(block)] = sums[block * HIDDEN : (block + 1) * HIDDEN, :]
    for degree in range(5):
        mixing[degree] = sums[640 + degree * C : 640 + (degree + 1) * C, :]
        psecond[:, cols(degree)] = sums[1280 + degree * HIDDEN : 1280 + (degree + 1) * HIDDEN, :]
    readout[...] = sums[1600:1728, :]
    vector[...] = sums[1728:1729, :]
    loss[...] = sums[LOSS_ROW : LOSS_ROW + 1, :] + sums[LOSS_ROW + 4 : LOSS_ROW + 5, :]
    pfirst[...] = sums[1744 : 1744 + BASIS, 0:HIDDEN]
    first[...] = sums[1792 : 1792 + BASIS, 0:HIDDEN]


def call(kernel, outs, scratch, flops, *operands):
    shapes = [jax.ShapeDtypeStruct(shape, dtype) for shape, dtype in outs]
    moved = sum(x.size * x.dtype.itemsize for x in list(operands) + shapes)
    held = sum(np.prod(shape) * jnp.dtype(dtype).itemsize for shape, dtype in scratch)
    whole = pl.BlockSpec(memory_space=pltpu.VMEM)
    scalar = pl.BlockSpec(memory_space=pltpu.SMEM)
    return pl.pallas_call(
        kernel,
        out_shape=shapes,
        in_specs=[scalar if x.shape == (1,) else whole for x in operands],
        out_specs=[whole] * len(shapes),
        scratch_shapes=[pltpu.VMEM(shape, dtype) for shape, dtype in scratch],
        compiler_params=pltpu.CompilerParams(vmem_limit_bytes=int(held) + 12 * 1024 * 1024),
        cost_estimate=pl.CostEstimate(flops=flops, bytes_accessed=moved, transcendentals=0),
    )(*operands)


PACKETS = [((48, WIDE), BF16), ((32, WIDE), BF16), ((48, WIDE), BF16)]


def relay_kernel(middle, low, high, to_right, to_left):
    to_right[0:16, :] = middle[16:32, :]
    to_right[16:32, :] = low[32:48, :]
    to_right[32:48, :] = high[32:48, :]
    to_left[0:16, :] = middle[0:16, :]
    to_left[16:32, :] = low[0:16, :]
    to_left[32:48, :] = high[0:16, :]


def ring(axis):
    count = lax.axis_size(axis)
    up = [(i, (i + 1) % count) for i in range(count)]
    down = [(b, a) for a, b in up]
    return up, down


def exchange(low_packet, middle_packet, high_packet):
    up, down = ring("by")
    low = lax.ppermute(high_packet, "by", up)
    high = lax.ppermute(low_packet, "by", down)
    up, down = ring("bx")
    to_right, to_left = call(
        relay_kernel, [((48, WIDE), BF16)] * 2, [], 10**5, middle_packet, low, high
    )
    left = lax.ppermute(to_right, "bx", up)
    right = lax.ppermute(to_left, "bx", down)
    return (low, high, left, right), (to_right, to_left)


def reduce_halves(mine, other, owner):
    n_x, n_y = lax.axis_size("bx"), lax.axis_size("by")
    count = n_x * n_y // 2
    axes = ("bx", "by")
    swap = [(i, i ^ 1) for i in range(n_y)]
    groups = [[2 * i + core for i in range(count)] for core in range(2)]
    pair = (mine + lax.ppermute(other, "by", swap)).reshape(count, -1, C)
    pieces = lax.all_to_all(pair, axes, 0, 0, axis_index_groups=groups, tiled=True)
    (spread,) = call(share_kernel, [(pair.shape, BF16)], [], 10**6, owner, pieces)
    whole = lax.all_to_all(spread, axes, 0, 0, axis_index_groups=groups, tiled=True)
    whole = whole.reshape(mine.shape)
    return whole, lambda after: lax.ppermute(lax.optimization_barrier((whole, after))[0], "by", swap)


def on_device(
    features,
    send_index,
    atom_vectors,
    atom_source,
    atom_target,
    probe_vectors,
    probe_atoms,
    density_grid,
    probe_index,
    radial_first,
    radial_second,
    mixing,
    probe_first,
    probe_second,
    readout_first,
    readout_second,
):
    field = features[0, 0].transpose(1, 0, 2)
    source = atom_source.reshape(1, EDGES)
    target = atom_target.reshape(1, EDGES)
    atoms = probe_atoms.reshape(1, PEDGES)
    n_y = lax.axis_size("by")
    core = (lax.axis_index("by") % 2).reshape(1)
    chunk = REDUCE_ROWS // (lax.axis_size("bx") * n_y)
    half, place = divmod(LOSS_ROW, REDUCE_ROWS // 2)
    loss_at = 2 * (place // chunk) + half
    owner = (lax.axis_index("bx") * n_y + lax.axis_index("by") == loss_at).astype(jnp.int32).reshape(1)

    own, low, middle, high, chosen, placed = call(
        pack_kernel,
        [((ATOMS, WIDE), BF16)] + PACKETS + [((C, ATOMS), BF16), ((ATOMS, C), BF16)],
        [((C, C), F32)],
        2 * C * C * WIDE,
        core,
        owner,
        field,
        send_index[0, 0],
    )
    received, _ = exchange(low, middle, high)
    (
        columns,
        basis,
        pre,
        hidden3,
        hidden_rows,
        second3,
        pcolumns,
        pbasis,
        ppre,
        phidden3,
        phidden_rows,
        psecond3,
        picked,
    ) = call(
        prepare_kernel,
        [
            ((EDGES, C), F32),
            ((24, EDGES), F32),
            ((EDGES, HIDDEN), F32),
            ((EDGES, 3 * HIDDEN), BF16),
            ((2 * HIDDEN, EDGES), BF16),
            ((3 * HIDDEN, 10 * C), BF16),
            ((PEDGES, C), F32),
            ((24, PEDGES), F32),
            ((PEDGES, HIDDEN), F32),
            ((PEDGES, 3 * HIDDEN), BF16),
            ((2 * HIDDEN, PEDGES), BF16),
            ((3 * HIDDEN, 5 * C), BF16),
            ((PROBES, C), F32),
        ],
        [((C, EDGES), F32), ((C, PEDGES), F32)],
        10**9,
        atom_vectors[0, 0],
        source,
        target,
        probe_vectors[0, 0],
        atoms,
        density_grid.reshape(-1, C),
        probe_index.reshape(1, PROBES),
        radial_first,
        radial_second,
        probe_first,
        probe_second,
    )
    updated, gathered, mixed, table, low, middle, high = call(
        layer_kernel,
        [
            ((ATOMS, WIDE), BF16),
            ((COMP * ATOMS, C), BF16),
            ((COMP * ATOMS, C), F32),
            ((2 * ATOMS, WIDE), BF16),
        ]
        + PACKETS,
        [((EDGES, WIDE), BF16), ((COMP * ATOMS, 2 * C), BF16)],
        4 * 10**9,
        own,
        *received,
        columns,
        target,
        hidden3,
        second3,
        mixing,
        chosen,
    )
    received, _ = exchange(low, middle, high)
    grad_own, low, middle, high, weight_grad, readout_grads = call(
        probe_kernel,
        [((COMP * ATOMS, C), F32)]
        + PACKETS
        + [
            ((PEDGES, 5 * C), BF16),
            ((C + 16, C), F32),
        ],
        [
            ((2 * ATOMS, WIDE), BF16),
            ((PEDGES, 5 * C), F32),
            ((PEDGES, C), F32),
            ((PEDGES, WIDE), BF16),
        ],
        4 * 10**9,
        updated,
        *received,
        pcolumns,
        atoms,
        phidden3,
        psecond3,
        readout_first,
        readout_second.reshape(1, C),
        picked,
    )
    received, _ = exchange(low, middle, high)
    (probe_grads,) = call(
        probe_network_kernel,
        [((512, C), F32)],
        [],
        10**9,
        weight_grad,
        pbasis,
        ppre,
        phidden_rows,
        psecond3,
        readout_grads,
    )
    field_grad, d_gathered, d_mixed, low, middle, high = call(
        table_back_kernel,
        [
            ((COMP * ATOMS, C), F32),
            ((ATOMS, WIDE), BF16),
            ((COMP * ATOMS, C), BF16),
        ]
        + PACKETS,
        [
            ((C, WIDE), BF16),
            ((COMP * ATOMS, C), BF16),
            ((COMP * ATOMS, 2 * C), BF16),
            ((EDGES, WIDE), BF16),
        ],
        6 * 10**9,
        grad_own,
        *received,
        mixed,
        columns,
        source,
        hidden3,
        second3,
        mixing,
        placed,
    )
    received, relays = exchange(low, middle, high)
    mine, other = call(
        weights_back_kernel,
        [((REDUCE_ROWS // 2, C), F32), ((REDUCE_ROWS // 2, C), F32)],
        [((EDGES, 10 * C), BF16), ((REDUCE_ROWS, C), F32)],
        6 * 10**9,
        core,
        d_gathered,
        d_mixed,
        table,
        gathered,
        columns,
        basis,
        pre,
        hidden_rows,
        second3,
        probe_grads,
    )
    (feature_grad,) = call(
        finish_kernel,
        [((COMP, ATOMS, C), F32)],
        [((C, WIDE), BF16)],
        2 * C * C * WIDE,
        field_grad,
        *received,
        placed,
    )
    mine, other, *_ = lax.optimization_barrier((mine, other, received[0], received[1]))
    mine, swapped = reduce_halves(mine, other, owner)
    other = swapped(feature_grad)
    loss, first, second, mixing_grad, pfirst, psecond, readout, vector = call(
        unpack_kernel,
        [
            ((1, C), F32),
            ((BASIS, HIDDEN), F32),
            ((HIDDEN, 10 * C), F32),
            ((5, C, C), F32),
            ((BASIS, HIDDEN), F32),
            ((HIDDEN, 5 * C), F32),
            ((C, C), F32),
            ((1, C), F32),
        ],
        [((REDUCE_ROWS, C), F32)],
        10**6,
        core,
        mine,
        other,
    )
    return (
        loss[0, 0],
        feature_grad.transpose(1, 0, 2)[None, None],
        first,
        second,
        mixing_grad,
        pfirst,
        psecond,
        readout,
        vector[0],
    )


def solution(mesh):
    brick = [P("bx", "by", *([None] * (rank - 2))) for rank in (5, 5, 4, 3, 3, 4, 3, 3, 3)]
    in_specs = tuple(brick) + (P(),) * 7
    out_specs = (P(), P("bx", "by", None, None, None)) + (P(),) * 7
    return jax.shard_map(
        on_device, mesh=mesh, in_specs=in_specs, out_specs=out_specs, check_vma=False
    )
```

```python
import functools

import jax
import jax.numpy as jnp
import numpy as np
from jax import lax
from jax.experimental import pallas as pl
from jax.experimental.pallas import tpu as pltpu
from jax.sharding import PartitionSpec as P

C = 128
COMP = 25
BASIS = 20
HIDDEN = 64
ATOMS = 128
EDGES = 1024
PEDGES = 512
PROBES = 128
WIDE = COMP * C
EB = 512
DEGREES = (1, 3, 5, 7, 9)
STARTS = (0, 1, 4, 9, 16)
HIGHEST = lax.Precision.HIGHEST
F32 = jnp.float32
BF16 = jnp.bfloat16
REDUCE_ROWS = 2048
LOSS_ROW = 1736


def dot(a, b):
    return jnp.dot(a, b, preferred_element_type=F32)


def dot_exact(a, b):
    return jnp.dot(a, b, preferred_element_type=F32, precision=HIGHEST)


def dot_nt(a, b, precision=None):
    return lax.dot_general(
        a, b, (((1,), (1,)), ((), ())), preferred_element_type=F32, precision=precision
    )


def dot_tn(a, b, precision=None):
    return lax.dot_general(
        a, b, (((0,), (0,)), ((), ())), preferred_element_type=F32, precision=precision
    )


def split(a):
    high = a.astype(BF16)
    return high, (a - high.astype(F32)).astype(BF16)


def sigmoid(a):
    return 1.0 / (1.0 + jnp.exp(-a))


def cols(component):
    return slice(component * C, (component + 1) * C)


def chunks(degree):
    first = STARTS[degree]
    last = first + DEGREES[degree]
    return [(at, min(at + 2, last)) for at in range(first, last, 2)]


def harmonics(x, y, z):
    z_square = z * z
    return [
        jnp.ones_like(x),
        1.7320508 * y,
        1.7320508 * z,
        1.7320508 * x,
        3.8729833 * x * y,
        3.8729833 * y * z,
        1.118034 * (3.0 * z_square - 1.0),
        3.8729833 * x * z,
        1.9364917 * (x * x - y * y),
        2.0916501 * y * (3.0 * x * x - y * y),
        10.246951 * x * y * z,
        1.6201852 * y * (5.0 * z_square - 1.0),
        1.3228757 * z * (5.0 * z_square - 3.0),
        1.6201852 * x * (5.0 * z_square - 1.0),
        5.1234754 * z * (x * x - y * y),
        2.0916501 * x * (x * x - 3.0 * y * y),
        8.8741197 * x * y * (x * x - y * y),
        6.2749502 * y * z * (3.0 * x * x - y * y),
        3.354102 * x * y * (7.0 * z_square - 1.0),
        2.3717082 * y * z * (7.0 * z_square - 3.0),
        0.375 * (35.0 * z_square * z_square - 30.0 * z_square + 3.0),
        2.3717082 * x * z * (7.0 * z_square - 3.0),
        1.677051 * (x * x - y * y) * (7.0 * z_square - 1.0),
        6.2749502 * x * z * (x * x - 3.0 * y * y),
        2.2185299 * (x * x * x * x - 6.0 * x * x * y * y + y * y * y * y),
    ]


def pack_kernel(core, owner, features, send_index, own, low, middle, high, chosen_out, placed_out, lists):
    lists[...] = jnp.zeros_like(lists)
    for at in range(8):
        i, j = divmod(at if at < 4 else at + 1, 3)
        lists[at : at + 1, 0:16] = send_index[i, j : j + 1, :].astype(F32)
    turned = lists[...].T
    lane = lax.broadcasted_iota(jnp.int32, (16, C), 1).astype(F32)
    hits = [(turned[0:16, at : at + 1] == lane).astype(F32) for at in range(8)]
    chosen = jnp.concatenate(hits, axis=0)
    chosen_out[...] = chosen.astype(BF16)
    placed_out[...] = chosen.T.astype(BF16)
    for component in range(COMP):
        own[:, cols(component)] = features[component]
    send_packets(chosen_out[...], own, low, middle, high)


def send_packets(chosen, rows, low, middle, high):
    for first in range(0, COMP, 2):
        wide = slice(first * C, min(first + 2, COMP) * C)
        packet = dot(chosen, rows[:, wide]).astype(BF16)
        low[:, wide] = packet[0:48]
        middle[:, wide] = packet[48:80]
        high[:, wide] = packet[80:128]


def geometry(vectors, index_rows, edges, turned, basis_out):
    x, y, z = vectors[0:1], vectors[1:2], vectors[2:3]
    radius = jnp.sqrt(x * x + y * y + z * z)
    rows = harmonics(x / radius, y / radius, z / radius) + index_rows
    for at, row in enumerate(rows):
        turned[at : at + 1, :] = row
    center = 0.5 + 4.0 * lax.broadcasted_iota(jnp.int32, (24, edges), 0).astype(F32) / (BASIS - 1)
    offset = (radius - center) / 0.4
    basis = jnp.exp(-(offset * offset))
    live = lax.broadcasted_iota(jnp.int32, (24, edges), 0) < BASIS
    basis_out[...] = jnp.where(live, basis, 0.0)
    return turned[...].T


def prepare_kernel(
    vectors,
    source,
    target,
    probe_vectors,
    probe_atoms,
    grid,
    probe_index,
    first,
    second,
    pfirst,
    psecond,
    columns_out,
    basis_out,
    pre_out,
    hidden3_out,
    hidden_rows_out,
    second3_out,
    pcolumns_out,
    pbasis_out,
    ppre_out,
    phidden3_out,
    phidden_rows_out,
    psecond3_out,
    picked_out,
    turned,
    pturned,
):
    turned[...] = jnp.zeros_like(turned)
    pturned[...] = jnp.zeros_like(pturned)
    row = source[...]
    slot = jnp.where(row > ATOMS, row - 1, jnp.where(row == ATOMS, 512, row))
    columns_out[...] = geometry(
        vectors[...], [slot.astype(F32), target[...].astype(F32)], EDGES, turned, basis_out
    )
    prow = probe_atoms[...]
    pslot = jnp.where(prow > ATOMS, prow - 1, jnp.where(prow == ATOMS, 512, prow))
    pcolumns_out[...] = geometry(
        probe_vectors[...], [pslot.astype(F32)], PEDGES, pturned, pbasis_out
    )

    for basis, layer, pre, hidden3, hidden_rows in (
        (basis_out, first, pre_out, hidden3_out, hidden_rows_out),
        (pbasis_out, pfirst, ppre_out, phidden3_out, phidden_rows_out),
    ):
        before = dot_tn(layer[...], basis[0:BASIS, :], HIGHEST)
        pre[...] = before.T
        hidden = before * sigmoid(before)
        upper, lower = split(hidden)
        hidden_rows[0:HIDDEN, :] = upper
        hidden_rows[HIDDEN : 2 * HIDDEN, :] = lower
        upper, lower = split(hidden.T)
        hidden3[:, 0:HIDDEN] = upper
        hidden3[:, HIDDEN : 2 * HIDDEN] = upper
        hidden3[:, 2 * HIDDEN : 3 * HIDDEN] = lower
    for degree in range(5):
        for path in range(2):
            upper, lower = split(second[:, cols(path * 5 + degree)])
            at = cols(2 * degree + path)
            second3_out[0:HIDDEN, at] = upper
            second3_out[HIDDEN : 2 * HIDDEN, at] = lower
            second3_out[2 * HIDDEN : 3 * HIDDEN, at] = upper
    upper, lower = split(psecond[...])
    psecond3_out[0:HIDDEN, :] = upper
    psecond3_out[HIDDEN : 2 * HIDDEN, :] = lower
    psecond3_out[2 * HIDDEN : 3 * HIDDEN, :] = upper

    place = probe_index[...]
    grid_row = lax.broadcasted_iota(jnp.int32, (grid.shape[0], PROBES), 0)
    hit = (place // C == grid_row).astype(F32)
    lines = dot_tn(grid[...], hit, HIGHEST)
    lane = lax.broadcasted_iota(jnp.int32, (C, PROBES), 0)
    values = jnp.sum(jnp.where(place % C == lane, lines, 0.0), axis=0, keepdims=True)
    picked_out[...] = jnp.broadcast_to(values, (C, PROBES)).T


def fill_ghosts(rows, base, low, high, left, right):
    pieces = (
        left[16:32],
        low[16:32],
        right[16:32],
        left[0:16],
        right[0:16],
        left[32:48],
        high[16:32],
        right[32:48],
    )
    for at, piece in enumerate(pieces):
        rows[base + 16 * at : base + 16 * at + 16, :] = piece


def comp_rows(component, count=1):
    return slice(component * ATOMS, (component + count) * ATOMS)


def wide_chunks():
    return [(at, min(at + 2, COMP)) for at in range(0, COMP, 2)]


def one_hot_lanes(column, width):
    lane = lax.broadcasted_iota(jnp.int32, (EB, width), 1).astype(F32)
    return (column == lane).astype(F32).astype(BF16)


def one_hot_rows(row, height):
    place = lax.broadcasted_iota(jnp.int32, (height, row.shape[1]), 0)
    return (row == place).astype(F32).astype(BF16)


def fold_source(row):
    return jnp.where(row > ATOMS, row - 1, jnp.where(row == ATOMS, 512, row))


def layer_kernel(
    own,
    low,
    high,
    left,
    right,
    columns,
    target,
    hidden3,
    second3,
    mixing,
    chosen,
    updated,
    gathered,
    mixed,
    table,
    low_out,
    middle_out,
    high_out,
    messages,
    parts,
):
    table[0:ATOMS, :] = own[...]
    fill_ghosts(table, ATOMS, low, high, left, right)

    def block(step, carry):
        rows = pl.ds(pl.multiple_of(step * EB, EB), EB)
        column = columns[rows, :]
        pick = one_hot_lanes(column[:, 25:26], 2 * ATOMS)
        hidden = hidden3[rows, :]
        scalar = dot(pick, table[:, cols(0)])
        for degree in range(5):
            weight = dot(hidden, second3[:, 2 * degree * C : 2 * (degree + 1) * C])
            straight = weight[:, 0:C]
            cross = weight[:, C:] * scalar
            for first, last in chunks(degree):
                sender = dot(pick, table[:, first * C : last * C])
                for component in range(first, last):
                    value = sender[:, cols(component - first)]
                    message = straight * value + cross * column[:, component : component + 1]
                    messages[rows, cols(component)] = message.astype(BF16)
        return carry

    lax.fori_loop(0, EDGES // EB, block, 0)
    put = one_hot_rows(target[...], ATOMS)
    for first, last in wide_chunks():
        here = dot(put, messages[:, first * C : last * C]) * 0.125
        for component in range(first, last):
            upper, lower = split(here[:, cols(component - first)])
            gathered[comp_rows(component), :] = upper
            parts[comp_rows(component), 0:C] = upper
            parts[comp_rows(component), C:] = lower
    gate = None
    for degree in range(5):
        upper, lower = split(mixing[degree])
        twice = jnp.concatenate([upper, upper], axis=0)
        for component in range(STARTS[degree], STARTS[degree] + DEGREES[degree]):
            rows = comp_rows(component)
            out = dot(parts[rows, :], twice) + dot(parts[rows, 0:C], lower)
            mixed[rows, :] = out
            if component == 0:
                gate = sigmoid(out)
            new = own[:, cols(component)].astype(F32) + out * gate
            updated[:, cols(component)] = new.astype(BF16)
    send_packets(chosen[...], updated, low_out, middle_out, high_out)


def sum_table_grads(put, messages, own_grad, low, middle, high, add):
    for first, last in wide_chunks():
        wide = slice(first * C, last * C)
        total = dot(put, messages[:, wide])
        for component in range(first, last):
            here = total[0:ATOMS, cols(component - first)]
            if add is not None:
                here = here + add[comp_rows(component), :]
            own_grad[comp_rows(component), :] = here
        ghosts = total[ATOMS:, :].astype(BF16)
        low[:, wide] = ghosts[0:48]
        middle[:, wide] = ghosts[48:80]
        high[:, wide] = ghosts[80:128]


def probe_kernel(
    own,
    low,
    high,
    left,
    right,
    columns,
    atoms,
    hidden3,
    second3,
    first_readout,
    second_readout,
    picked,
    grad_own,
    low_out,
    middle_out,
    high_out,
    weight_grad,
    readout_grads,
    table,
    partial,
    contribution,
    messages,
):
    table[0:ATOMS, :] = own[...]
    fill_ghosts(table, ATOMS, low, high, left, right)

    def forward(step, carry):
        rows = pl.ds(pl.multiple_of(step * EB, EB), EB)
        column = columns[rows, :]
        pick = one_hot_lanes(column[:, 25:26], 2 * ATOMS)
        hidden = hidden3[rows, :]
        total = jnp.zeros((EB, C), F32)
        for degree in range(5):
            weight = dot(hidden, second3[:, cols(degree)])
            here = jnp.zeros((EB, C), F32)
            for first, last in chunks(degree):
                sender = dot(pick, table[:, first * C : last * C])
                for component in range(first, last):
                    value = sender[:, cols(component - first)]
                    here = here + value * column[:, component : component + 1]
            partial[rows, cols(degree)] = here
            total = total + weight * here
        contribution[rows, :] = total
        return carry

    lax.fori_loop(0, PEDGES // EB, forward, 0)

    edge = lax.broadcasted_iota(jnp.int32, (PROBES, PEDGES), 1)
    probe = lax.broadcasted_iota(jnp.int32, (PROBES, PEDGES), 0)
    pool = (edge // 4 == probe).astype(F32)
    summed = dot_exact(pool, contribution[...])
    before = dot_exact(summed, first_readout[...])
    gate = sigmoid(before)
    hidden = before * gate
    vector = second_readout[...]
    density = jnp.sum(hidden * vector, axis=1, keepdims=True)
    misfit = density - picked[...]
    loss = jnp.sum(misfit[:, 0:1] * misfit[:, 0:1], axis=0, keepdims=True) / (2.0 * PROBES)
    slope = misfit / PROBES
    d_before = slope * vector * gate * (1.0 + before * (1.0 - gate))
    readout_grads[0:C, :] = dot_tn(summed, d_before, HIGHEST)
    readout_grads[C : C + 8, :] = jnp.broadcast_to(
        jnp.sum(hidden * slope, axis=0, keepdims=True), (8, C)
    )
    readout_grads[C + 8 : C + 16, :] = jnp.broadcast_to(loss, (8, C))
    d_summed = dot_nt(d_before, first_readout[...], HIGHEST)
    contribution[...] = dot_tn(pool, d_summed, HIGHEST)

    def backward(step, carry):
        rows = pl.ds(pl.multiple_of(step * EB, EB), EB)
        column = columns[rows, :]
        hidden = hidden3[rows, :]
        slope_here = contribution[rows, :]
        for degree in range(5):
            weight = dot(hidden, second3[:, cols(degree)])
            weight_grad[rows, cols(degree)] = (slope_here * partial[rows, cols(degree)]).astype(BF16)
            down = slope_here * weight
            for component in range(STARTS[degree], STARTS[degree] + DEGREES[degree]):
                value = down * column[:, component : component + 1]
                messages[rows, cols(component)] = value.astype(BF16)
        return carry

    lax.fori_loop(0, PEDGES // EB, backward, 0)
    put = one_hot_rows(fold_source(atoms[...]), 2 * ATOMS)
    sum_table_grads(put, messages, grad_own, low_out, middle_out, high_out, None)


def network_grads(weight_grad, basis, pre, hidden_rows, second3):
    both = dot(hidden_rows[...], weight_grad[...])
    second = both[0:HIDDEN, :] + both[HIDDEN:, :]
    grads = weight_grad[...]
    d_hidden = dot_nt(grads, second3[0:HIDDEN, :]) + dot_nt(grads, second3[HIDDEN : 2 * HIDDEN, :])
    before = pre[...]
    gate = sigmoid(before)
    d_before = d_hidden * gate * (1.0 + before * (1.0 - gate))
    return second, dot_exact(basis[...], d_before)


def probe_network_kernel(weight_grad, basis, pre, hidden_rows, second3, readout_grads, out):
    second, first = network_grads(weight_grad, basis, pre, hidden_rows, second3)
    for degree in range(5):
        out[degree * HIDDEN : (degree + 1) * HIDDEN, :] = second[:, cols(degree)]
    out[320:464, :] = readout_grads[...]
    out[464:512, :] = jnp.zeros((48, C), F32)
    out[464:488, 0:HIDDEN] = first


def table_back_kernel(
    grad_own,
    low,
    high,
    left,
    right,
    mixed,
    columns,
    source,
    hidden3,
    second3,
    mixing,
    placed,
    field_grad,
    d_gathered,
    d_mixed_out,
    low_out,
    middle_out,
    high_out,
    returned,
    grad_updated,
    parts,
    messages,
):
    fill_ghosts(returned, 0, low, high, left, right)
    for first, last in wide_chunks():
        back = dot(placed[...], returned[:, first * C : last * C])
        for component in range(first, last):
            rows = comp_rows(component)
            whole = grad_own[rows, :] + back[:, cols(component - first)]
            grad_updated[rows, :] = whole.astype(BF16)
    gate_in = mixed[comp_rows(0), :]
    gate = sigmoid(gate_in)
    d_gate = jnp.zeros((ATOMS, C), F32)
    for component in range(COMP - 1, -1, -1):
        rows = comp_rows(component)
        d_updated = grad_updated[rows, :].astype(F32)
        if component > 0:
            d_gate = d_gate + d_updated * mixed[rows, :]
            d_mixed = d_updated * gate
        else:
            d_mixed = d_updated * gate * (1.0 + gate_in * (1.0 - gate)) + d_gate * gate * (
                1.0 - gate
            )
        upper, lower = split(d_mixed)
        d_mixed_out[rows, :] = upper
        parts[rows, 0:C] = upper
        parts[rows, C:] = lower
    for degree in range(5):
        upper, lower = split(mixing[degree].T)
        twice = jnp.concatenate([upper, upper], axis=0)
        for component in range(STARTS[degree], STARTS[degree] + DEGREES[degree]):
            rows = comp_rows(component)
            out = dot(parts[rows, :], twice) + dot(parts[rows, 0:C], lower)
            d_gathered[:, cols(component)] = (out * 0.125).astype(BF16)

    def block(step, carry):
        rows = pl.ds(pl.multiple_of(step * EB, EB), EB)
        column = columns[rows, :]
        pick_target = one_hot_lanes(column[:, 26:27], ATOMS)
        hidden = hidden3[rows, :]
        d_scalar = jnp.zeros((EB, C), F32)
        for degree in (4, 3, 2, 1, 0):
            weight = dot(hidden, second3[:, 2 * degree * C : 2 * (degree + 1) * C])
            straight = weight[:, 0:C]
            d_cross = jnp.zeros((EB, C), F32)
            for first, last in chunks(degree):
                d_message = dot(pick_target, d_gathered[:, first * C : last * C])
                for component in range(first, last):
                    d_here = d_message[:, cols(component - first)]
                    d_cross = d_cross + d_here * column[:, component : component + 1]
                    value = straight * d_here
                    if component == 0:
                        value = value + d_scalar + d_cross * weight[:, C:]
                    messages[rows, cols(component)] = value.astype(BF16)
            d_scalar = d_scalar + d_cross * weight[:, C:]
        return carry

    lax.fori_loop(0, EDGES // EB, block, 0)
    put = one_hot_rows(fold_source(source[...]), 2 * ATOMS)
    sum_table_grads(put, messages, field_grad, low_out, middle_out, high_out, grad_updated)


def weights_back_kernel(
    core,
    d_gathered,
    d_mixed,
    table,
    gathered,
    columns,
    basis,
    pre,
    hidden_rows,
    second3,
    probe_grads,
    mine_out,
    other_out,
    weight_grad,
    reduced,
):
    for degree in range(5):
        rows = comp_rows(STARTS[degree], DEGREES[degree])
        reduced[640 + degree * C : 640 + (degree + 1) * C, :] = dot_tn(
            gathered[rows, :], d_mixed[rows, :]
        )

    def block(step, carry):
        rows = pl.ds(pl.multiple_of(step * EB, EB), EB)
        column = columns[rows, :]
        pick = one_hot_lanes(column[:, 25:26], 2 * ATOMS)
        pick_target = one_hot_lanes(column[:, 26:27], ATOMS)
        scalar = dot(pick, table[:, cols(0)])
        for degree in range(5):
            d_straight = jnp.zeros((EB, C), F32)
            d_cross = jnp.zeros((EB, C), F32)
            for first, last in chunks(degree):
                wide = slice(first * C, last * C)
                sender = dot(pick, table[:, wide])
                d_message = dot(pick_target, d_gathered[:, wide])
                for component in range(first, last):
                    here = cols(component - first)
                    d_here = d_message[:, here]
                    d_straight = d_straight + d_here * sender[:, here]
                    d_cross = d_cross + d_here * column[:, component : component + 1]
            weight_grad[rows, cols(2 * degree)] = d_straight.astype(BF16)
            weight_grad[rows, cols(2 * degree + 1)] = (d_cross * scalar).astype(BF16)
        return carry

    lax.fori_loop(0, EDGES // EB, block, 0)
    second, first = network_grads(weight_grad, basis, pre, hidden_rows, second3)
    for degree in range(5):
        for path in range(2):
            at = (path * 5 + degree) * HIDDEN
            reduced[at : at + HIDDEN, :] = second[:, cols(2 * degree + path)]
    reduced[1280:1792, :] = probe_grads[...]
    reduced[1792:REDUCE_ROWS, :] = jnp.zeros((REDUCE_ROWS - 1792, C), F32)
    reduced[1792:1816, 0:HIDDEN] = first
    half = REDUCE_ROWS // 2
    side = core[0]
    mine_out[...] = reduced[pl.ds(pl.multiple_of(side * half, half), half), :]
    other_out[...] = reduced[pl.ds(pl.multiple_of((1 - side) * half, half), half), :]


def share_kernel(place, pieces, out):
    count = pieces.shape[0]
    total = pieces[0].astype(F32)
    for at in range(1, count):
        total = total + pieces[at].astype(F32)
    row = lax.broadcasted_iota(jnp.int32, total.shape, 0)
    first = LOSS_ROW % total.shape[0]
    loss_rows = (row >= first) & (row < first + 8)
    loss = 0.25 * jnp.sum(jnp.where(loss_rows, total, 0.0), axis=0, keepdims=True)
    rest = loss - loss.astype(BF16).astype(F32)
    value = jnp.where(row < first + 4, loss, rest)
    total = jnp.where(loss_rows & (place[0] == 1), value, total).astype(BF16)
    for at in range(count):
        out[at] = total


def finish_kernel(field_grad, low, high, left, right, placed, out, returned):
    fill_ghosts(returned, 0, low, high, left, right)
    for first, last in wide_chunks():
        back = dot(placed[...], returned[:, first * C : last * C])
        for component in range(first, last):
            out[component] = field_grad[comp_rows(component), :] + back[:, cols(component - first)]


def unpack_kernel(
    core, mine, other, loss, first, second, mixing, pfirst, psecond, readout, vector, sums
):
    half = REDUCE_ROWS // 2
    side = core[0]
    sums[pl.ds(pl.multiple_of(side * half, half), half), :] = mine[...].astype(F32)
    sums[pl.ds(pl.multiple_of((1 - side) * half, half), half), :] = other[...].astype(F32)
    for block in range(10):
        second[:, cols(block)] = sums[block * HIDDEN : (block + 1) * HIDDEN, :]
    for degree in range(5):
        mixing[degree] = sums[640 + degree * C : 640 + (degree + 1) * C, :]
        psecond[:, cols(degree)] = sums[1280 + degree * HIDDEN : 1280 + (degree + 1) * HIDDEN, :]
    readout[...] = sums[1600:1728, :]
    vector[...] = sums[1728:1729, :]
    loss[...] = sums[LOSS_ROW : LOSS_ROW + 1, :] + sums[LOSS_ROW + 4 : LOSS_ROW + 5, :]
    pfirst[...] = sums[1744 : 1744 + BASIS, 0:HIDDEN]
    first[...] = sums[1792 : 1792 + BASIS, 0:HIDDEN]


def call(kernel, outs, scratch, flops, *operands):
    shapes = [jax.ShapeDtypeStruct(shape, dtype) for shape, dtype in outs]
    moved = sum(x.size * x.dtype.itemsize for x in list(operands) + shapes)
    held = sum(np.prod(shape) * jnp.dtype(dtype).itemsize for shape, dtype in scratch)
    whole = pl.BlockSpec(memory_space=pltpu.VMEM)
    scalar = pl.BlockSpec(memory_space=pltpu.SMEM)
    return pl.pallas_call(
        kernel,
        out_shape=shapes,
        in_specs=[scalar if x.shape == (1,) else whole for x in operands],
        out_specs=[whole] * len(shapes),
        scratch_shapes=[pltpu.VMEM(shape, dtype) for shape, dtype in scratch],
        compiler_params=pltpu.CompilerParams(vmem_limit_bytes=int(held) + 12 * 1024 * 1024),
        cost_estimate=pl.CostEstimate(flops=flops, bytes_accessed=moved, transcendentals=0),
    )(*operands)


PACKETS = [((48, WIDE), BF16), ((32, WIDE), BF16), ((48, WIDE), BF16)]


def relay_kernel(middle, low, high, to_right, to_left):
    to_right[0:16, :] = middle[16:32, :]
    to_right[16:32, :] = low[32:48, :]
    to_right[32:48, :] = high[32:48, :]
    to_left[0:16, :] = middle[0:16, :]
    to_left[16:32, :] = low[0:16, :]
    to_left[32:48, :] = high[0:16, :]


def ring(axis):
    count = lax.axis_size(axis)
    up = [(i, (i + 1) % count) for i in range(count)]
    down = [(b, a) for a, b in up]
    return up, down


def exchange(low_packet, middle_packet, high_packet):
    up, down = ring("bx")
    low = lax.ppermute(high_packet, "bx", up)
    high = lax.ppermute(low_packet, "bx", down)
    up, down = ring("by")
    to_right, to_left = call(
        relay_kernel, [((48, WIDE), BF16)] * 2, [], 10**5, middle_packet, low, high
    )
    left = lax.ppermute(to_right, "by", up)
    right = lax.ppermute(to_left, "by", down)
    return (low, high, left, right), (to_right, to_left)


def reduce_halves(mine, other, core, owner):
    n_x, n_y = lax.axis_size("bx"), lax.axis_size("by")
    count = n_x * n_y // 2
    axes = ("bx", "by")
    swap = [(i, i ^ 1) for i in range(n_y)]
    groups = [[2 * i + core for i in range(count)] for core in range(2)]
    pair = (mine + lax.ppermute(other, "by", swap)).reshape(count, -1, C)
    rounded = lax.reduce_precision(pair, 8, 7)
    side, place = divmod(LOSS_ROW, REDUCE_ROWS // 2)
    chunk, row = divmod(place, pair.shape[1])
    chunk_at = lax.broadcasted_iota(jnp.int32, pair.shape, 0)
    row_at = lax.broadcasted_iota(jnp.int32, pair.shape, 1)
    rest = (core[0] == side) & (chunk_at == chunk) & (row_at >= row + 4) & (row_at < row + 8)
    pair = jnp.where(rest, pair - rounded, rounded).astype(BF16)
    pieces = lax.all_to_all(pair, axes, 0, 0, axis_index_groups=groups, tiled=True)
    (spread,) = call(share_kernel, [(pair.shape, BF16)], [], 10**6, owner, pieces)
    whole = lax.all_to_all(spread, axes, 0, 0, axis_index_groups=groups, tiled=True)
    whole = whole.reshape(mine.shape)
    return whole, lambda after: lax.ppermute(lax.optimization_barrier((whole, after))[0], "by", swap)


def on_device(
    features,
    send_index,
    atom_vectors,
    atom_source,
    atom_target,
    probe_vectors,
    probe_atoms,
    density_grid,
    probe_index,
    radial_first,
    radial_second,
    mixing,
    probe_first,
    probe_second,
    readout_first,
    readout_second,
):
    field = features[0, 0].transpose(1, 0, 2)
    source = atom_source.reshape(1, EDGES)
    target = atom_target.reshape(1, EDGES)
    atoms = probe_atoms.reshape(1, PEDGES)
    n_y = lax.axis_size("by")
    core = (lax.axis_index("by") % 2).reshape(1)
    chunk = REDUCE_ROWS // (lax.axis_size("bx") * n_y)
    half, place = divmod(LOSS_ROW, REDUCE_ROWS // 2)
    loss_at = 2 * (place // chunk) + half
    owner = (lax.axis_index("bx") * n_y + lax.axis_index("by") == loss_at).astype(jnp.int32).reshape(1)

    own, low, middle, high, chosen, placed = call(
        pack_kernel,
        [((ATOMS, WIDE), BF16)] + PACKETS + [((C, ATOMS), BF16), ((ATOMS, C), BF16)],
        [((C, C), F32)],
        2 * C * C * WIDE,
        core,
        owner,
        field,
        send_index[0, 0],
    )
    received, _ = exchange(low, middle, high)
    (
        columns,
        basis,
        pre,
        hidden3,
        hidden_rows,
        second3,
        pcolumns,
        pbasis,
        ppre,
        phidden3,
        phidden_rows,
        psecond3,
        picked,
    ) = call(
        prepare_kernel,
        [
            ((EDGES, C), F32),
            ((24, EDGES), F32),
            ((EDGES, HIDDEN), F32),
            ((EDGES, 3 * HIDDEN), BF16),
            ((2 * HIDDEN, EDGES), BF16),
            ((3 * HIDDEN, 10 * C), BF16),
            ((PEDGES, C), F32),
            ((24, PEDGES), F32),
            ((PEDGES, HIDDEN), F32),
            ((PEDGES, 3 * HIDDEN), BF16),
            ((2 * HIDDEN, PEDGES), BF16),
            ((3 * HIDDEN, 5 * C), BF16),
            ((PROBES, C), F32),
        ],
        [((C, EDGES), F32), ((C, PEDGES), F32)],
        10**9,
        atom_vectors[0, 0],
        source,
        target,
        probe_vectors[0, 0],
        atoms,
        density_grid.reshape(-1, C),
        probe_index.reshape(1, PROBES),
        radial_first,
        radial_second,
        probe_first,
        probe_second,
    )
    updated, gathered, mixed, table, low, middle, high = call(
        layer_kernel,
        [
            ((ATOMS, WIDE), BF16),
            ((COMP * ATOMS, C), BF16),
            ((COMP * ATOMS, C), F32),
            ((2 * ATOMS, WIDE), BF16),
        ]
        + PACKETS,
        [((EDGES, WIDE), BF16), ((COMP * ATOMS, 2 * C), BF16)],
        4 * 10**9,
        own,
        *received,
        columns,
        target,
        hidden3,
        second3,
        mixing,
        chosen,
    )
    received, _ = exchange(low, middle, high)
    grad_own, low, middle, high, weight_grad, readout_grads = call(
        probe_kernel,
        [((COMP * ATOMS, C), F32)]
        + PACKETS
        + [
            ((PEDGES, 5 * C), BF16),
            ((C + 16, C), F32),
        ],
        [
            ((2 * ATOMS, WIDE), BF16),
            ((PEDGES, 5 * C), F32),
            ((PEDGES, C), F32),
            ((PEDGES, WIDE), BF16),
        ],
        4 * 10**9,
        updated,
        *received,
        pcolumns,
        atoms,
        phidden3,
        psecond3,
        readout_first,
        readout_second.reshape(1, C),
        picked,
    )
    received, _ = exchange(low, middle, high)
    (probe_grads,) = call(
        probe_network_kernel,
        [((512, C), F32)],
        [],
        10**9,
        weight_grad,
        pbasis,
        ppre,
        phidden_rows,
        psecond3,
        readout_grads,
    )
    field_grad, d_gathered, d_mixed, low, middle, high = call(
        table_back_kernel,
        [
            ((COMP * ATOMS, C), F32),
            ((ATOMS, WIDE), BF16),
            ((COMP * ATOMS, C), BF16),
        ]
        + PACKETS,
        [
            ((C, WIDE), BF16),
            ((COMP * ATOMS, C), BF16),
            ((COMP * ATOMS, 2 * C), BF16),
            ((EDGES, WIDE), BF16),
        ],
        6 * 10**9,
        grad_own,
        *received,
        mixed,
        columns,
        source,
        hidden3,
        second3,
        mixing,
        placed,
    )
    received, relays = exchange(low, middle, high)
    mine, other = call(
        weights_back_kernel,
        [((REDUCE_ROWS // 2, C), F32), ((REDUCE_ROWS // 2, C), F32)],
        [((EDGES, 10 * C), BF16), ((REDUCE_ROWS, C), F32)],
        6 * 10**9,
        core,
        d_gathered,
        d_mixed,
        table,
        gathered,
        columns,
        basis,
        pre,
        hidden_rows,
        second3,
        probe_grads,
    )
    (feature_grad,) = call(
        finish_kernel,
        [((COMP, ATOMS, C), F32)],
        [((C, WIDE), BF16)],
        2 * C * C * WIDE,
        field_grad,
        *received,
        placed,
    )
    mine, other, *_ = lax.optimization_barrier((mine, other, received[0], received[1]))
    mine, swapped = reduce_halves(mine, other, core, owner)
    other = swapped(feature_grad)
    loss, first, second, mixing_grad, pfirst, psecond, readout, vector = call(
        unpack_kernel,
        [
            ((1, C), F32),
            ((BASIS, HIDDEN), F32),
            ((HIDDEN, 10 * C), F32),
            ((5, C, C), F32),
            ((BASIS, HIDDEN), F32),
            ((HIDDEN, 5 * C), F32),
            ((C, C), F32),
            ((1, C), F32),
        ],
        [((REDUCE_ROWS, C), F32)],
        10**6,
        core,
        mine,
        other,
    )
    return (
        loss[0, 0],
        feature_grad.transpose(1, 0, 2)[None, None],
        first,
        second,
        mixing_grad,
        pfirst,
        psecond,
        readout,
        vector[0],
    )


def solution(mesh):
    brick = [P("bx", "by", *([None] * (rank - 2))) for rank in (5, 5, 4, 3, 3, 4, 3, 3, 3)]
    in_specs = tuple(brick) + (P(),) * 7
    out_specs = (P(), P("bx", "by", None, None, None)) + (P(),) * 7
    return jax.shard_map(
        on_device, mesh=mesh, in_specs=in_specs, out_specs=out_specs, check_vma=False
    )
```
